32 devices in a mesh: pipe: 2 (over x), dp: 16 (over z, y, core).
Axes of the slice: x: 2, y: 2, z: 4, core: 2. Of those that a mesh axis runs over, the one named last changes fastest.
Arguments:
- content_ends: bfloat16 [2, 4096, 768], P('pipe', 'dp'), may hold values from -6 to 6
- query_ends: bfloat16 [2, 512, 768], P('pipe', 'dp'), may hold values from -6 to 6
- w_query: bfloat16 [2, 768, 768], P('pipe'), may hold values from -0.21875 to 0.21875
- b_query: float32 [2, 768], P('pipe'), may hold values from -4 to 4
- w_key: bfloat16 [2, 768, 768], P('pipe'), may hold values from -0.21875 to 0.21875
- w_value: bfloat16 [2, 768, 768], P('pipe'), may hold values from -0.21875 to 0.21875
- b_value: float32 [2, 768], P('pipe'), may hold values from -4 to 4
- w_out: bfloat16 [2, 768, 768], P('pipe'), may hold values from -0.875 to 0.875
- b_out: float32 [2, 768], P('pipe'), may hold values from -4 to 4
- gain_attn: float32 [2, 768], P('pipe'), may hold values from 0.25 to 1.75
- shift_attn: float32 [2, 768], P('pipe'), may hold values from -4 to 4
- w_up: bfloat16 [2, 768, 3072], P('pipe'), may hold values from -0.21875 to 0.21875
- b_up: float32 [2, 3072], P('pipe'), may hold values from -4 to 4
- w_down: bfloat16 [2, 3072, 768], P('pipe'), may hold values from -0.109375 to 0.109375
- b_down: float32 [2, 768], P('pipe'), may hold values from -4 to 4
- gain_ffn: float32 [2, 768], P('pipe'), may hold values from 0.25 to 1.75
- shift_ffn: float32 [2, 768], P('pipe'), may hold values from -4 to 4
- rel_table: float32 [2, 32, 12], P('pipe'), may hold values from -6 to 6
- doc_lengths: int32 [32, 4], P('dp'), may hold values from 1 to 96, 128 in all within a row
- position_order: int32 [32, 128], P('dp'), may hold values from 0 to 127, each once within a row
Outputs:
- content_out: bfloat16 [2, 4096, 768], P('pipe', 'dp')
- query_out: bfloat16 [2, 512, 768], P('pipe', 'dp')
- grad_w_query: float32 [2, 768, 768], P('pipe')
- grad_b_query: float32 [2, 768], P('pipe')
- grad_w_key: float32 [2, 768, 768], P('pipe')
- grad_w_value: float32 [2, 768, 768], P('pipe')
- grad_b_value: float32 [2, 768], P('pipe')
- grad_w_out: float32 [2, 768, 768], P('pipe')
- grad_b_out: float32 [2, 768], P('pipe')
- grad_gain_attn: float32 [2, 768], P('pipe')
- grad_shift_attn: float32 [2, 768], P('pipe')
- grad_w_up: float32 [2, 768, 3072], P('pipe')
- grad_b_up: float32 [2, 3072], P('pipe')
- grad_w_down: float32 [2, 3072, 768], P('pipe')
- grad_b_down: float32 [2, 768], P('pipe')
- grad_gain_ffn: float32 [2, 768], P('pipe')
- grad_shift_ffn: float32 [2, 768], P('pipe')
- grad_rel_table: float32 [2, 32, 12], P('pipe')
The draws below stay inside these ranges and needn't reach their ends.
Inputs may be any that keep to these rules, and one draw needn't show every extreme that they name: `doc_lengths`: each row lists the lengths of the 4 documents packed in order into one bucket; they sum to 128, and the longest is exactly 96. `position_order`: each row is a permutation of the 128 positions of one bucket; the positions named by its last 16 entries are the predicted ones.
All inputs are finite; a program needn't handle non-finite values.
Results may differ from the reference program's by a relative error of at most 0.03.
Values may be sent and summed in bfloat16 or wider, within the bound.
A program may use at most 256 MiB of HBM per device.

```python
import math
import jax
import jax.numpy as jnp
import numpy as np
from jax import lax

D = 768
H = 12
FF = 3072
BUCKETS = 32
HD = 64
L = 128
MB = 2
DOCS = 4
QL = 16
MOST = 96
TOKENS = 4096
QTOKENS = 512
N_DP = 16


def block_levels(own_key, dims, split, least, largest):
    factor_of, own = 1.0, jax.random.fold_in(own_key, 6)
    for axis_at, shards_of in split:
        heights = jnp.exp(jax.random.uniform(jax.random.fold_in(own, axis_at), (shards_of,), jnp.float32, least / len(split), largest / len(split)))
        factor_of = factor_of * jnp.repeat(heights, dims[axis_at] // shards_of).reshape([-1 if axis == axis_at else 1 for axis in range(len(dims))])
    return factor_of


def split_up(number_of, total, bound, skew):
    loads = [(1 << 20) // math.isqrt(rank ** skew) + 1 for rank in range(2, number_of + 1)]
    spare, holding = total - bound - (number_of - 1), [1] * (number_of - 1)
    while spare > 0:
        candidates = [i for i in range(number_of - 1) if holding[i] < bound]
        pool, remaining = sum([loads[i] for i in candidates]), spare
        for i in candidates:
            extra = min(bound - holding[i], max(1, remaining * loads[i] // pool), spare)
            holding[i] = holding[i] + extra
            spare = spare - extra
    return np.array([bound] + holding)


def ragged(stream_key, number_of, total, limit, slope):
    if number_of == 2:
        one = jax.random.randint(stream_key, (), max(1, total - limit), min(limit, total - 1) + 1)
        return jnp.stack([one, total - one])
    sizes = jnp.asarray(split_up(number_of, total, limit, slope), jnp.int32)
    twos = (number_of - 1) // 2
    giver, receiver = sizes[1:1 + 2 * twos:2], sizes[2:2 + 2 * twos:2]
    margin = jnp.minimum(giver - 1, limit - receiver)
    passed = jax.random.randint(jax.random.fold_in(stream_key, 1), (twos,), 0, 1 << 20) % (margin + 1)
    sizes = sizes.at[1:1 + 2 * twos:2].set(giver - passed).at[2:2 + 2 * twos:2].set(receiver + passed)
    return sizes[jax.random.permutation(jax.random.fold_in(stream_key, 2), number_of)]


def normal_values(own_key, extent, scale, limit, cuts=(), kind=jnp.bfloat16):
    result = scale * jax.random.normal(own_key, extent, jnp.float32)
    if cuts:
        result = result * block_levels(own_key, extent, cuts, -0.22, 0.18)
    return jnp.clip(result, -limit, limit).astype(kind)


def setup_inputs(seed: int = 0) -> dict:
    arg_keys = jax.random.split(jax.random.key(seed), 21)
    return {
        "content_ends": normal_values(arg_keys[0], (2, TOKENS, D), 1.0, 6.0, ((0, 2), (1, 16))),
        "query_ends": normal_values(arg_keys[1], (2, QTOKENS, D), 1.0, 6.0, ((0, 2), (1, 16))),
        "w_query": normal_values(arg_keys[2], (2, D, D), D ** -0.5, 0.21875, ((0, 2),)),
        "b_query": normal_values(arg_keys[3], (2, D), 0.3, 4.0, ((0, 2),), jnp.float32),
        "w_key": normal_values(arg_keys[4], (2, D, D), D ** -0.5, 0.21875, ((0, 2),)),
        "w_value": normal_values(arg_keys[5], (2, D, D), D ** -0.5, 0.21875, ((0, 2),)),
        "b_value": normal_values(arg_keys[6], (2, D), 0.3, 4.0, ((0, 2),), jnp.float32),
        "w_out": normal_values(arg_keys[7], (2, D, D), (D // 16) ** -0.5, 0.875, ((0, 2),)),
        "b_out": normal_values(arg_keys[8], (2, D), 0.3, 4.0, ((0, 2),), jnp.float32),
        "gain_attn": jnp.clip(1.0 + 0.15 * jax.random.normal(arg_keys[9], (2, D), jnp.float32), 0.25, 1.75),
        "shift_attn": normal_values(arg_keys[10], (2, D), 0.3, 4.0, ((0, 2),), jnp.float32),
        "w_up": normal_values(arg_keys[11], (2, D, FF), D ** -0.5, 0.21875, ((0, 2),)),
        "b_up": normal_values(arg_keys[12], (2, FF), 0.3, 4.0, ((0, 2),), jnp.float32),
        "w_down": normal_values(arg_keys[13], (2, FF, D), FF ** -0.5, 0.109375, ((0, 2),)),
        "b_down": normal_values(arg_keys[14], (2, D), 0.3, 4.0, ((0, 2),), jnp.float32),
        "gain_ffn": jnp.clip(1.0 + 0.15 * jax.random.normal(arg_keys[15], (2, D), jnp.float32), 0.25, 1.75),
        "shift_ffn": normal_values(arg_keys[16], (2, D), 0.3, 4.0, ((0, 2),), jnp.float32),
        "rel_table": normal_values(arg_keys[17], (2, BUCKETS, H), 1.0, 6.0, ((0, 2),), jnp.float32),
        "doc_lengths": jax.vmap(lambda own: ragged(own, DOCS, L, MOST, 2))(jax.random.split(arg_keys[18], (N_DP * MB))).reshape((N_DP * MB, DOCS)).astype(jnp.int32),
        "position_order": jax.vmap(lambda own: jax.random.permutation(own, L))(jax.random.split(arg_keys[19], (N_DP * MB))).reshape((N_DP * MB, L)).astype(jnp.int32),
    }


NORM_EPS = 1e-05
NEG_FILL = -1e+30
THRESHOLDS = (12, 16, 23, 32, 46, 64, 91)
HIGHEST = lax.Precision.HIGHEST

@jax.custom_vjp
def low(v):
    return lax.optimization_barrier(v.astype(jnp.bfloat16)).astype(jnp.float32)

@jax.custom_vjp
def low_back(v):
    return v

def low_keep(v):
    return (low(v), None)

def low_pass(kept, grad):
    return (grad,)

def back_keep(v):
    return (v, None)

def back_low(kept, grad):
    return (low(grad),)
low.defvjp(low_keep, low_pass)
low_back.defvjp(back_keep, back_low)

def rounded(value_in):
    return low_back(low(value_in))

def bucket_of(offset):
    distance = jnp.abs(offset)
    bucket = jnp.minimum(distance, 8) + 16 * (offset < 0).astype(jnp.int32)
    for bound_at in THRESHOLDS:
        bucket = bucket + (distance >= bound_at).astype(jnp.int32)
    return bucket

def layout(lengths, position_order):
    places = jnp.arange(L, dtype=jnp.int32)
    doc_ends = jnp.cumsum(lengths).astype(jnp.int32)
    doc_of = lax.optimization_barrier(jnp.sum((places[:, None] >= doc_ends[None, :]).astype(jnp.int32), axis=1, dtype=jnp.int32))
    ranked = lax.optimization_barrier(jnp.sum(jnp.where(position_order[None, :] == places[:, None], places[None, :], 0), axis=1, dtype=jnp.int32))
    visible_from = L - QL
    query_place = position_order[visible_from:]
    at_place = query_place[:, None] == places[None, :]
    query_doc = lax.optimization_barrier(jnp.sum(jnp.where(at_place, doc_of[None, :], 0), axis=1, dtype=jnp.int32))
    query_rank = visible_from + jnp.arange(QL, dtype=jnp.int32)
    unmasked = ranked[None, :] < visible_from
    content_mask = (doc_of[:, None] == doc_of[None, :]) & (unmasked | (ranked[None, :] <= ranked[:, None]))
    predict_mask = (query_doc[:, None] == doc_of[None, :]) & (unmasked | (ranked[None, :] < query_rank[:, None]) | at_place)
    content_bucket = bucket_of(places[:, None] - places[None, :])
    predict_bucket = bucket_of(query_place[:, None] - places[None, :])
    return (content_mask, predict_mask, content_bucket, predict_bucket)

def layer_norm(stacked, gain_vec, shift_vec):
    centered = stacked - lax.optimization_barrier(jnp.mean(stacked, axis=-1, keepdims=True))
    spread = lax.rsqrt(lax.optimization_barrier(jnp.mean(centered * centered, axis=-1, keepdims=True)) + NORM_EPS)
    return centered * spread * gain_vec + shift_vec

def product(left_rows, right_rows):
    return jnp.dot(left_rows, right_rows, precision=HIGHEST)

def attend(queries, key_rows, value_rows, bias_table, buckets, visible):
    count_rows = queries.shape[0]
    query_heads = queries.reshape(count_rows, H, HD)
    key_heads = key_rows.reshape(L, H, HD)
    value_heads = value_rows.reshape(L, H, HD)
    scaled = jnp.einsum('rhd,lhd->hrl', query_heads, key_heads, precision=HIGHEST) * HD ** (-0.5)
    offsets = jnp.transpose(bias_table[buckets], (2, 0, 1))
    scores = jnp.where(visible[None], low_back(scaled + offsets), NEG_FILL)
    weights_low = low(jax.nn.softmax(scores, axis=-1))
    mixed_rows = jnp.einsum('hrl,lhd->rhd', weights_low, value_heads, precision=HIGHEST)
    return rounded(mixed_rows.reshape(count_rows, D))

def finish(params, stream_in, mixed_rows):
    attn_sum = stream_in + low_back(product(mixed_rows, params['w_out']) + params['b_out'])
    normed = rounded(layer_norm(attn_sum, params['gain_attn'], params['shift_attn']))
    up_value = low_back(product(normed, params['w_up']) + params['b_up'])
    activated = low(jax.nn.gelu(up_value))
    ffn_sum = normed + low_back(product(activated, params['w_down']) + params['b_down'])
    return low(layer_norm(ffn_sum, params['gain_ffn'], params['shift_ffn']))

def layer(params, content, predicted, arranged):
    content = low_back(content)
    predicted = low_back(predicted)
    content_mask, predict_mask, content_bucket, predict_bucket = arranged
    queries_content = rounded(product(content, params['w_query']) + params['b_query'])
    queries_predict = rounded(product(predicted, params['w_query']) + params['b_query'])
    key_rows = rounded(product(content, params['w_key']))
    value_rows = rounded(product(content, params['w_value']) + params['b_value'])
    mixed_content = attend(queries_content, key_rows, value_rows, params['rel_table'], content_bucket, content_mask)
    mixed_predict = attend(queries_predict, key_rows, value_rows, params['rel_table'], predict_bucket, predict_mask)
    return (finish(params, content, mixed_content), finish(params, predicted, mixed_predict))

def two_layers(params, content, predicted, arranged):
    for layer_idx in range(2):
        chosen = {param_name: value_now[layer_idx] for param_name, value_now in params.items()}
        content, predicted = layer(chosen, content, predicted, arranged)
    return (content, predicted)

def reference(content_ends, query_ends, w_query, b_query, w_key, w_value, b_value, w_out, b_out, gain_attn, shift_attn, w_up, b_up, w_down, b_down, gain_ffn, shift_ffn, rel_table, doc_lengths, position_order):
    params = {'w_query': w_query.astype(jnp.float32), 'b_query': b_query, 'w_key': w_key.astype(jnp.float32), 'w_value': w_value.astype(jnp.float32), 'b_value': b_value, 'w_out': w_out.astype(jnp.float32), 'b_out': b_out, 'gain_attn': gain_attn, 'shift_attn': shift_attn, 'w_up': w_up.astype(jnp.float32), 'b_up': b_up, 'w_down': w_down.astype(jnp.float32), 'b_down': b_down, 'gain_ffn': gain_ffn, 'shift_ffn': shift_ffn, 'rel_table': rel_table}
    count_slots = N_DP * MB
    start_content = content_ends[0].astype(jnp.float32).reshape(count_slots, L, D)
    start_predict = query_ends[0].astype(jnp.float32).reshape(count_slots, QL, D)
    cot_content = content_ends[1].astype(jnp.float32).reshape(count_slots, L, D)
    cot_predict = query_ends[1].astype(jnp.float32).reshape(count_slots, QL, D)

    def bucket_step(running, slot_data):
        slot_content, slot_predict, slot_cot_content, slot_cot_predict, slot_lengths, slot_order = slot_data
        arranged = layout(slot_lengths, slot_order)
        outputs_now, pull_back = jax.vjp(lambda weights_now, content, predicted: two_layers(weights_now, content, predicted, arranged), params, slot_content, slot_predict)
        grad_params, grad_content, grad_predict = pull_back((slot_cot_content, slot_cot_predict))
        running = jax.tree.map(jnp.add, running, grad_params)
        return (running, (outputs_now[0], outputs_now[1], grad_content, grad_predict))
    zeros_tree = jax.tree.map(jnp.zeros_like, params)
    totals, stacked_out = lax.scan(bucket_step, zeros_tree, (start_content, start_predict, cot_content, cot_predict, doc_lengths, position_order))
    out_content, out_predict, grad_content, grad_predict = stacked_out
    content_out = jnp.stack([grad_content.reshape(-1, D), out_content.reshape(-1, D)]).astype(jnp.bfloat16)
    query_out = jnp.stack([grad_predict.reshape(-1, D), out_predict.reshape(-1, D)]).astype(jnp.bfloat16)
    return (content_out, query_out, totals['w_query'], totals['b_query'], totals['w_key'], totals['w_value'], totals['b_value'], totals['w_out'], totals['b_out'], totals['gain_attn'], totals['shift_attn'], totals['w_up'], totals['b_up'], totals['w_down'], totals['b_down'], totals['gain_ffn'], totals['shift_ffn'], totals['rel_table'])
```

```python
import functools
import math
from typing import Any, NamedTuple

import jax
import jax.numpy as jnp
from jax import lax
from jax.experimental import pallas as pl
from jax.experimental.pallas import tpu as pltpu
from jax.sharding import PartitionSpec as P

MESH = pl.DeviceIdType.MESH
F32 = jnp.float32
BF16 = jnp.bfloat16
NORM_EPS = 1e-05
NEG_FILL = -1e30
THRESHOLDS = (12, 16, 23, 32, 46, 64, 91)
TILE = 256
LANES = 128
MATRICES = 6
VMEM_LIMIT = 60 * 2**20


def reduce_kernel(steps, lag, grads, smalls, out, smalls_out, core_in, own, final, from_y, end_b, end_a, mid_a, mid_b, rung_b, small_in, small_sum,
                  own_sem, core_sem, y_sem, eb_sem, ea_sem, ma_sem, mb_sem, rb_sem, fe_sem, fy_sem, fm_sem, fb_sem, sib_sem, small_sem, small_send, store_sem, send_sem):
    pipe, place = lax.axis_index("pipe"), lax.axis_index("dp")
    base = place // 16 * 16
    local = place % 16
    z, y, c = local // 4, local // 2 % 2, local % 2
    is_end = (z == 0) | (z == 3)
    is_mid = (z == 1) | (z == 2)
    inner = jnp.where(z == 0, 1, 2)
    outer = jnp.where(z == 1, 0, 3)
    mine = z + 1
    other = 4 - z

    def at(zz, yy, cc):
        return (pipe, base + zz * 4 + yy * 2 + cc)

    sibling, y_peer, z_in, z_out, z_mid = at(z, y, 1 - c), at(z, 1 - y, c), at(inner, y, c), at(outer, y, c), at(3 - z, y, c)
    partners = [(pipe, base + jnp.bitwise_xor(local, 1 << j)) for j in range(4)]

    barrier = pltpu.get_barrier_semaphore()

    def greet(device):
        pl.semaphore_signal(barrier, inc=1, device_id=device, device_id_type=MESH)

    for device in partners:
        greet(device)
    @pl.when(is_mid)
    def _():
        greet(z_mid)
        pl.semaphore_wait(barrier, 5)

    @pl.when(is_end)
    def _():
        pl.semaphore_wait(barrier, 4)

    def remote(src, dst, which, sem, device):
        return pltpu.make_async_remote_copy(src_ref=src, dst_ref=dst, send_sem=send_sem.at[which], recv_sem=sem, device_id=device, device_id_type=MESH)

    def recv(dst, sem):
        pltpu.make_async_copy(dst, dst, sem).wait()

    def small_copy(j):
        src = smalls if j == 0 else small_sum.at[j - 1]
        return pltpu.make_async_remote_copy(src_ref=src, dst_ref=small_in.at[j], send_sem=small_send.at[j], recv_sem=small_sem.at[j], device_id=partners[j], device_id_type=MESH)

    def small_step(j):
        cp = small_copy(j)
        cp.wait()
        held = smalls[...] if j == 0 else small_sum[j - 1]
        if j < 3:
            small_sum[j] = held + small_in[j]
            small_copy(j + 1).start()
        else:
            smalls_out[...] = held + small_in[j]

    small_copy(0).start()

    def s0(k):
        remote(grads.at[1 - c, k], core_in.at[k], 0, core_sem.at[k], sibling).start()
        pltpu.make_async_copy(grads.at[c, k], own.at[k], own_sem.at[k]).start()

    def s1(k):
        pltpu.make_async_copy(grads.at[c, k], own.at[k], own_sem.at[k]).wait()
        recv(core_in.at[k], core_sem.at[k])
        core_in[k] = (core_in[k].astype(F32) + own[k].astype(F32)).astype(BF16)
        remote(core_in.at[k, 1 - y], from_y.at[k], 1, y_sem.at[k], y_peer).start()

        @pl.when(is_end)
        def _():
            remote(core_in.at[k, pl.ds(2, 2)], end_b.at[k], 2, eb_sem.at[k], z_in).start()

    def s2(k):
        recv(from_y.at[k], y_sem.at[k])
        core_in[k, y] = (core_in[k, y].astype(F32) + from_y[k].astype(F32)).astype(BF16)

        @pl.when(is_end)
        def _():
            remote(core_in.at[k, y], end_a.at[k], 3, ea_sem.at[k], z_in).start()

        @pl.when(is_mid)
        def _():
            recv(end_b.at[k], eb_sem.at[k])
            core_in[k, pl.ds(2, 2)] = (core_in[k, pl.ds(2, 2)].astype(F32) + end_b[k].astype(F32)).astype(BF16)
            remote(core_in.at[k, other], mid_b.at[k], 4, mb_sem.at[k], z_mid).start()

    def s3(k):
        @pl.when(is_mid)
        def _():
            recv(end_a.at[k], ea_sem.at[k])
            core_in[k, y] = (core_in[k, y].astype(F32) + end_a[k].astype(F32)).astype(BF16)
            remote(core_in.at[k, y], mid_a.at[k], 5, ma_sem.at[k], z_mid).start()
            recv(mid_b.at[k], mb_sem.at[k])
            core_in[k, mine] = (core_in[k, mine].astype(F32) + mid_b[k].astype(F32)).astype(BF16)
            remote(core_in.at[k, mine], rung_b.at[k], 6, rb_sem.at[k], y_peer).start()

    def s4(k):
        @pl.when(is_mid)
        def _():
            recv(mid_a.at[k], ma_sem.at[k])
            final[c, k, y] = (core_in[k, y].astype(F32) + mid_a[k].astype(F32)).astype(BF16)
            remote(final.at[c, k, y], final.at[c, k, y], 7, fe_sem.at[k], z_out).start()
            remote(final.at[c, k, y], final.at[c, k, y], 8, fy_sem.at[k], y_peer).start()
            recv(rung_b.at[k], rb_sem.at[k])
            final[c, k, mine] = (core_in[k, mine].astype(F32) + rung_b[k].astype(F32)).astype(BF16)
            remote(final.at[c, k, mine], final.at[c, k, mine], 9, fm_sem.at[k], z_mid).start()

    def s5(k):
        @pl.when(is_end)
        def _():
            recv(final.at[c, k, y], fe_sem.at[k])
            remote(final.at[c, k, y], final.at[c, k, y], 8, fy_sem.at[k], y_peer).start()

        @pl.when(is_mid)
        def _():
            recv(final.at[c, k, other], fm_sem.at[k])
            remote(final.at[c, k, pl.ds(2, 2)], final.at[c, k, pl.ds(2, 2)], 10, fb_sem.at[k], z_out).start()

    def s6(k):
        recv(final.at[c, k, 1 - y], fy_sem.at[k])

        @pl.when(is_end)
        def _():
            recv(final.at[c, k, pl.ds(2, 2)], fb_sem.at[k])

        remote(final.at[c, k], final.at[c, k], 11, sib_sem.at[k], sibling).start()
        pltpu.make_async_copy(final.at[c, k], out.at[c, k], store_sem.at[0]).start()

    def s7(k):
        recv(final.at[1 - c, k], sib_sem.at[k])
        pltpu.make_async_copy(final.at[1 - c, k], out.at[1 - c, k], store_sem.at[1]).start()

    stages = (s0, s1, s2, s3, s4, s5, s6, s7)
    offsets = lag
    at_small = [min(steps - 1, 4 * (j + 1)) for j in range(4)]

    @pl.loop(0, steps + offsets[-1])
    def _(t):
        for stage, off in zip(stages, offsets):
            k = t - off

            @pl.when((k >= 0) & (k < steps))
            def _():
                stage(jnp.clip(k, 0, steps - 1))

        for j in range(4):
            @pl.when(t == 4 * (j + 1))
            def _():
                small_step(j)

    def sent(ref, which):
        pltpu.make_async_copy(ref, ref, send_sem.at[which]).wait()

    sent(core_in, 0)
    sent(from_y, 1)
    sent(final.at[0], 11)
    pltpu.make_async_copy(final.at[0], out.at[0], store_sem.at[0]).wait()
    pltpu.make_async_copy(final.at[0], out.at[0], store_sem.at[1]).wait()
    sent(from_y, 8)

    @pl.when(is_end)
    def _():
        sent(end_b, 2)
        sent(end_a, 3)

    @pl.when(is_mid)
    def _():
        for which in (4, 5, 6, 7, 9):
            sent(mid_a, which)
        sent(end_b, 10)


def reduce_call(grads, smalls, lag, cid=1):
    _, steps, _, rows, width = grads.shape
    block = (steps, rows, width)
    sems = [pltpu.SemaphoreType.DMA((steps,)) for _ in range(13)]
    return pl.pallas_call(
        functools.partial(reduce_kernel, steps, lag),
        out_shape=(jax.ShapeDtypeStruct(grads.shape, BF16), jax.ShapeDtypeStruct(smalls.shape, F32)),
        in_specs=[pl.BlockSpec(memory_space=pl.ANY), pl.BlockSpec(memory_space=pltpu.VMEM)],
        out_specs=(pl.BlockSpec(memory_space=pl.ANY), pl.BlockSpec(memory_space=pltpu.VMEM)),
        scratch_shapes=[
            pltpu.VMEM((steps, 4, rows, width), BF16),
            pltpu.VMEM((steps, 4, rows, width), BF16),
            pltpu.VMEM(grads.shape, BF16),
            pltpu.VMEM(block, BF16),
            pltpu.VMEM((steps, 2, rows, width), BF16),
            pltpu.VMEM(block, BF16),
            pltpu.VMEM(block, BF16),
            pltpu.VMEM(block, BF16),
            pltpu.VMEM(block, BF16),
            pltpu.VMEM((4,) + smalls.shape, F32),
            pltpu.VMEM((3,) + smalls.shape, F32),
            *sems,
            pltpu.SemaphoreType.DMA((4,)),
            pltpu.SemaphoreType.DMA((4,)),
            pltpu.SemaphoreType.DMA((2,)),
            pltpu.SemaphoreType.DMA((12,)),
        ],
        compiler_params=pltpu.CompilerParams(collective_id=cid, has_side_effects=True, vmem_limit_bytes=56 * 2**20),
    )(grads, smalls)


class Sizes(NamedTuple):
    micro: int
    seq: int
    query: int
    width: int
    heads: int
    hidden: int
    buckets: int

    @property
    def block(self):
        return self.seq + self.query

    @property
    def rows(self):
        return self.micro * self.block

    @property
    def pairs(self):
        return self.width // LANES


class Weights(NamedTuple):
    query: Any
    key: Any
    value: Any
    out: Any
    up: Any
    down: Any


class Vectors(NamedTuple):
    b_query: Any
    b_value: Any
    b_out: Any
    gain_attn: Any
    shift_attn: Any
    b_up: Any
    b_down: Any
    gain_ffn: Any
    shift_ffn: Any
    rel_table: Any
    lengths: Any
    order: Any


class State(NamedTuple):
    left: Any
    qkv: Any
    slope: Any
    probs: Any
    norm_attn: Any
    norm_ffn: Any
    spread_attn: Any
    spread_ffn: Any


def state_shapes(n):
    return State(
        ((n.rows, 3 * n.width + n.hidden), BF16),
        ((n.rows, 3 * n.width), BF16),
        ((n.rows, n.hidden), BF16),
        ((n.micro * n.pairs, 2 * n.block, n.seq), F32),
        ((n.rows, n.width), F32),
        ((n.rows, n.width), F32),
        ((n.rows, 1), F32),
        ((n.rows, 1), F32),
    )


def dot(a, b):
    return jnp.dot(a, b, preferred_element_type=F32)


def dot_nt(a, b, precision=None):
    return lax.dot_general(a, b, (((1,), (1,)), ((), ())), precision=precision, preferred_element_type=F32)


def dot_tn(a, b, precision=None):
    return lax.dot_general(a, b, (((0,), (0,)), ((), ())), precision=precision, preferred_element_type=F32)


def iota(shape, dim):
    return lax.broadcasted_iota(jnp.int32, shape, dim)


def cols(at, size=TILE):
    return pl.ds(pl.multiple_of(at * size, size), size)


def bucket_of(offset):
    distance = jnp.abs(offset)
    bucket = jnp.minimum(distance, 8) + jnp.where(offset < 0, 16, 0)
    for bound_at in THRESHOLDS:
        bucket = bucket + jnp.where(distance >= bound_at, 1, 0)
    return bucket


def place_buckets(n):
    shape = (n.buckets, 2 * n.seq)
    at = iota(shape, 1)
    offset = jnp.where(at < n.seq, -at, 2 * n.seq - at)
    return jnp.where(bucket_of(offset) == iota(shape, 0), 1.0, 0.0)


def to_column(row, n):
    shape = (n.seq, n.seq)
    return jnp.sum(jnp.where(iota(shape, 0) == iota(shape, 1), row, 0.0), axis=1, keepdims=True)


def picked(order_col, n, place):
    return order_col[n.seq - n.query :] == place.astype(F32)


def bias_and_mask(n, v, bias):
    seq, query = n.seq, n.query
    base = dot_tn(v.rel_table[0], place_buckets(n), lax.Precision.HIGHEST)
    square = (seq, seq)
    row_at, col_at = iota(square, 0).astype(F32), iota(square, 1).astype(F32)
    visible_from = float(seq - query)
    content_sees, query_sees, chosen = [], [], []
    for b in range(n.micro):
        order_row = v.order[b : b + 1, :].astype(F32)
        order_col = to_column(order_row, n)
        rank_row = jnp.sum(jnp.where(order_col == col_at, row_at, 0.0), axis=0, keepdims=True)
        rank_col = to_column(rank_row, n)
        ends, total = [], jnp.int32(0)
        for d in range(v.lengths.shape[1]):
            total = total + v.lengths[b, d]
            ends.append(total)

        def doc_of(at):
            found = jnp.zeros(at.shape, F32)
            for end in ends:
                found = found + jnp.where(at >= end.astype(F32), 1.0, 0.0)
            return found

        doc_row = doc_of(iota((1, seq), 1).astype(F32))
        doc_col = doc_of(iota((seq, 1), 0).astype(F32))
        unmasked = rank_row < visible_from
        content_sees.append((doc_col == doc_row) & (unmasked | (rank_row <= rank_col)))
        at_place = picked(order_col, n, iota((query, seq), 1))
        place = order_col[seq - query :]
        rank = visible_from + iota((query, 1), 0).astype(F32)
        query_sees.append((doc_of(place) == doc_row) & (unmasked | (rank_row < rank) | at_place))
        chosen.append(jnp.where(at_place, 1.0, 0.0).astype(BF16))
    for h in range(n.heads):
        spread = jnp.broadcast_to(base[h : h + 1, :], (seq, 2 * seq))
        table = pltpu.roll(spread, 0, 1, stride=1, stride_axis=0)[:, :seq]
        high = table.astype(BF16)
        rest = table - high.astype(F32)
        middle = rest.astype(BF16)
        low = (rest - middle.astype(F32)).astype(BF16)
        for b in range(n.micro):
            of_query = dot(chosen[b], high) + dot(chosen[b], middle) + dot(chosen[b], low)
            start = (h % 2) * n.block
            bias[b, h // 2, start : start + seq, :] = jnp.where(content_sees[b], table, NEG_FILL)
            bias[b, h // 2, start + seq : start + n.block, :] = jnp.where(query_sees[b], of_query, NEG_FILL)


def half_masks():
    at = iota((1, LANES), 1)
    return jnp.where(at < LANES // 2, 1.0, 0.0).astype(BF16), jnp.where(at < LANES // 2, 0.0, 1.0).astype(BF16)


def both_heads(values):
    first, second = half_masks()
    return jnp.concatenate([values * first, values * second], axis=0)


def side_by_side(stacked):
    half = stacked.shape[0] // 2
    return jnp.concatenate([stacked[:half], stacked[half:]], axis=1)


def norm_rows(n, summed, spread_ref, gain, shift, write):
    step = n.block // 3

    @pl.loop(0, n.rows // step)
    def _(i):
        rows = pl.ds(pl.multiple_of(i * step, step), step)
        r = summed[rows, :]
        centered = r - jnp.mean(r, axis=1, keepdims=True)
        spread = lax.rsqrt(jnp.mean(centered * centered, axis=1, keepdims=True) + NORM_EPS)
        normed = centered * spread
        summed[rows, :] = normed
        spread_ref[rows, :] = spread
        write(rows, (normed * gain + shift).astype(BF16))


def norm_back(n, grad_of, normed_ref, spread_ref, gain, write):
    step = n.block // 3

    def body(i, sums):
        rows = pl.ds(pl.multiple_of(i * step, step), step)
        grad = grad_of(rows)
        normed = normed_ref[rows, :]
        scaled = grad * gain
        inner = jnp.mean(scaled * normed, axis=1, keepdims=True)
        back = spread_ref[rows, :] * (scaled - jnp.mean(scaled, axis=1, keepdims=True) - normed * inner)
        write(rows, back)
        low = back.astype(BF16).astype(F32)
        return (
            sums[0] + jnp.sum(grad * normed, axis=0, keepdims=True),
            sums[1] + jnp.sum(grad, axis=0, keepdims=True),
            sums[2] + jnp.sum(low, axis=0, keepdims=True),
        )

    zero = jnp.zeros((1, n.width), F32)
    return lax.fori_loop(0, n.rows // step, body, (zero, zero, zero))


def forward(n, ready, w, v, bias, s, y):
    width, tiles = n.width, n.width // TILE
    left_o, left_h, left_u = tiles, 2 * tiles, 3 * tiles
    for i, matrix in enumerate((w.query, w.key, w.value)):
        ready(i)

        @pl.loop(0, tiles)
        def _(t):
            product = dot(s.left[:, :width], matrix[:, cols(t)])
            if i == 0:
                product = product + v.b_query[:, cols(t)]
            if i == 2:
                product = product + v.b_value[:, cols(t)]
            s.qkv[:, cols(i * tiles + t)] = product.astype(BF16)

    factor = (LANES // 2) ** -0.5

    @pl.loop(0, n.micro * n.pairs)
    def _(it):
        b, pair = it // n.pairs, it % n.pairs
        rows = pl.ds(pl.multiple_of(b * n.block, 16), n.block)
        keys = pl.ds(pl.multiple_of(b * n.block, 16), n.seq)
        q = both_heads(s.qkv[rows, cols(pair, LANES)])
        k = s.qkv[keys, cols(n.pairs + pair, LANES)]
        val = both_heads(s.qkv[keys, cols(2 * n.pairs + pair, LANES)])
        scores = dot_nt(q, k) * factor + bias[b, pair]
        powers = jnp.exp(scores - jnp.max(scores, axis=1, keepdims=True))
        probs = powers / jnp.sum(powers, axis=1, keepdims=True)
        s.probs[it] = probs
        mixed = dot(side_by_side(probs.astype(BF16)), val)
        s.left[rows, cols(n.pairs + pair, LANES)] = mixed.astype(BF16)

    ready(3)

    @pl.loop(0, tiles)
    def _(t):
        product = dot(s.left[:, width : 2 * width], w.out[:, cols(t)])
        s.norm_attn[:, cols(t)] = s.left[:, cols(t)].astype(F32) + product + v.b_out[:, cols(t)]

    def keep_h1(rows, value):
        s.left[rows, 2 * width : 3 * width] = value

    norm_rows(n, s.norm_attn, s.spread_attn, v.gain_attn[...], v.shift_attn[...], keep_h1)
    ready(4)

    @pl.loop(0, n.hidden // TILE)
    def _(t):
        z = dot(s.left[:, 2 * width : 3 * width], w.up[:, cols(t)]) + v.b_up[:, cols(t)]
        c = (2 / math.pi) ** 0.5
        square = z * z
        bend = jnp.tanh(c * z * (1.0 + 0.044715 * square))
        half = 0.5 * (1.0 + bend)
        s.left[:, cols(left_u + t)] = (z * half).astype(BF16)
        s.slope[:, cols(t)] = (half + 0.5 * c * z * (1.0 - bend * bend) * (1.0 + 0.134145 * square)).astype(BF16)

    ready(5)

    @pl.loop(0, tiles)
    def _(t):
        product = dot(s.left[:, 3 * width :], w.down[:, cols(t)])
        s.norm_ffn[:, cols(t)] = s.left[:, cols(left_h + t)].astype(F32) + product + v.b_down[:, cols(t)]

    def keep_y(rows, value):
        y[rows, :] = value

    norm_rows(n, s.norm_ffn, s.spread_ffn, v.gain_ffn[...], v.shift_ffn[...], keep_y)


def backward(n, ready, w, v, s, dy, right, smalls, resid, table_sum, dx):
    width, tiles = n.width, n.width // TILE
    hidden_tiles = n.hidden // TILE
    at_da, at_dz = 3 * tiles, 4 * tiles
    at_df = at_dz + hidden_tiles
    df_cols = slice(at_df * TILE, at_df * TILE + width)
    da_cols = slice(3 * width, 4 * width)

    def keep_df(rows, value):
        resid[rows, :] = value
        right[rows, df_cols] = value.astype(BF16)

    gain, shift, low = norm_back(n, lambda rows: dy[rows, :].astype(F32), s.norm_ffn, s.spread_ffn, v.gain_ffn[...], keep_df)
    smalls[10:11, :], smalls[11:12, :], smalls[9:10, :] = gain, shift, low
    ready(5)

    @pl.loop(0, n.hidden // width)
    def _(group):
        @pl.loop(0, tiles)
        def _(inside):
            t = group * tiles + inside
            spread = dot_nt(right[:, df_cols], w.down[cols(t), :])
            dz = (spread * s.slope[:, cols(t)].astype(F32)).astype(BF16)
            right[:, cols(at_dz + t)] = dz
            smalls[pl.ds(5 + group, 1), cols(inside)] = jnp.sum(dz.astype(F32), axis=0, keepdims=True)

    ready(4)

    @pl.loop(0, tiles)
    def _(t):
        spread = dot_nt(right[:, at_dz * TILE : at_df * TILE], w.up[cols(t), :])
        dy[:, cols(t)] = (spread + resid[:, cols(t)]).astype(BF16)

    def keep_da(rows, value):
        resid[rows, :] = value
        right[rows, da_cols] = value.astype(BF16)

    gain, shift, low = norm_back(n, lambda rows: dy[rows, :].astype(F32), s.norm_attn, s.spread_attn, v.gain_attn[...], keep_da)
    smalls[3:4, :], smalls[4:5, :], smalls[2:3, :] = gain, shift, low
    ready(3)

    @pl.loop(0, tiles)
    def _(t):
        dy[:, cols(t)] = dot_nt(right[:, da_cols], w.out[cols(t), :]).astype(BF16)

    factor = (LANES // 2) ** -0.5
    table_sum[...] = jnp.zeros(table_sum.shape, F32)
    for b in range(n.micro):
        order_col = to_column(v.order[b : b + 1, :].astype(F32), n)
        square = (n.seq, n.seq)
        same = jnp.where(iota(square, 0) + iota(square, 1) == n.seq - 1, 1.0, 0.0)
        predicted = picked(order_col, n, n.seq - 1 - iota((n.query, n.seq), 1))
        chosen = jnp.concatenate([same, jnp.where(predicted, 1.0, 0.0)], axis=0).astype(BF16)

        @pl.loop(0, n.pairs)
        def _(pair):
            it = b * n.pairs + pair
            rows = slice(b * n.block, (b + 1) * n.block)
            keys = slice(b * n.block, b * n.block + n.seq)
            rest = slice(b * n.block + n.seq, (b + 1) * n.block)
            grad = both_heads(dy[rows, cols(pair, LANES)])
            q = both_heads(s.qkv[rows, cols(pair, LANES)])
            k = both_heads(s.qkv[keys, cols(n.pairs + pair, LANES)])
            val = s.qkv[keys, cols(2 * n.pairs + pair, LANES)]
            probs = s.probs[it]
            grad_probs = dot_nt(grad, val)
            inner = jnp.sum(probs * grad_probs, axis=1, keepdims=True)
            grad_scores = (probs * (grad_probs - inner)).astype(BF16)
            right[rows, cols(pair, LANES)] = (dot(side_by_side(grad_scores), k) * factor).astype(BF16)
            right[keys, cols(n.pairs + pair, LANES)] = (dot_tn(grad_scores, q) * factor).astype(BF16)
            right[keys, cols(2 * n.pairs + pair, LANES)] = dot_tn(probs.astype(BF16), grad).astype(BF16)
            none = jnp.zeros((n.query, LANES), BF16)
            right[rest, cols(n.pairs + pair, LANES)] = none
            right[rest, cols(2 * n.pairs + pair, LANES)] = none
            for half in range(2):
                of_head = grad_scores[half * n.block : (half + 1) * n.block]
                table_sum[2 * pair + half] += dot_tn(chosen, of_head)

    smalls[0:1, :] = jnp.sum(right[:, :width].astype(F32), axis=0, keepdims=True)
    smalls[1:2, :] = jnp.sum(right[:, 2 * width : 3 * width].astype(F32), axis=0, keepdims=True)
    by_place = []
    for h in range(n.heads):
        wide = jnp.concatenate([table_sum[h], jnp.zeros((n.seq, n.seq), F32)], axis=1)
        turned = pltpu.roll(wide, n.seq + 1, 1, stride=1, stride_axis=0)
        by_place.append(jnp.sum(turned, axis=0, keepdims=True))
    by_place = jnp.concatenate(by_place, axis=0)
    smalls[12 : 12 + n.heads, : n.buckets] = dot_nt(by_place, place_buckets(n), lax.Precision.HIGHEST)
    ready(0)
    ready(1)
    ready(2)

    @pl.loop(0, tiles)
    def _(t):
        total = resid[:, cols(t)]
        for i, matrix in enumerate((w.query, w.key, w.value)):
            total = total + dot_nt(right[:, i * width : (i + 1) * width], matrix[cols(t), :])
        dx[:, cols(t)] = total.astype(BF16)


def weight_grads(n, left, right, packed, write):
    width, tiles = n.width, n.width // TILE
    up_groups = n.hidden // width

    def tile(at, left_tile, right_group):
        lhs = left[:, cols(left_tile)]
        rhs = right[:, pl.ds(pl.multiple_of(right_group * width, width), width)]
        packed[cols(at), :] = dot_tn(lhs, rhs).astype(BF16)
        write(at)

    @pl.loop(0, 3 * tiles)
    def _(i):
        tile(i, i % tiles, i // tiles)

    @pl.loop(0, tiles)
    def _(i):
        tile(3 * tiles + i, tiles + i, 3)

    @pl.loop(0, up_groups * tiles)
    def _(i):
        tile(4 * tiles + i, 2 * tiles + i % tiles, 4 + i // tiles)

    @pl.loop(0, n.hidden // TILE)
    def _(i):
        tile((4 + up_groups) * tiles + i, 3 * tiles + i, 4 + up_groups)


def copies_of(pairs, sems):
    return [pltpu.make_async_copy(src, dst, sems.at[i]) for i, (src, dst) in enumerate(pairs)]


def rows_in(n, content, query, wide, sems, back=False):
    pairs = []
    for b in range(n.micro):
        pairs.append((content.at[0, pl.ds(b * n.seq, n.seq)], wide.at[pl.ds(b * n.block, n.seq)]))
        pairs.append((query.at[0, pl.ds(b * n.query, n.query)], wide.at[pl.ds(b * n.block + n.seq, n.query)]))
    if back:
        pairs = [(dst, src) for src, dst in pairs]
    return copies_of(pairs, sems)


def once(copies):
    done = set()

    def ready(i):
        if i not in done:
            done.add(i)
            copies[i].wait()

    return ready


def first_kernel(n, *refs):
    content, query, *refs = refs
    w_hbm, refs = Weights(*refs[:6]), refs[6:]
    v, refs = Vectors(*refs[:12]), refs[12:]
    y, refs = refs[0], refs[1:]
    s_out, refs = State(*refs[:8]), refs[8:]
    w, refs = Weights(*refs[:6]), refs[6:]
    s, refs = State(*refs[:8]), refs[8:]
    bias, w_sem, row_sem, s_sem = refs

    @pl.when(lax.axis_index("pipe") == 0)
    def _():
        rows = rows_in(n, content, query, s.left.at[:, pl.ds(0, n.width)], row_sem)
        for cp in rows:
            cp.start()
        weights = copies_of([(a.at[0], b) for a, b in zip(w_hbm, w)], w_sem)
        for cp in weights:
            cp.start()
        bias_and_mask(n, v, bias)
        for cp in rows:
            cp.wait()
        forward(n, once(weights), w, v, bias, s, y)
        kept = copies_of(list(zip(s, s_out)), s_sem)
        for cp in kept:
            cp.start()
        for cp in kept:
            cp.wait()


def second_kernel(n, *refs):
    arrived, content, query, *refs = refs
    w_hbm, refs = Weights(*refs[:6]), refs[6:]
    v, refs = Vectors(*refs[:12]), refs[12:]
    y, dx, left_out, right_out, smalls, *refs = refs
    w, refs = Weights(*refs[:6]), refs[6:]
    s, refs = State(*refs[:8]), refs[8:]
    bias, dy, right, resid, table_sum, w_sem, row_sem, s_sem = refs

    @pl.when(lax.axis_index("pipe") == 1)
    def _():
        rows = rows_in(n, content, query, dy, row_sem)
        mine = pltpu.make_async_copy(arrived, s.left.at[:, pl.ds(0, n.width)], s_sem.at[0])
        mine.start()
        weights = copies_of([(a.at[0], b) for a, b in zip(w_hbm, w)], w_sem)
        for cp in weights:
            cp.start()
        for cp in rows:
            cp.start()
        bias_and_mask(n, v, bias)
        mine.wait()
        ready = once(weights)
        forward(n, ready, w, v, bias, s, y)
        for cp in rows:
            cp.wait()
        kept = pltpu.make_async_copy(s.left, left_out, s_sem.at[0])
        kept.start()
        backward(n, ready, w, v, s, dy, right, smalls, resid, table_sum, dx)
        also = pltpu.make_async_copy(right, right_out, s_sem.at[1])
        also.start()
        kept.wait()
        also.wait()


def third_kernel(n, *refs):
    arrived, y, left_in, right_in, smalls_in, *refs = refs
    s_in, refs = State(*refs[:8]), refs[8:]
    w_hbm, refs = Weights(*refs[:6]), refs[6:]
    v, refs = Vectors(*refs[:12]), refs[12:]
    content_out, query_out, packed_out, smalls, *refs = refs
    w, refs = Weights(*refs[:6]), refs[6:]
    s, refs = State(*refs[:8]), refs[8:]
    dy, dx, right, resid, table_sum, packed, w_sem, row_sem, s_sem, out_sem = refs
    pipe = lax.axis_index("pipe")

    @pl.when(pipe == 0)
    def _():
        mine = pltpu.make_async_copy(arrived, dy, row_sem.at[0])
        mine.start()
        kept = copies_of(list(zip(s_in, s)), s_sem)
        for cp in reversed(kept):
            cp.start()
        weights = copies_of([(a.at[0], b) for a, b in zip(w_hbm, w)], w_sem)
        for cp in reversed(weights):
            cp.start()
        mine.wait()
        for cp in kept:
            cp.wait()
        backward(n, once(weights), w, v, s, dy, right, smalls, resid, table_sum, dx)

    @pl.when(pipe == 1)
    def _():
        kept = copies_of([(left_in, s.left), (right_in, right), (y, dx)], s_sem)
        for cp in kept:
            cp.start()
        smalls[...] = smalls_in[...]
        for cp in kept:
            cp.wait()

    outs = rows_in(n, content_out, query_out, dx, row_sem, back=True)
    for cp in outs:
        cp.start()

    def store(at):
        return pltpu.make_async_copy(packed.at[cols(at)], packed_out.at[cols(at)], out_sem)

    weight_grads(n, s.left, right, packed, lambda at: store(at).start())
    for cp in outs:
        cp.wait()
    pltpu.make_async_copy(packed, packed_out, out_sem).wait()


def any_specs(count):
    return [pl.BlockSpec(memory_space=pl.ANY)] * count


def vector_specs():
    vmem = pl.BlockSpec(memory_space=pltpu.VMEM)
    return [vmem] * 10 + [pl.BlockSpec(memory_space=pltpu.SMEM), vmem]


def shaped(shape, dtype=BF16):
    return jax.ShapeDtypeStruct(shape, dtype)


def run_layers(n, content, query, w, v):
    rows, width = n.rows, n.width
    act = shaped((rows, width))
    packed = ((4 * width + 2 * n.hidden), width)
    right = (rows, 5 * width + n.hidden)
    small_shape = (24, width)
    w_scratch = [pltpu.VMEM(m.shape[1:], BF16) for m in w]
    s_shapes = state_shapes(n)
    s_scratch = [pltpu.VMEM(shape, dtype) for shape, dtype in s_shapes]
    bias = pltpu.VMEM((n.micro, n.pairs, 2 * n.block, n.seq), F32)
    dma = pltpu.SemaphoreType.DMA
    params = pltpu.CompilerParams(vmem_limit_bytes=VMEM_LIMIT)
    vmem, anywhere = pl.BlockSpec(memory_space=pltpu.VMEM), pl.BlockSpec(memory_space=pl.ANY)
    y0, *kept = pl.pallas_call(
        functools.partial(first_kernel, n),
        out_shape=[act] + [shaped(*s) for s in s_shapes],
        in_specs=any_specs(8) + vector_specs(),
        out_specs=[vmem] + any_specs(8),
        scratch_shapes=w_scratch + s_scratch + [bias, dma((6,)), dma((2 * n.micro,)), dma((8,))],
        compiler_params=params,
    )(content, query, *w, *v)
    arrived = lax.ppermute(y0, "pipe", [(0, 1)])
    y1, dx1, left1, right1, smalls1 = pl.pallas_call(
        functools.partial(second_kernel, n),
        out_shape=[act, act, shaped(s_shapes.left[0]), shaped(right), shaped(small_shape, F32)],
        in_specs=any_specs(9) + vector_specs(),
        out_specs=[vmem, vmem, anywhere, anywhere, vmem],
        scratch_shapes=w_scratch
        + s_scratch
        + [bias, pltpu.VMEM((rows, width), BF16), pltpu.VMEM(right, BF16), pltpu.VMEM((rows, width), F32), pltpu.VMEM((n.heads, n.seq, n.seq), F32)]
        + [dma((6,)), dma((2 * n.micro,)), dma((2,))],
        compiler_params=params,
    )(arrived, content, query, *w, *v)
    returned = lax.ppermute(dx1, "pipe", [(1, 0)])
    return pl.pallas_call(
        functools.partial(third_kernel, n),
        out_shape=[shaped(content.shape), shaped(query.shape), shaped(packed), shaped(small_shape, F32)],
        in_specs=any_specs(4) + [vmem] + any_specs(14) + vector_specs(),
        out_specs=any_specs(3) + [vmem],
        scratch_shapes=w_scratch
        + s_scratch
        + [pltpu.VMEM((rows, width), BF16), pltpu.VMEM((rows, width), BF16), pltpu.VMEM(right, BF16), pltpu.VMEM((rows, width), F32), pltpu.VMEM((n.heads, n.seq, n.seq), F32), pltpu.VMEM(packed, BF16)]
        + [dma((6,)), dma((2 * n.micro,)), dma((8,)), dma],
        compiler_params=params,
    )(returned, y1, left1, right1, smalls1, *kept, *w, *v)


def unpack(n, packed, smalls):
    width, heads = n.width, n.heads
    parts = packed.reshape(-1, width, width)
    groups = n.hidden // width
    whole = [parts[i].astype(F32)[None] for i in range(4)]
    whole.append(jnp.concatenate([parts[4 + i] for i in range(groups)], axis=1).astype(F32)[None])
    whole.append(packed[(4 + groups) * width :].astype(F32)[None])
    vectors = [smalls[i : i + 1] for i in range(5)]
    vectors.append(smalls[5 : 5 + groups].reshape(1, n.hidden))
    vectors += [smalls[i : i + 1] for i in range(5 + groups, 8 + groups)]
    vectors.append(smalls[12 : 12 + heads, : n.buckets].T[None])
    return whole, vectors


def all_sums(packed, smalls):
    steps_of = 8 * 16
    size = lax.axis_size("dp")
    if size % 16 or packed.shape[0] % steps_of:
        return lax.psum(packed.astype(F32), "dp"), lax.psum(smalls, "dp")
    lag = (0, 2, 4, 6, 8, 10, 12, 14)
    width = packed.shape[1]
    final, smalls = reduce_call(packed.reshape(2, packed.shape[0] // steps_of, 4, 16, width), smalls, lag)
    if size > 16:
        groups = [[b * 16 + i for b in range(size // 16)] for i in range(16)]
        final = lax.psum(final.astype(F32), "dp", axis_index_groups=groups)
        smalls = lax.psum(smalls, "dp", axis_index_groups=groups)
    return final.reshape(packed.shape), smalls


def on_device(content_ends, query_ends, w_query, b_query, w_key, w_value, b_value, w_out, b_out, gain_attn, shift_attn, w_up, b_up, w_down, b_down, gain_ffn, shift_ffn, rel_table, doc_lengths, position_order):
    micro, seq = position_order.shape
    n = Sizes(micro, seq, query_ends.shape[1] // micro, content_ends.shape[2], rel_table.shape[2], w_up.shape[2], rel_table.shape[1])
    w = Weights(w_query, w_key, w_value, w_out, w_up, w_down)
    v = Vectors(b_query, b_value, b_out, gain_attn, shift_attn, b_up, b_down, gain_ffn, shift_ffn, rel_table, doc_lengths, position_order)
    content_out, query_out, packed, smalls = run_layers(n, content_ends, query_ends, w, v)
    packed, smalls = all_sums(packed, smalls)
    g, d = unpack(n, packed, smalls)
    return content_out, query_out, g[0], d[0], g[1], g[2], d[1], g[3], d[2], d[3], d[4], g[4], d[5], g[5], d[6], d[7], d[8], d[9]


def solution(mesh):
    rows, matrix, vector, buckets = P("pipe", "dp", None), P("pipe", None, None), P("pipe", None), P("dp", None)
    grads = (matrix, vector, matrix, matrix, vector, matrix, vector, vector, vector, matrix, vector, matrix, vector, vector, vector, matrix)
    return jax.shard_map(on_device, mesh=mesh, in_specs=(rows, rows, *grads, buckets, buckets), out_specs=(rows, rows, *grads), check_vma=False)
```

```python
import functools
import math
from typing import Any, NamedTuple

import jax
import jax.numpy as jnp
from jax import lax
from jax.experimental import pallas as pl
from jax.experimental.pallas import tpu as pltpu
from jax.sharding import PartitionSpec as P

MESH = pl.DeviceIdType.MESH
F32 = jnp.float32
BF16 = jnp.bfloat16
NORM_EPS = 1e-05
NEG_FILL = -1e30
THRESHOLDS = (12, 16, 23, 32, 46, 64, 91)
TILE = 256
LANES = 128
UNROLL = 3
EARLY = 3
LAG = 2
CHUNK = 16
VMEM_LIMIT = 63 * 2**20


class Sizes(NamedTuple):
    micro: int
    seq: int
    query: int
    width: int
    heads: int
    hidden: int
    buckets: int

    @property
    def block(self):
        return self.seq + self.query

    @property
    def rows(self):
        return self.micro * self.block

    @property
    def pairs(self):
        return self.width // LANES


class Weights(NamedTuple):
    query: Any
    key: Any
    value: Any
    out: Any
    up: Any
    down: Any


class Vectors(NamedTuple):
    b_query: Any
    b_value: Any
    b_out: Any
    gain_attn: Any
    shift_attn: Any
    b_up: Any
    b_down: Any
    gain_ffn: Any
    shift_ffn: Any
    rel_table: Any
    lengths: Any
    order: Any


class State(NamedTuple):
    left: Any
    qkv: Any
    slope: Any
    probs: Any
    norm_attn: Any
    norm_ffn: Any
    spread_attn: Any
    spread_ffn: Any


def state_shapes(n):
    return State(
        ((n.rows, 3 * n.width + n.hidden), BF16),
        ((n.rows, 3 * n.width), BF16),
        ((n.rows, n.hidden), BF16),
        ((n.micro * n.pairs, 2 * n.block, n.seq), F32),
        ((n.rows, n.width), F32),
        ((n.rows, n.width), F32),
        ((n.rows, 1), F32),
        ((n.rows, 1), F32),
    )


def dot(a, b):
    return jnp.dot(a, b, preferred_element_type=F32)


def dot_nt(a, b, precision=None):
    return lax.dot_general(a, b, (((1,), (1,)), ((), ())), precision=precision, preferred_element_type=F32)


def dot_tn(a, b, precision=None):
    return lax.dot_general(a, b, (((0,), (0,)), ((), ())), precision=precision, preferred_element_type=F32)


def iota(shape, dim):
    return lax.broadcasted_iota(jnp.int32, shape, dim)


def cols(at, size=TILE):
    return pl.ds(pl.multiple_of(at * size, size), size)


def bucket_of(offset):
    distance = jnp.abs(offset)
    bucket = jnp.minimum(distance, 8) + jnp.where(offset < 0, 16, 0)
    for bound_at in THRESHOLDS:
        bucket = bucket + jnp.where(distance >= bound_at, 1, 0)
    return bucket


def place_buckets(n):
    shape = (n.buckets, 2 * n.seq)
    at = iota(shape, 1)
    offset = jnp.where(at < n.seq, -at, 2 * n.seq - at)
    return jnp.where(bucket_of(offset) == iota(shape, 0), 1.0, 0.0)


def to_column(row, n):
    shape = (n.seq, n.seq)
    return jnp.sum(jnp.where(iota(shape, 0) == iota(shape, 1), row, 0.0), axis=1, keepdims=True)


def picked(order_col, n, place):
    return order_col[n.seq - n.query :] == place.astype(F32)


def bias_and_mask(n, v, bias):
    seq, query = n.seq, n.query
    base = dot_tn(v.rel_table[0], place_buckets(n), lax.Precision.HIGHEST)
    square = (seq, seq)
    row_at, col_at = iota(square, 0).astype(F32), iota(square, 1).astype(F32)
    visible_from = float(seq - query)
    content_sees, query_sees, chosen = [], [], []
    for b in range(n.micro):
        order_row = v.order[b : b + 1, :].astype(F32)
        order_col = to_column(order_row, n)
        rank_row = jnp.sum(jnp.where(order_col == col_at, row_at, 0.0), axis=0, keepdims=True)
        rank_col = to_column(rank_row, n)
        ends, total = [], jnp.int32(0)
        for d in range(v.lengths.shape[1]):
            total = total + v.lengths[b, d]
            ends.append(total)

        def doc_of(at):
            found = jnp.zeros(at.shape, F32)
            for end in ends:
                found = found + jnp.where(at >= end.astype(F32), 1.0, 0.0)
            return found

        doc_row = doc_of(iota((1, seq), 1).astype(F32))
        doc_col = doc_of(iota((seq, 1), 0).astype(F32))
        unmasked = rank_row < visible_from
        content_sees.append((doc_col == doc_row) & (unmasked | (rank_row <= rank_col)))
        at_place = picked(order_col, n, iota((query, seq), 1))
        place = order_col[seq - query :]
        rank = visible_from + iota((query, 1), 0).astype(F32)
        query_sees.append((doc_of(place) == doc_row) & (unmasked | (rank_row < rank) | at_place))
        chosen.append(jnp.where(at_place, 1.0, 0.0).astype(BF16))
    for h in range(n.heads):
        spread = jnp.broadcast_to(base[h : h + 1, :], (seq, 2 * seq))
        table = pltpu.roll(spread, 0, 1, stride=1, stride_axis=0)[:, :seq]
        high = table.astype(BF16)
        rest = table - high.astype(F32)
        middle = rest.astype(BF16)
        low = (rest - middle.astype(F32)).astype(BF16)
        for b in range(n.micro):
            of_query = dot(chosen[b], high) + dot(chosen[b], middle) + dot(chosen[b], low)
            start = (h % 2) * n.block
            bias[b * n.pairs + h // 2, start : start + seq, :] = jnp.where(content_sees[b], table, NEG_FILL)
            bias[b * n.pairs + h // 2, start + seq : start + n.block, :] = jnp.where(query_sees[b], of_query, NEG_FILL)


def half_masks():
    at = iota((1, LANES), 1)
    return jnp.where(at < LANES // 2, 1.0, 0.0).astype(BF16), jnp.where(at < LANES // 2, 0.0, 1.0).astype(BF16)


def both_heads(values):
    first, second = half_masks()
    return jnp.concatenate([values * first, values * second], axis=0)


def side_by_side(stacked):
    half = stacked.shape[0] // 2
    return jnp.concatenate([stacked[:half], stacked[half:]], axis=1)


def norm_rows(n, summed, spread_ref, gain, shift, write):
    step = n.block // 3

    @pl.loop(0, n.rows // step)
    def _(i):
        rows = pl.ds(pl.multiple_of(i * step, step), step)
        r = summed[rows, :]
        centered = r - jnp.mean(r, axis=1, keepdims=True)
        spread = lax.rsqrt(jnp.mean(centered * centered, axis=1, keepdims=True) + NORM_EPS)
        normed = centered * spread
        summed[rows, :] = normed
        spread_ref[rows, :] = spread
        write(rows, (normed * gain + shift).astype(BF16))


def norm_back(n, grad_of, normed_ref, spread_ref, gain, write):
    step = n.block // 3

    def body(i, sums):
        rows = pl.ds(pl.multiple_of(i * step, step), step)
        grad = grad_of(rows)
        normed = normed_ref[rows, :]
        scaled = grad * gain
        inner = jnp.mean(scaled * normed, axis=1, keepdims=True)
        back = spread_ref[rows, :] * (scaled - jnp.mean(scaled, axis=1, keepdims=True) - normed * inner)
        write(rows, back)
        low = back.astype(BF16).astype(F32)
        return (
            sums[0] + jnp.sum(grad * normed, axis=0, keepdims=True),
            sums[1] + jnp.sum(grad, axis=0, keepdims=True),
            sums[2] + jnp.sum(low, axis=0, keepdims=True),
        )

    zero = jnp.zeros((1, n.width), F32)
    return lax.fori_loop(0, n.rows // step, body, (zero, zero, zero))


def project(n, ready, w, v, s):
    width, tiles = n.width, n.width // TILE
    for i, matrix in enumerate((w.query, w.key, w.value)):
        ready(i)

        @pl.loop(0, tiles, unroll=True)
        def _(t):
            product = dot(s.left[:, :width], matrix[:, cols(t)])
            if i == 0:
                product = product + v.b_query[:, cols(t)]
            if i == 2:
                product = product + v.b_value[:, cols(t)]
            s.qkv[:, cols(i * tiles + t)] = product.astype(BF16)


def attend(n, s):
    factor = (LANES // 2) ** -0.5

    @pl.loop(0, n.micro * n.pairs, unroll=UNROLL)
    def _(it):
        b, pair = it // n.pairs, it % n.pairs
        rows = pl.ds(pl.multiple_of(b * n.block, 16), n.block)
        keys = pl.ds(pl.multiple_of(b * n.block, 16), n.seq)
        q = both_heads(s.qkv[rows, cols(pair, LANES)])
        k = s.qkv[keys, cols(n.pairs + pair, LANES)]
        val = both_heads(s.qkv[keys, cols(2 * n.pairs + pair, LANES)])
        scores = dot_nt(q, k) * factor + s.probs[it]
        powers = jnp.exp(scores - jnp.max(scores, axis=1, keepdims=True))
        probs = powers / jnp.sum(powers, axis=1, keepdims=True)
        s.probs[it] = probs
        mixed = dot(side_by_side(probs.astype(BF16)), val)
        s.left[rows, cols(n.pairs + pair, LANES)] = mixed.astype(BF16)


def attend_out(n, w, v, s):
    width, tiles = n.width, n.width // TILE

    @pl.loop(0, tiles, unroll=True)
    def _(t):
        product = dot(s.left[:, width : 2 * width], w.out[:, cols(t)])
        s.norm_attn[:, cols(t)] = s.left[:, cols(t)].astype(F32) + product + v.b_out[:, cols(t)]


def attend_norm(n, v, s):
    width = n.width

    def keep_h1(rows, value):
        s.left[rows, 2 * width : 3 * width] = value

    norm_rows(n, s.norm_attn, s.spread_attn, v.gain_attn[...], v.shift_attn[...], keep_h1)


def go_up(n, w, v, s):
    width, tiles, left_u = n.width, n.width // TILE, 3 * (n.width // TILE)
    step = n.block // 3
    c = (2 / math.pi) ** 0.5
    staged = s.norm_ffn

    def bend(t, i):
        for at in range(0, n.rows, step):
            rows = slice(at, at + step)
            z = staged[rows, i * TILE : (i + 1) * TILE] + v.b_up[:, cols(t)]
            square = z * z
            half = 0.5 + 0.5 * jnp.tanh(z * (c + 0.044715 * c * square))
            value = z * half
            s.left[rows, cols(left_u + t)] = value.astype(BF16)
            s.slope[rows, cols(t)] = (half + value * (1.0 - half) * (2.0 * c + 0.26829 * c * square)).astype(BF16)

    @pl.loop(0, n.hidden // width)
    def _(group):
        for i in range(tiles):
            staged[:, i * TILE : (i + 1) * TILE] = dot(s.left[:, 2 * width : 3 * width], w.up[:, cols(group * tiles + i)])
            if i:
                bend(group * tiles + i - 1, i - 1)
        bend(group * tiles + tiles - 1, tiles - 1)


def go_down(n, w, v, s):
    width, tiles = n.width, n.width // TILE

    @pl.loop(0, tiles, unroll=True)
    def _(t):
        product = dot(s.left[:, 3 * width :], w.down[:, cols(t)])
        s.norm_ffn[:, cols(t)] = s.left[:, cols(2 * tiles + t)].astype(F32) + product + v.b_down[:, cols(t)]


def ffn_norm(n, v, s, y):
    def keep_y(rows, value):
        y[rows, :] = value

    norm_rows(n, s.norm_ffn, s.spread_ffn, v.gain_ffn[...], v.shift_ffn[...], keep_y)


def ffn_norm_back(n, v, s, dy, right, smalls, resid):
    width = n.width
    df_cols = slice(4 * width + n.hidden, 5 * width + n.hidden)

    def keep_df(rows, value):
        resid[rows, :] = value
        right[rows, df_cols] = value.astype(BF16)

    gain, shift, low = norm_back(n, lambda rows: dy[rows, :].astype(F32), s.norm_ffn, s.spread_ffn, v.gain_ffn[...], keep_df)
    smalls[10:11, :], smalls[11:12, :], smalls[9:10, :] = gain, shift, low


def down_back(n, w, s, right, smalls, sent):
    width, tiles = n.width, n.width // TILE
    df_cols = slice(4 * width + n.hidden, 5 * width + n.hidden)
    step = n.block // 3
    staged = s.norm_ffn

    def bend(group, i):
        t = group * tiles + i
        total = jnp.zeros((8, TILE), F32)
        for at in range(0, n.rows, step):
            rows = slice(at, at + step)
            dz = (staged[rows, i * TILE : (i + 1) * TILE] * s.slope[rows, cols(t)].astype(F32)).astype(BF16)
            right[rows, cols(4 * tiles + t)] = dz
            total = total + jnp.sum(dz.astype(F32).reshape(step // 8, 8, TILE), axis=0)
        smalls[pl.ds(5 + group, 1), cols(i)] = jnp.sum(total, axis=0, keepdims=True)

    @pl.loop(0, n.hidden // width)
    def _(group):
        for i in range(tiles):
            staged[:, i * TILE : (i + 1) * TILE] = dot_nt(right[:, df_cols], w.down[cols(group * tiles + i), :])
            if i:
                bend(group, i - 1)
        bend(group, tiles - 1)
        sent(group)


def up_back(n, w, dy, right, resid):
    width, tiles = n.width, n.width // TILE

    @pl.loop(0, tiles, unroll=True)
    def _(t):
        spread = dot_nt(right[:, 4 * width : 4 * width + n.hidden], w.up[cols(t), :])
        dy[:, cols(t)] = (spread + resid[:, cols(t)]).astype(BF16)


def attend_norm_back(n, v, s, dy, right, smalls, resid):
    width = n.width

    def keep_da(rows, value):
        resid[rows, :] = value
        right[rows, 3 * width : 4 * width] = value.astype(BF16)

    gain, shift, low = norm_back(n, lambda rows: dy[rows, :].astype(F32), s.norm_attn, s.spread_attn, v.gain_attn[...], keep_da)
    smalls[3:4, :], smalls[4:5, :], smalls[2:3, :] = gain, shift, low


def out_back(n, w, dy, right):
    width, tiles = n.width, n.width // TILE

    @pl.loop(0, tiles, unroll=True)
    def _(t):
        dy[:, cols(t)] = dot_nt(right[:, 3 * width : 4 * width], w.out[cols(t), :]).astype(BF16)


def attend_back(n, v, s, dy, right, smalls, table_sum, chosen, between):
    width = n.width
    factor = (LANES // 2) ** -0.5
    table_sum[...] = jnp.zeros(table_sum.shape, F32)
    square = (n.seq, n.seq)
    same = jnp.where(iota(square, 0) + iota(square, 1) == n.seq - 1, 1.0, 0.0).astype(BF16)
    for b in range(n.micro):
        order_col = to_column(v.order[b : b + 1, :].astype(F32), n)
        predicted = picked(order_col, n, n.seq - 1 - iota((n.query, n.seq), 1))
        chosen[b, : n.seq, :] = same
        chosen[b, n.seq :, :] = jnp.where(predicted, 1.0, 0.0).astype(BF16)

    @pl.loop(0, n.micro * n.pairs // UNROLL)
    def _(outside):
        for inside in range(UNROLL):
            it = outside * UNROLL + inside
            b, pair = it // n.pairs, it % n.pairs
            start = b * n.block
            rows = pl.ds(pl.multiple_of(start, 16), n.block)
            keys = pl.ds(pl.multiple_of(start, 16), n.seq)
            rest = pl.ds(pl.multiple_of(start + n.seq, 16), n.query)
            grad = both_heads(dy[rows, cols(pair, LANES)])
            q = both_heads(s.qkv[rows, cols(pair, LANES)])
            k = both_heads(s.qkv[keys, cols(n.pairs + pair, LANES)])
            val = s.qkv[keys, cols(2 * n.pairs + pair, LANES)]
            probs = s.probs[it]
            grad_probs = dot_nt(grad, val)
            inner = jnp.sum(probs * grad_probs, axis=1, keepdims=True)
            grad_scores = (probs * (grad_probs - inner)).astype(BF16)
            right[rows, cols(pair, LANES)] = (dot(side_by_side(grad_scores), k) * factor).astype(BF16)
            right[keys, cols(n.pairs + pair, LANES)] = (dot_tn(grad_scores, q) * factor).astype(BF16)
            right[keys, cols(2 * n.pairs + pair, LANES)] = dot_tn(probs.astype(BF16), grad).astype(BF16)
            none = jnp.zeros((n.query, LANES), BF16)
            right[rest, cols(n.pairs + pair, LANES)] = none
            right[rest, cols(2 * n.pairs + pair, LANES)] = none
            for half in range(2):
                of_head = grad_scores[half * n.block : (half + 1) * n.block]
                table_sum[2 * pair + half] += dot_tn(chosen[b], of_head)
        between(outside)

    smalls[0:1, :] = jnp.sum(right[:, :width].astype(F32), axis=0, keepdims=True)
    smalls[1:2, :] = jnp.sum(right[:, 2 * width : 3 * width].astype(F32), axis=0, keepdims=True)


def table_back(n, smalls, table_sum):
    by_place = []
    for h in range(n.heads):
        wide = jnp.concatenate([table_sum[h], jnp.zeros((n.seq, n.seq), F32)], axis=1)
        turned = pltpu.roll(wide, n.seq + 1, 1, stride=1, stride_axis=0)
        by_place.append(jnp.sum(turned, axis=0, keepdims=True))
    by_place = jnp.concatenate(by_place, axis=0)
    smalls[12 : 12 + n.heads, : n.buckets] = dot_nt(by_place, place_buckets(n), lax.Precision.HIGHEST)


def inputs_back(n, w, right, resid, dx):
    width, tiles = n.width, n.width // TILE

    @pl.loop(0, tiles, unroll=True)
    def _(t):
        total = resid[:, cols(t)]
        for i, matrix in enumerate((w.query, w.key, w.value)):
            total = total + dot_nt(right[:, i * width : (i + 1) * width], matrix[cols(t), :])
        dx[:, cols(t)] = total.astype(BF16)


def tiles_of(n, core):
    tiles, groups = n.width // TILE, n.hidden // n.width
    down = groups * tiles // 2

    def ffn(i):
        is_down = i < down
        up = i - down
        left = jnp.where(is_down, 3 * tiles + core * down + i, 2 * tiles + up % tiles)
        return left, jnp.where(is_down, 4 + groups, 4 + core * (groups // 2) + up // tiles)

    def attention(i):
        group = i // tiles
        return i % tiles + jnp.where(core * group == 1, tiles, 0), 2 * core + group

    return (ffn, 2 * down), (attention, 2 * tiles)


def weight_grads(n, of, count, first, left, right, packed):
    per = TILE // packed.shape[2] // packed.shape[1]
    by = math.gcd(count, UNROLL)

    @pl.loop(0, count // by)
    def _(outside):
        for inside in range(by):
            i = outside * by + inside
            left_tile, group = of(i)
            rhs = right[:, pl.ds(pl.multiple_of(group * n.width, n.width), n.width)]
            product = dot_tn(left[:, cols(left_tile)], rhs).astype(BF16)
            packed[pl.ds((first + i) * per, per)] = product.reshape((per,) + packed.shape[1:])


class Landing(NamedTuple):
    from_y: Any
    end_b: Any
    end_a: Any
    mid_a: Any
    mid_b: Any
    rung_b: Any


class Arrival(NamedTuple):
    y: Any
    end_b: Any
    end_a: Any
    mid_a: Any
    mid_b: Any
    rung: Any
    own_a: Any
    own_b: Any
    end_final: Any
    y_final: Any
    mid_final: Any
    end_both: Any
    sibling: Any


class Place(NamedTuple):
    core: Any
    y: Any
    mine: Any
    other: Any
    is_end: Any
    is_mid: Any
    sibling: Any
    y_peer: Any
    z_in: Any
    z_out: Any
    z_mid: Any
    across: Any
    doubling: Any


def find_place():
    pipe, index = lax.axis_index("pipe"), lax.axis_index("dp")
    base, local = index // 16 * 16, index % 16
    z, y, core = local // 4, local // 2 % 2, local % 2

    def at(zz, yy, cc):
        return (pipe, base + zz * 4 + yy * 2 + cc)

    return Place(
        core,
        y,
        z + 1,
        4 - z,
        (z == 0) | (z == 3),
        (z == 1) | (z == 2),
        at(z, y, 1 - core),
        at(z, 1 - y, core),
        at(jnp.where(z == 0, 1, 2), y, core),
        at(jnp.where(z == 1, 0, 3), y, core),
        at(3 - z, y, core),
        (1 - pipe, index),
        [(pipe, base + jnp.bitwise_xor(local, 1 << j)) for j in range(4)],
    )


def greet_all(me):
    barrier = pltpu.get_barrier_semaphore()
    for device in me.doubling + [me.across]:
        pl.semaphore_signal(barrier, inc=1, device_id=device, device_id_type=MESH)

    @pl.when(me.is_mid)
    def _():
        pl.semaphore_signal(barrier, inc=1, device_id=me.z_mid, device_id_type=MESH)
        pl.semaphore_wait(barrier, 6)

    @pl.when(me.is_end)
    def _():
        pl.semaphore_wait(barrier, 5)


def remote(src, dst, send, recv, device):
    return pltpu.make_async_remote_copy(src_ref=src, dst_ref=dst, send_sem=send, recv_sem=recv, device_id=device, device_id_type=MESH)


def wait_for(ref, sem):
    pltpu.make_async_copy(ref, ref, sem).wait()


def added(a, b):
    return (a.astype(F32) + b.astype(F32)).astype(BF16)


def sums(me, packed, out, land, sem, send):
    steps = packed.shape[0]
    c, y, mine, other = me.core, me.y, me.mine, me.other
    both = pl.ds(2, 2)

    def s0(k):
        remote(packed.at[k, 1 - y], land.from_y.at[k], send.at[0], sem.y.at[k], me.y_peer).start()

        @pl.when(me.is_end)
        def _():
            remote(packed.at[k, both], land.end_b.at[k], send.at[1], sem.end_b.at[k], me.z_in).start()

    def s1(k):
        wait_for(land.from_y.at[k], sem.y.at[k])
        packed[k, y] = added(packed[k, y], land.from_y[k])

        @pl.when(me.is_end)
        def _():
            remote(packed.at[k, y], land.end_a.at[k], send.at[2], sem.end_a.at[k], me.z_in).start()

        @pl.when(me.is_mid)
        def _():
            wait_for(land.end_b.at[k], sem.end_b.at[k])
            packed[k, both] = added(packed[k, both], land.end_b[k])
            remote(packed.at[k, other], land.mid_b.at[k], send.at[3], sem.mid_b.at[k], me.z_mid).start()

    def s2(k):
        @pl.when(me.is_mid)
        def _():
            wait_for(land.end_a.at[k], sem.end_a.at[k])
            packed[k, y] = added(packed[k, y], land.end_a[k])
            remote(packed.at[k, y], land.mid_a.at[k], send.at[4], sem.mid_a.at[k], me.z_mid).start()
            wait_for(land.mid_b.at[k], sem.mid_b.at[k])
            packed[k, mine] = added(packed[k, mine], land.mid_b[k])
            remote(packed.at[k, mine], land.rung_b.at[k], send.at[5], sem.rung.at[k], me.y_peer).start()

    def s3(k):
        @pl.when(me.is_mid)
        def _():
            wait_for(land.mid_a.at[k], sem.mid_a.at[k])
            total = land.from_y.at[k]
            total[...] = added(packed[k, y], land.mid_a[k])
            remote(total, out.at[c, k, y], send.at[6], sem.end_final.at[k], me.z_out).start()
            remote(total, out.at[c, k, y], send.at[7], sem.y_final.at[k], me.y_peer).start()
            pltpu.make_async_copy(total, out.at[c, k, y], sem.own_a.at[k]).start()
            wait_for(land.rung_b.at[k], sem.rung.at[k])
            total = land.end_a.at[k]
            total[...] = added(packed[k, mine], land.rung_b[k])
            remote(total, out.at[c, k, mine], send.at[8], sem.mid_final.at[k], me.z_mid).start()
            pltpu.make_async_copy(total, out.at[c, k, mine], sem.own_b.at[k]).start()

    def s4(k):
        @pl.when(me.is_end)
        def _():
            wait_for(out.at[c, k, y], sem.end_final.at[k])
            remote(out.at[c, k, y], out.at[c, k, y], send.at[7], sem.y_final.at[k], me.y_peer).start()

        @pl.when(me.is_mid)
        def _():
            wait_for(out.at[c, k, other], sem.mid_final.at[k])
            wait_for(out.at[c, k, mine], sem.own_b.at[k])
            remote(out.at[c, k, both], out.at[c, k, both], send.at[9], sem.end_both.at[k], me.z_out).start()

    def s5(k):
        wait_for(out.at[c, k, 1 - y], sem.y_final.at[k])

        @pl.when(me.is_end)
        def _():
            wait_for(out.at[c, k, both], sem.end_both.at[k])

        @pl.when(me.is_mid)
        def _():
            wait_for(out.at[c, k, y], sem.own_a.at[k])

        remote(out.at[c, k], out.at[c, k], send.at[10], sem.sibling.at[k], me.sibling).start()

    def s6(k):
        wait_for(out.at[1 - c, k], sem.sibling.at[k])

    stages = (s0, s1, s2, s3, s4, s5, s6)

    def slot(t):
        for i, stage in enumerate(stages):
            k = t - i * LAG

            @pl.when((k >= 0) & (k < steps))
            def _():
                stage(jnp.clip(k, 0, steps - 1))

    def finish():
        section = land.from_y
        wait_for(section, send.at[0])
        wait_for(section, send.at[7])
        wait_for(packed, send.at[10])

        @pl.when(me.is_end)
        def _():
            wait_for(land.end_b, send.at[1])
            wait_for(section, send.at[2])

        @pl.when(me.is_mid)
        def _():
            for which in (3, 4, 5, 6, 8):
                wait_for(section, send.at[which])
            wait_for(land.end_b, send.at[9])

    return slot, steps + (len(stages) - 1) * LAG, finish


def small_sums(me, smalls, held, total, recv, send):
    def source(j):
        return smalls if j == 0 else held.at[1, j - 1]

    def copy(j):
        return remote(source(j), held.at[0, j], send.at[j], recv.at[j], me.doubling[j])

    def step(j):
        if j >= 0:
            copy(j).wait()
            summed = source(j)[...] + held[0, j]
            if j == 3:
                total[...] = summed
            else:
                held[1, j] = summed
        if j < 3:
            copy(j + 1).start()

    return step


def copies_of(pairs, sems):
    return [pltpu.make_async_copy(src, dst, sems.at[i]) for i, (src, dst) in enumerate(pairs)]


def bucket_rows(n, content, query, wide):
    pairs = []
    for b in range(n.micro):
        pairs.append((content.at[0, pl.ds(b * n.seq, n.seq)], wide.at[pl.ds(b * n.block, n.seq)]))
        pairs.append((query.at[0, pl.ds(b * n.query, n.query)], wide.at[pl.ds(b * n.block + n.seq, n.query)]))
    return pairs


def whole_kernel(n, *refs):
    content, query, *refs = refs
    w_hbm, refs = Weights(*refs[:6]), refs[6:]
    v, refs = Vectors(*refs[:12]), refs[12:]
    content_out, query_out, out, total, *refs = refs
    w, refs = Weights(*refs[:6]), refs[6:]
    left, right, y, dx, dy, resid, table_sum, chosen, smalls, held, packed, *refs = refs
    s, refs = State(left.at[pl.ds(0, n.rows)], *refs[:7]), refs[7:]
    land, refs = Landing(*refs[:6]), refs[6:]
    arrive, refs = Arrival(*refs[:13]), refs[13:]
    w_sem, in_sem, grad_sem, out_sem, pipe_send, pipe_recv, core_send, core_recv, small_send, small_recv, sum_send = refs
    width, rows = n.width, n.rows
    inputs = s.left.at[:, pl.ds(0, width)]
    mine_right = right.at[pl.ds(0, rows)]
    groups = n.hidden // width
    first, last = lax.axis_index("pipe") == 0, lax.axis_index("pipe") == 1
    me = find_place()

    weights = copies_of([(a.at[0], b) for a, b in zip(w_hbm, w)], w_sem)
    own_rows = copies_of(bucket_rows(n, content, query, inputs), in_sem)
    own_grads = copies_of(bucket_rows(n, content, query, dy), in_sem)

    @pl.when(first)
    def _():
        for cp in own_rows:
            cp.start()

    @pl.when(last)
    def _():
        for cp in own_grads:
            cp.start()

    for cp in weights:
        cp.start()
    greet_all(me)
    bias_and_mask(n, v, s.probs)
    hand_up = remote(y, inputs, pipe_send, pipe_recv, me.across)
    hand_down = remote(dx, dy, pipe_send, pipe_recv, me.across)

    def to_core(which, src, dst):
        return remote(src, dst, core_send.at[which], core_recv.at[which], me.sibling)

    def left_copy(which, at, size):
        return to_core(which, left.at[pl.ds(0, rows), pl.ds(at, size)], left.at[pl.ds(rows, rows), pl.ds(at, size)])

    def right_copy(which, at, size):
        return to_core(which, right.at[pl.ds(0, rows), pl.ds(at, size)], right.at[pl.ds(rows, rows), pl.ds(at, size)])

    share_left = left_copy(0, 0, 3 * width + n.hidden)
    share_attention = right_copy(1, 0, 3 * width)
    share_da = right_copy(2, 3 * width, width)
    share_df = right_copy(3, (4 + groups) * width, width)

    def share_dz(group):
        return right_copy(4 + group, pl.multiple_of((4 + group) * width, width), width)

    @pl.when(first)
    def _():
        for cp in own_rows:
            cp.wait()

    @pl.when(last)
    def _():
        hand_up.wait_recv()

    done = set()

    def ready(i):
        if i not in done:
            done.add(i)
            weights[i].wait()

    project(n, ready, w, v, s)
    attend(n, s)
    ready(3)
    attend_out(n, w, v, s)
    attend_norm(n, v, s)
    ready(4)
    go_up(n, w, v, s)
    ready(5)
    go_down(n, w, v, s)
    ffn_norm(n, v, s, y)

    @pl.when(first)
    def _():
        hand_up.start()

    share_left.start()
    results = copies_of([(b, a) for a, b in bucket_rows(n, content_out, query_out, y)], out_sem)
    results_back = copies_of([(b, a) for a, b in bucket_rows(n, content_out, query_out, dx)], out_sem)

    @pl.when(last)
    def _():
        for cp in results:
            cp.start()
        for cp in own_grads:
            cp.wait()

    @pl.when(first)
    def _():
        hand_up.wait_send()
        hand_down.wait_recv()

    slot, slots, finish = sums(me, packed, out, land, arrive, sum_send)
    (ffn, ffn_count), (attention, attention_count) = tiles_of(n, me.core)
    ffn_norm_back(n, v, s, dy, mine_right, smalls, resid)
    share_df.start()
    down_back(n, w, s, mine_right, smalls, lambda group: share_dz(group).start())
    up_back(n, w, dy, mine_right, resid)

    def ffn_grads():
        share_left.wait_recv()
        share_df.wait_recv()
        for group in range(groups):
            share_dz(group).wait_recv()
        weight_grads(n, ffn, ffn_count, 0, left, right, packed)

    pl.when(first)(ffn_grads)
    attend_norm_back(n, v, s, dy, mine_right, smalls, resid)
    share_da.start()
    out_back(n, w, dy, mine_right)
    early = n.micro * n.pairs // UNROLL * EARLY

    def between(outside):
        @pl.when(first)
        def _():
            @pl.loop(0, EARLY)
            def _(i):
                slot(outside * EARLY + i)

    attend_back(n, v, s, dy, mine_right, smalls, table_sum, chosen, between)
    share_attention.start()
    inputs_back(n, w, mine_right, resid, dx)

    @pl.when(last)
    def _():
        hand_down.start()

    table_back(n, smalls, table_sum)
    small_step = small_sums(me, smalls, held, total, small_recv, small_send)
    small_step(-1)

    @pl.when(first)
    def _():
        for cp in results_back:
            cp.start()

    pl.when(last)(ffn_grads)
    share_attention.wait_recv()
    share_da.wait_recv()
    weight_grads(n, attention, attention_count, ffn_count, left, right, packed)
    start = jnp.where(first, early, 0)

    @pl.loop(0, slots - start)
    def _(i):
        slot(start + i)
        for j in range(4):
            pl.when(i == 4 * (j + 1))(functools.partial(small_step, j))

    finish()
    for which in [share_left, share_attention, share_da, share_df] + [share_dz(group) for group in range(groups)]:
        which.wait_send()
    for cp in results:
        cp.wait()

    @pl.when(last)
    def _():
        hand_down.wait_send()


def shaped(shape, dtype=BF16):
    return jax.ShapeDtypeStruct(shape, dtype)


def run_layers(n, content, query, w, v):
    rows, width = n.rows, n.width
    vmem, smem, anywhere = (pl.BlockSpec(memory_space=space) for space in (pltpu.VMEM, pltpu.SMEM, pl.ANY))
    dma = pltpu.SemaphoreType.DMA
    steps = (4 * width + 2 * n.hidden) // (2 * 4 * CHUNK)
    half = (steps, 4, CHUNK, width)
    section, sections = pltpu.VMEM((steps, CHUNK, width), BF16), pltpu.VMEM((steps, 2, CHUNK, width), BF16)
    small_shape = (24, width)
    left, *others = state_shapes(n)
    scratch = [pltpu.VMEM(m.shape[1:], BF16) for m in w]
    scratch += [
        pltpu.VMEM((2 * rows, left[0][1]), BF16),
        pltpu.VMEM((2 * rows, 5 * width + n.hidden), BF16),
        pltpu.VMEM((rows, width), BF16),
        pltpu.VMEM((rows, width), BF16),
        pltpu.VMEM((rows, width), BF16),
        pltpu.VMEM((rows, width), F32),
        pltpu.VMEM((n.heads, n.seq, n.seq), F32),
        pltpu.VMEM((n.micro, n.block, n.seq), BF16),
        pltpu.VMEM(small_shape, F32),
        pltpu.VMEM((2, 4) + small_shape, F32),
        pltpu.VMEM(half, BF16),
    ]
    scratch += [pltpu.VMEM(shape, dtype) for shape, dtype in others]
    scratch += [section, sections, section, section, section, section]
    scratch += [dma((steps,))] * 13
    shares = 4 + n.hidden // width
    scratch += [dma((6,)), dma((2 * n.micro,)), dma((2 * n.micro,)), dma((2 * n.micro,)), dma, dma, dma((shares,)), dma((shares,)), dma((4,)), dma((4,)), dma((11,))]
    return pl.pallas_call(
        functools.partial(whole_kernel, n),
        out_shape=[shaped(content.shape), shaped(query.shape), shaped((2,) + half), shaped(small_shape, F32)],
        in_specs=[anywhere] * 8 + [vmem] * 10 + [smem, vmem],
        out_specs=[anywhere] * 3 + [vmem],
        scratch_shapes=scratch,
        compiler_params=pltpu.CompilerParams(collective_id=1, has_side_effects=True, vmem_limit_bytes=VMEM_LIMIT),
    )(content, query, *w, *v)


def unpack(n, packed, smalls):
    width, heads = n.width, n.heads
    groups = n.hidden // width
    half_down, half_groups = n.hidden // 2, groups // 2
    halves = [packed[core].reshape(-1, width) for core in range(2)]
    down = jnp.concatenate([half[:half_down] for half in halves], axis=0).astype(F32)[None]
    blocks = [[half[half_down + i * width : half_down + (i + 1) * width] for i in range(half_groups + 2)] for half in halves]
    up = jnp.concatenate(blocks[0][:half_groups] + blocks[1][:half_groups], axis=1).astype(F32)[None]
    query, key, value, out = (block.astype(F32)[None] for block in blocks[0][half_groups:] + blocks[1][half_groups:])
    vectors = [smalls[i : i + 1] for i in range(5)]
    vectors.append(smalls[5 : 5 + groups].reshape(1, n.hidden))
    vectors += [smalls[i : i + 1] for i in (9, 10, 11)]
    vectors.append(smalls[12 : 12 + heads, : n.buckets].T[None])
    return (query, key, value, out, up, down), vectors


def across_blocks(packed, smalls):
    blocks = lax.axis_size("dp") // 16
    if blocks > 1:
        groups = [[block * 16 + i for block in range(blocks)] for i in range(16)]
        packed = lax.psum(packed.astype(F32), "dp", axis_index_groups=groups)
        smalls = lax.psum(smalls, "dp", axis_index_groups=groups)
    return packed, smalls


def on_device(content_ends, query_ends, w_query, b_query, w_key, w_value, b_value, w_out, b_out, gain_attn, shift_attn, w_up, b_up, w_down, b_down, gain_ffn, shift_ffn, rel_table, doc_lengths, position_order):
    micro, seq = position_order.shape
    n = Sizes(micro, seq, query_ends.shape[1] // micro, content_ends.shape[2], rel_table.shape[2], w_up.shape[2], rel_table.shape[1])
    w = Weights(w_query, w_key, w_value, w_out, w_up, w_down)
    v = Vectors(b_query, b_value, b_out, gain_attn, shift_attn, b_up, b_down, gain_ffn, shift_ffn, rel_table, doc_lengths, position_order)
    content_out, query_out, packed, smalls = run_layers(n, content_ends, query_ends, w, v)
    packed, smalls = across_blocks(packed, smalls)
    g, d = unpack(n, packed, smalls)
    return content_out, query_out, g[0], d[0], g[1], g[2], d[1], g[3], d[2], d[3], d[4], g[4], d[5], g[5], d[6], d[7], d[8], d[9]


def solution(mesh):
    rows, matrix, vector, buckets = P("pipe", "dp", None), P("pipe", None, None), P("pipe", None), P("dp", None)
    grads = (matrix, vector, matrix, matrix, vector, matrix, vector, vector, vector, matrix, vector, matrix, vector, vector, vector, matrix)
    return jax.shard_map(on_device, mesh=mesh, in_specs=(rows, rows, *grads, buckets, buckets), out_specs=(rows, rows, *grads), check_vma=False)
```

```python
import functools
import math
from typing import Any, NamedTuple

import jax
import jax.numpy as jnp
from jax import lax
from jax.experimental import pallas as pl
from jax.experimental.pallas import tpu as pltpu
from jax.sharding import PartitionSpec as P

MESH = pl.DeviceIdType.MESH
F32 = jnp.float32
BF16 = jnp.bfloat16
NORM_EPS = 1e-05
NEG_FILL = -1e30
THRESHOLDS = (12, 16, 23, 32, 46, 64, 91)
TILE = 256
LANES = 128
UNROLL = 3
EARLY = 3
LAG = 2
RING = 16
CHUNK = 16
VMEM_LIMIT = 63 * 2**20


class Sizes(NamedTuple):
    micro: int
    seq: int
    query: int
    width: int
    heads: int
    hidden: int
    buckets: int

    @property
    def block(self):
        return self.seq + self.query

    @property
    def rows(self):
        return self.micro * self.block

    @property
    def pairs(self):
        return self.width // LANES


class Weights(NamedTuple):
    query: Any
    key: Any
    value: Any
    out: Any
    up: Any
    down: Any


class Vectors(NamedTuple):
    b_query: Any
    b_value: Any
    b_out: Any
    gain_attn: Any
    shift_attn: Any
    b_up: Any
    b_down: Any
    gain_ffn: Any
    shift_ffn: Any
    rel_table: Any
    lengths: Any
    order: Any


class State(NamedTuple):
    left: Any
    qkv: Any
    slope: Any
    probs: Any
    norm_attn: Any
    norm_ffn: Any
    spread_attn: Any
    spread_ffn: Any


def state_shapes(n):
    return State(
        ((n.rows, 3 * n.width + n.hidden), BF16),
        ((n.rows, 3 * n.width), BF16),
        ((n.rows, n.hidden), BF16),
        ((n.micro * n.pairs, 2 * n.block, n.seq), F32),
        ((n.rows, n.width), F32),
        ((n.rows, n.width), F32),
        ((n.rows, 1), F32),
        ((n.rows, 1), F32),
    )


def dot(a, b):
    return jnp.dot(a, b, preferred_element_type=F32)


def dot_nt(a, b, precision=None):
    return lax.dot_general(a, b, (((1,), (1,)), ((), ())), precision=precision, preferred_element_type=F32)


def dot_tn(a, b):
    return lax.dot_general(a, b, (((0,), (0,)), ((), ())), preferred_element_type=F32)


def iota(shape, dim):
    return lax.broadcasted_iota(jnp.int32, shape, dim)


def cols(at, size=TILE):
    return pl.ds(pl.multiple_of(at * size, size), size)


def bucket_of(offset):
    distance = jnp.abs(offset)
    bucket = jnp.minimum(distance, 8) + jnp.where(offset < 0, 16, 0)
    for bound_at in THRESHOLDS:
        bucket = bucket + jnp.where(distance >= bound_at, 1, 0)
    return bucket


def place_buckets(n):
    shape = (n.buckets, 2 * n.seq)
    at = iota(shape, 1)
    offset = jnp.where(at < n.seq, -at, 2 * n.seq - at)
    return jnp.where(bucket_of(offset) == iota(shape, 0), 1.0, 0.0)


def to_column(row, n):
    shape = (n.seq, n.seq)
    return jnp.sum(jnp.where(iota(shape, 0) == iota(shape, 1), row, 0.0), axis=1, keepdims=True)


def picked(order_col, n, place):
    return order_col[n.seq - n.query :] == place.astype(F32)


def bias_and_mask(n, v, bias):
    seq, query = n.seq, n.query
    by_head = jnp.concatenate([v.rel_table[h] for h in range(n.heads)], axis=0)
    base = jnp.dot(by_head, place_buckets(n), precision=lax.Precision.HIGHEST, preferred_element_type=F32)
    square = (seq, seq)
    row_at, col_at = iota(square, 0).astype(F32), iota(square, 1).astype(F32)
    visible_from = float(seq - query)
    content_sees, query_sees, chosen = [], [], []
    for b in range(n.micro):
        order_row = v.order[b : b + 1, :].astype(F32)
        order_col = to_column(order_row, n)
        rank_row = jnp.sum(jnp.where(order_col == col_at, row_at, 0.0), axis=0, keepdims=True)
        rank_col = to_column(rank_row, n)
        ends, total = [], jnp.int32(0)
        for d in range(v.lengths.shape[1]):
            total = total + v.lengths[b, d]
            ends.append(total)

        def doc_of(at):
            found = jnp.zeros(at.shape, F32)
            for end in ends:
                found = found + jnp.where(at >= end.astype(F32), 1.0, 0.0)
            return found

        doc_row = doc_of(iota((1, seq), 1).astype(F32))
        doc_col = doc_of(iota((seq, 1), 0).astype(F32))
        unmasked = rank_row < visible_from
        content_sees.append((doc_col == doc_row) & (unmasked | (rank_row <= rank_col)))
        at_place = picked(order_col, n, iota((query, seq), 1))
        place = order_col[seq - query :]
        rank = visible_from + iota((query, 1), 0).astype(F32)
        query_sees.append((doc_of(place) == doc_row) & (unmasked | (rank_row < rank) | at_place))
        chosen.append(jnp.where(at_place, 1.0, 0.0).astype(BF16))
    for h in range(n.heads):
        spread = jnp.broadcast_to(base[h : h + 1, :], (seq, 2 * seq))
        table = pltpu.roll(spread, 0, 1, stride=1, stride_axis=0)[:, :seq]
        high = table.astype(BF16)
        rest = table - high.astype(F32)
        middle = rest.astype(BF16)
        low = (rest - middle.astype(F32)).astype(BF16)
        for b in range(n.micro):
            of_query = dot(chosen[b], high) + dot(chosen[b], middle) + dot(chosen[b], low)
            start = (h % 2) * n.block
            bias[b * n.pairs + h // 2, start : start + seq, :] = jnp.where(content_sees[b], table, NEG_FILL)
            bias[b * n.pairs + h // 2, start + seq : start + n.block, :] = jnp.where(query_sees[b], of_query, NEG_FILL)


def half_masks():
    at = iota((1, LANES), 1)
    return jnp.where(at < LANES // 2, 1.0, 0.0).astype(BF16), jnp.where(at < LANES // 2, 0.0, 1.0).astype(BF16)


def both_heads(values):
    first, second = half_masks()
    return jnp.concatenate([values * first, values * second], axis=0)


def side_by_side(stacked):
    half = stacked.shape[0] // 2
    return jnp.concatenate([stacked[:half], stacked[half:]], axis=1)


def norm_rows(n, summed, spread_ref, gain, shift, write):
    step = n.block // 3

    @pl.loop(0, n.rows // step)
    def _(i):
        rows = pl.ds(pl.multiple_of(i * step, step), step)
        r = summed[rows, :]
        centered = r - jnp.mean(r, axis=1, keepdims=True)
        spread = lax.rsqrt(jnp.mean(centered * centered, axis=1, keepdims=True) + NORM_EPS)
        normed = centered * spread
        summed[rows, :] = normed
        spread_ref[rows, :] = spread
        write(rows, (normed * gain + shift).astype(BF16))


def norm_back(n, grad_of, normed_ref, spread_ref, gain, write):
    step = n.block // 3

    def body(i, sums):
        rows = pl.ds(pl.multiple_of(i * step, step), step)
        grad = grad_of(rows)
        normed = normed_ref[rows, :]
        scaled = grad * gain
        inner = jnp.mean(scaled * normed, axis=1, keepdims=True)
        back = spread_ref[rows, :] * (scaled - jnp.mean(scaled, axis=1, keepdims=True) - normed * inner)
        write(rows, back)
        low = back.astype(BF16).astype(F32)
        return (
            sums[0] + jnp.sum(grad * normed, axis=0, keepdims=True),
            sums[1] + jnp.sum(grad, axis=0, keepdims=True),
            sums[2] + jnp.sum(low, axis=0, keepdims=True),
        )

    zero = jnp.zeros((1, n.width), F32)
    return lax.fori_loop(0, n.rows // step, body, (zero, zero, zero))


def project(n, ready, w, v, s):
    width, tiles = n.width, n.width // TILE
    for i, matrix in enumerate((w.query, w.key, w.value)):
        ready(i)

        @pl.loop(0, tiles, unroll=True)
        def _(t):
            product = dot(s.left[:, :width], matrix[:, cols(t)])
            if i == 0:
                product = product + v.b_query[:, cols(t)]
            if i == 2:
                product = product + v.b_value[:, cols(t)]
            s.qkv[:, cols(i * tiles + t)] = product.astype(BF16)


def attend(n, s):
    factor = (LANES // 2) ** -0.5

    @pl.loop(0, n.micro * n.pairs, unroll=UNROLL)
    def _(it):
        b, pair = it // n.pairs, it % n.pairs
        rows = pl.ds(pl.multiple_of(b * n.block, 16), n.block)
        keys = pl.ds(pl.multiple_of(b * n.block, 16), n.seq)
        q = both_heads(s.qkv[rows, cols(pair, LANES)])
        k = s.qkv[keys, cols(n.pairs + pair, LANES)]
        val = both_heads(s.qkv[keys, cols(2 * n.pairs + pair, LANES)])
        scores = dot_nt(q, k) * factor + s.probs[it]
        powers = jnp.exp(scores - jnp.max(scores, axis=1, keepdims=True))
        probs = powers / jnp.sum(powers, axis=1, keepdims=True)
        s.probs[it] = probs
        mixed = dot(side_by_side(probs.astype(BF16)), val)
        s.left[rows, cols(n.pairs + pair, LANES)] = mixed.astype(BF16)


def attend_out(n, w, v, s):
    width, tiles = n.width, n.width // TILE

    @pl.loop(0, tiles, unroll=True)
    def _(t):
        product = dot(s.left[:, width : 2 * width], w.out[:, cols(t)])
        s.norm_attn[:, cols(t)] = s.left[:, cols(t)].astype(F32) + product + v.b_out[:, cols(t)]


def attend_norm(n, v, s):
    width = n.width

    def keep_h1(rows, value):
        s.left[rows, 2 * width : 3 * width] = value

    norm_rows(n, s.norm_attn, s.spread_attn, v.gain_attn[...], v.shift_attn[...], keep_h1)


def go_up(n, w, v, s):
    width, tiles, left_u = n.width, n.width // TILE, 3 * (n.width // TILE)
    step = n.block // 3
    c = (2 / math.pi) ** 0.5
    staged = s.norm_ffn

    def bend(t, i):
        for at in range(0, n.rows, step):
            rows = slice(at, at + step)
            z = staged[rows, i * TILE : (i + 1) * TILE] + v.b_up[:, cols(t)]
            square = z * z
            half = 0.5 + 0.5 * jnp.tanh(z * (c + 0.044715 * c * square))
            value = z * half
            s.left[rows, cols(left_u + t)] = value.astype(BF16)
            s.slope[rows, cols(t)] = (half + value * (1.0 - half) * (2.0 * c + 0.26829 * c * square)).astype(BF16)

    @pl.loop(0, n.hidden // width)
    def _(group):
        for i in range(tiles):
            staged[:, i * TILE : (i + 1) * TILE] = dot(s.left[:, 2 * width : 3 * width], w.up[:, cols(group * tiles + i)])
            if i:
                bend(group * tiles + i - 1, i - 1)
        bend(group * tiles + tiles - 1, tiles - 1)


def go_down(n, w, v, s):
    width, tiles = n.width, n.width // TILE

    @pl.loop(0, tiles, unroll=True)
    def _(t):
        product = dot(s.left[:, 3 * width :], w.down[:, cols(t)])
        s.norm_ffn[:, cols(t)] = s.left[:, cols(2 * tiles + t)].astype(F32) + product + v.b_down[:, cols(t)]


def ffn_norm(n, v, s, y):
    def keep_y(rows, value):
        y[rows, :] = value

    norm_rows(n, s.norm_ffn, s.spread_ffn, v.gain_ffn[...], v.shift_ffn[...], keep_y)


def ffn_norm_back(n, v, s, dy, right, smalls, resid):
    width = n.width
    df_cols = slice(4 * width + n.hidden, 5 * width + n.hidden)

    def keep_df(rows, value):
        resid[rows, :] = value
        right[rows, df_cols] = value.astype(BF16)

    gain, shift, low = norm_back(n, lambda rows: dy[rows, :].astype(F32), s.norm_ffn, s.spread_ffn, v.gain_ffn[...], keep_df)
    smalls[10:11, :], smalls[11:12, :], smalls[9:10, :] = gain, shift, low


def down_back(n, w, s, right, smalls, sent):
    width, tiles = n.width, n.width // TILE
    df_cols = slice(4 * width + n.hidden, 5 * width + n.hidden)
    step = n.block // 3
    staged = s.norm_ffn

    def bend(group, i):
        t = group * tiles + i
        total = jnp.zeros((8, TILE), F32)
        for at in range(0, n.rows, step):
            rows = slice(at, at + step)
            dz = (staged[rows, i * TILE : (i + 1) * TILE] * s.slope[rows, cols(t)].astype(F32)).astype(BF16)
            right[rows, cols(4 * tiles + t)] = dz
            total = total + jnp.sum(dz.astype(F32).reshape(step // 8, 8, TILE), axis=0)
        smalls[pl.ds(5 + group, 1), cols(i)] = jnp.sum(total, axis=0, keepdims=True)

    @pl.loop(0, n.hidden // width)
    def _(group):
        for i in range(tiles):
            staged[:, i * TILE : (i + 1) * TILE] = dot_nt(right[:, df_cols], w.down[cols(group * tiles + i), :])
            if i:
                bend(group, i - 1)
        bend(group, tiles - 1)
        sent(group)


def up_back(n, w, dy, right, resid):
    width, tiles = n.width, n.width // TILE

    @pl.loop(0, tiles, unroll=True)
    def _(t):
        spread = dot_nt(right[:, 4 * width : 4 * width + n.hidden], w.up[cols(t), :])
        dy[:, cols(t)] = (spread + resid[:, cols(t)]).astype(BF16)


def attend_norm_back(n, v, s, dy, right, smalls, resid):
    width = n.width

    def keep_da(rows, value):
        resid[rows, :] = value
        right[rows, 3 * width : 4 * width] = value.astype(BF16)

    gain, shift, low = norm_back(n, lambda rows: dy[rows, :].astype(F32), s.norm_attn, s.spread_attn, v.gain_attn[...], keep_da)
    smalls[3:4, :], smalls[4:5, :], smalls[2:3, :] = gain, shift, low


def out_back(n, w, dy, right):
    width, tiles = n.width, n.width // TILE

    @pl.loop(0, tiles, unroll=True)
    def _(t):
        dy[:, cols(t)] = dot_nt(right[:, 3 * width : 4 * width], w.out[cols(t), :]).astype(BF16)


def attend_back(n, v, s, dy, right, smalls, table_sum, chosen, between):
    width = n.width
    factor = (LANES // 2) ** -0.5
    table_sum[...] = jnp.zeros(table_sum.shape, F32)
    square = (n.seq, n.seq)
    same = jnp.where(iota(square, 0) + iota(square, 1) == n.seq - 1, 1.0, 0.0).astype(BF16)
    for b in range(n.micro):
        order_col = to_column(v.order[b : b + 1, :].astype(F32), n)
        predicted = picked(order_col, n, n.seq - 1 - iota((n.query, n.seq), 1))
        chosen[b, : n.seq, :] = same
        chosen[b, n.seq :, :] = jnp.where(predicted, 1.0, 0.0).astype(BF16)

    @pl.loop(0, n.micro * n.pairs // UNROLL)
    def _(outside):
        for inside in range(UNROLL):
            it = outside * UNROLL + inside
            b, pair = it // n.pairs, it % n.pairs
            start = b * n.block
            rows = pl.ds(pl.multiple_of(start, 16), n.block)
            keys = pl.ds(pl.multiple_of(start, 16), n.seq)
            rest = pl.ds(pl.multiple_of(start + n.seq, 16), n.query)
            grad = both_heads(dy[rows, cols(pair, LANES)])
            q = both_heads(s.qkv[rows, cols(pair, LANES)])
            k = both_heads(s.qkv[keys, cols(n.pairs + pair, LANES)])
            val = s.qkv[keys, cols(2 * n.pairs + pair, LANES)]
            probs = s.probs[it]
            grad_probs = dot_nt(grad, val)
            inner = jnp.sum(probs * grad_probs, axis=1, keepdims=True)
            grad_scores = (probs * (grad_probs - inner)).astype(BF16)
            right[rows, cols(pair, LANES)] = (dot(side_by_side(grad_scores), k) * factor).astype(BF16)
            right[keys, cols(n.pairs + pair, LANES)] = (dot_tn(grad_scores, q) * factor).astype(BF16)
            right[keys, cols(2 * n.pairs + pair, LANES)] = dot_tn(probs.astype(BF16), grad).astype(BF16)
            none = jnp.zeros((n.query, LANES), BF16)
            right[rest, cols(n.pairs + pair, LANES)] = none
            right[rest, cols(2 * n.pairs + pair, LANES)] = none
            for half in range(2):
                of_head = grad_scores[half * n.block : (half + 1) * n.block]
                table_sum[2 * pair + half] += dot_tn(chosen[b], of_head)
        between(outside)

    smalls[0:1, :] = jnp.sum(right[:, :width].astype(F32), axis=0, keepdims=True)
    smalls[1:2, :] = jnp.sum(right[:, 2 * width : 3 * width].astype(F32), axis=0, keepdims=True)


def table_back(n, smalls, table_sum):
    by_place = []
    for h in range(n.heads):
        wide = jnp.concatenate([table_sum[h], jnp.zeros((n.seq, n.seq), F32)], axis=1)
        turned = pltpu.roll(wide, n.seq + 1, 1, stride=1, stride_axis=0)
        by_place.append(jnp.sum(turned, axis=0, keepdims=True))
    by_place = jnp.concatenate(by_place, axis=0)
    smalls[12 : 12 + n.heads, : n.buckets] = dot_nt(by_place, place_buckets(n), lax.Precision.HIGHEST)


def inputs_back(n, w, right, resid, dx):
    width, tiles = n.width, n.width // TILE

    @pl.loop(0, tiles, unroll=True)
    def _(t):
        total = resid[:, cols(t)]
        for i, matrix in enumerate((w.query, w.key, w.value)):
            total = total + dot_nt(right[:, i * width : (i + 1) * width], matrix[cols(t), :])
        dx[:, cols(t)] = total.astype(BF16)


def tiles_of(n, core):
    tiles, groups = n.width // TILE, n.hidden // n.width
    down = groups * tiles // 2

    def ffn(i):
        is_down = i < down
        up = i - down
        left = jnp.where(is_down, 3 * tiles + core * down + i, 2 * tiles + up % tiles)
        return left, jnp.where(is_down, 4 + groups, 4 + core * (groups // 2) + up // tiles)

    def attention(i):
        group = i // tiles
        return i % tiles + jnp.where(core * group == 1, tiles, 0), 2 * core + group

    return (ffn, 2 * down), (attention, 2 * tiles)


def weight_grads(n, of, count, first, left, right, packed):
    per = TILE // packed.shape[2] // packed.shape[1]
    by = math.gcd(count, UNROLL)

    @pl.loop(0, count // by)
    def _(outside):
        for inside in range(by):
            i = outside * by + inside
            left_tile, group = of(i)
            rhs = right[:, pl.ds(pl.multiple_of(group * n.width, n.width), n.width)]
            product = dot_tn(left[:, cols(left_tile)], rhs).astype(BF16)
            packed[pl.ds((first + i) * per, per)] = product.reshape((per,) + packed.shape[1:])


class Landing(NamedTuple):
    from_y: Any
    end_b: Any
    end_a: Any
    mid_a: Any
    mid_b: Any
    rung_b: Any


class Arrival(NamedTuple):
    y: Any
    end_b: Any
    end_a: Any
    mid_a: Any
    mid_b: Any
    rung: Any
    own_a: Any
    own_b: Any
    end_final: Any
    y_final: Any
    mid_final: Any
    end_both: Any
    sibling: Any


class Place(NamedTuple):
    core: Any
    y: Any
    mine: Any
    other: Any
    is_end: Any
    is_mid: Any
    sibling: Any
    y_peer: Any
    z_in: Any
    z_out: Any
    z_mid: Any
    across: Any
    doubling: Any


def find_place():
    pipe, index = lax.axis_index("pipe"), lax.axis_index("dp")
    base, local = index // 16 * 16, index % 16
    z, y, core = local // 4, local // 2 % 2, local % 2

    def at(zz, yy, cc):
        return (pipe, base + zz * 4 + yy * 2 + cc)

    return Place(
        core,
        y,
        z + 1,
        4 - z,
        (z == 0) | (z == 3),
        (z == 1) | (z == 2),
        at(z, y, 1 - core),
        at(z, 1 - y, core),
        at(jnp.where(z == 0, 1, 2), y, core),
        at(jnp.where(z == 1, 0, 3), y, core),
        at(3 - z, y, core),
        (1 - pipe, index),
        [(pipe, base + jnp.bitwise_xor(local, 1 << j)) for j in range(4)],
    )


def greet_all(me):
    barrier = pltpu.get_barrier_semaphore()
    for device in me.doubling + [me.across]:
        pl.semaphore_signal(barrier, inc=1, device_id=device, device_id_type=MESH)

    @pl.when(me.is_mid)
    def _():
        pl.semaphore_signal(barrier, inc=1, device_id=me.z_mid, device_id_type=MESH)
        pl.semaphore_wait(barrier, 6)

    @pl.when(me.is_end)
    def _():
        pl.semaphore_wait(barrier, 5)


def remote(src, dst, send, recv, device):
    return pltpu.make_async_remote_copy(src_ref=src, dst_ref=dst, send_sem=send, recv_sem=recv, device_id=device, device_id_type=MESH)


def wait_for(ref, sem):
    pltpu.make_async_copy(ref, ref, sem).wait()


def added(a, b):
    return (a.astype(F32) + b.astype(F32)).astype(BF16)


def sums(me, packed, out, land, sem, send):
    steps = packed.shape[0]
    c, y, mine, other = me.core, me.y, me.mine, me.other
    both = pl.ds(2, 2)

    def s0(k):
        remote(packed.at[k, 1 - y], land.from_y.at[k], send.at[0], sem.y.at[jnp.bitwise_and(k, RING - 1)], me.y_peer).start()

        @pl.when(me.is_end)
        def _():
            remote(packed.at[k, both], land.end_b.at[k], send.at[1], sem.end_b.at[jnp.bitwise_and(k, RING - 1)], me.z_in).start()

    def s1(k):
        wait_for(land.from_y.at[k], sem.y.at[jnp.bitwise_and(k, RING - 1)])
        packed[k, y] = added(packed[k, y], land.from_y[k])

        @pl.when(me.is_end)
        def _():
            remote(packed.at[k, y], land.end_a.at[k], send.at[2], sem.end_a.at[jnp.bitwise_and(k, RING - 1)], me.z_in).start()

        @pl.when(me.is_mid)
        def _():
            wait_for(land.end_b.at[k], sem.end_b.at[jnp.bitwise_and(k, RING - 1)])
            packed[k, both] = added(packed[k, both], land.end_b[k])
            remote(packed.at[k, other], land.mid_b.at[k], send.at[3], sem.mid_b.at[jnp.bitwise_and(k, RING - 1)], me.z_mid).start()

    def s2(k):
        @pl.when(me.is_mid)
        def _():
            wait_for(land.end_a.at[k], sem.end_a.at[jnp.bitwise_and(k, RING - 1)])
            packed[k, y] = added(packed[k, y], land.end_a[k])
            remote(packed.at[k, y], land.mid_a.at[k], send.at[4], sem.mid_a.at[jnp.bitwise_and(k, RING - 1)], me.z_mid).start()
            wait_for(land.mid_b.at[k], sem.mid_b.at[jnp.bitwise_and(k, RING - 1)])
            packed[k, mine] = added(packed[k, mine], land.mid_b[k])
            remote(packed.at[k, mine], land.rung_b.at[k], send.at[5], sem.rung.at[jnp.bitwise_and(k, RING - 1)], me.y_peer).start()

    def s3(k):
        @pl.when(me.is_mid)
        def _():
            wait_for(land.mid_a.at[k], sem.mid_a.at[jnp.bitwise_and(k, RING - 1)])
            total = land.from_y.at[k]
            total[...] = added(packed[k, y], land.mid_a[k])
            remote(total, out.at[c, k, y], send.at[6], sem.end_final.at[jnp.bitwise_and(k, RING - 1)], me.z_out).start()
            remote(total, out.at[c, k, y], send.at[7], sem.y_final.at[jnp.bitwise_and(k, RING - 1)], me.y_peer).start()
            pltpu.make_async_copy(total, out.at[c, k, y], sem.own_a.at[jnp.bitwise_and(k, RING - 1)]).start()
            wait_for(land.rung_b.at[k], sem.rung.at[jnp.bitwise_and(k, RING - 1)])
            total = land.end_a.at[k]
            total[...] = added(packed[k, mine], land.rung_b[k])
            remote(total, out.at[c, k, mine], send.at[8], sem.mid_final.at[jnp.bitwise_and(k, RING - 1)], me.z_mid).start()
            pltpu.make_async_copy(total, out.at[c, k, mine], sem.own_b.at[jnp.bitwise_and(k, RING - 1)]).start()

    def s4(k):
        @pl.when(me.is_end)
        def _():
            wait_for(out.at[c, k, y], sem.end_final.at[jnp.bitwise_and(k, RING - 1)])
            remote(out.at[c, k, y], out.at[c, k, y], send.at[7], sem.y_final.at[jnp.bitwise_and(k, RING - 1)], me.y_peer).start()

        @pl.when(me.is_mid)
        def _():
            wait_for(out.at[c, k, other], sem.mid_final.at[jnp.bitwise_and(k, RING - 1)])
            wait_for(out.at[c, k, mine], sem.own_b.at[jnp.bitwise_and(k, RING - 1)])
            remote(out.at[c, k, both], out.at[c, k, both], send.at[9], sem.end_both.at[jnp.bitwise_and(k, RING - 1)], me.z_out).start()

    def s5(k):
        wait_for(out.at[c, k, 1 - y], sem.y_final.at[jnp.bitwise_and(k, RING - 1)])

        @pl.when(me.is_end)
        def _():
            wait_for(out.at[c, k, both], sem.end_both.at[jnp.bitwise_and(k, RING - 1)])

        @pl.when(me.is_mid)
        def _():
            wait_for(out.at[c, k, y], sem.own_a.at[jnp.bitwise_and(k, RING - 1)])

        remote(out.at[c, k], out.at[c, k], send.at[10], sem.sibling.at[jnp.bitwise_and(k, RING - 1)], me.sibling).start()

    def s6(k):
        wait_for(out.at[1 - c, k], sem.sibling.at[jnp.bitwise_and(k, RING - 1)])

    stages = (s0, s1, s2, s3, s4, s5, s6)

    def slot(t):
        for i, stage in enumerate(stages):
            k = t - i * LAG

            @pl.when((k >= 0) & (k < steps))
            def _():
                stage(jnp.clip(k, 0, steps - 1))

    def finish():
        section = land.from_y
        wait_for(section, send.at[0])
        wait_for(section, send.at[7])
        wait_for(packed, send.at[10])

        @pl.when(me.is_end)
        def _():
            wait_for(land.end_b, send.at[1])
            wait_for(section, send.at[2])

        @pl.when(me.is_mid)
        def _():
            for which in (3, 4, 5, 6, 8):
                wait_for(section, send.at[which])
            wait_for(land.end_b, send.at[9])

    return slot, steps + (len(stages) - 1) * LAG, finish


def small_sums(me, smalls, held, total, recv, send):
    def source(j):
        return smalls if j == 0 else held.at[1, j - 1]

    def copy(j):
        return remote(source(j), held.at[0, j], send.at[j], recv.at[j], me.doubling[j])

    def step(j):
        if j >= 0:
            copy(j).wait()
            summed = source(j)[...] + held[0, j]
            if j == 3:
                total[...] = summed
            else:
                held[1, j] = summed
        if j < 3:
            copy(j + 1).start()

    return step


def copies_of(pairs, sems):
    return [pltpu.make_async_copy(src, dst, sems.at[i]) for i, (src, dst) in enumerate(pairs)]


def bucket_rows(n, content, query, wide):
    pairs = []
    for b in range(n.micro):
        pairs.append((content.at[0, pl.ds(b * n.seq, n.seq)], wide.at[pl.ds(b * n.block, n.seq)]))
        pairs.append((query.at[0, pl.ds(b * n.query, n.query)], wide.at[pl.ds(b * n.block + n.seq, n.query)]))
    return pairs


def whole_kernel(n, *refs):
    content, query, *refs = refs
    w_hbm, refs = Weights(*refs[:6]), refs[6:]
    v, refs = Vectors(*refs[:12]), refs[12:]
    content_out, query_out, out, total, *refs = refs
    w, refs = Weights(*refs[:6]), refs[6:]
    left, right, y, dx, dy, resid, table_sum, chosen, smalls, held, packed, *refs = refs
    s, refs = State(left.at[pl.ds(0, n.rows)], *refs[:7]), refs[7:]
    land, refs = Landing(*refs[:6]), refs[6:]
    arrive, refs = Arrival(*refs[:13]), refs[13:]
    w_sem, in_sem, grad_sem, out_sem, pipe_send, pipe_recv, core_send, core_recv, small_send, small_recv, sum_send = refs
    width, rows = n.width, n.rows
    inputs = s.left.at[:, pl.ds(0, width)]
    mine_right = right.at[pl.ds(0, rows)]
    groups = n.hidden // width
    first, last = lax.axis_index("pipe") == 0, lax.axis_index("pipe") == 1
    me = find_place()

    weights = copies_of([(a.at[0], b) for a, b in zip(w_hbm, w)], w_sem)
    own_rows = copies_of(bucket_rows(n, content, query, inputs), in_sem)
    own_grads = copies_of(bucket_rows(n, content, query, dy), in_sem)

    @pl.when(first)
    def _():
        for cp in own_rows:
            cp.start()

    @pl.when(last)
    def _():
        for cp in own_grads:
            cp.start()

    for cp in weights:
        cp.start()
    greet_all(me)
    bias_and_mask(n, v, s.probs)
    hand_up = remote(y, inputs, pipe_send, pipe_recv, me.across)
    hand_down = remote(dx, dy, pipe_send, pipe_recv, me.across)

    def to_core(which, src, dst):
        return remote(src, dst, core_send.at[which], core_recv.at[which], me.sibling)

    def left_copy(which, at, size):
        return to_core(which, left.at[pl.ds(0, rows), pl.ds(at, size)], left.at[pl.ds(rows, rows), pl.ds(at, size)])

    def right_copy(which, at, size):
        return to_core(which, right.at[pl.ds(0, rows), pl.ds(at, size)], right.at[pl.ds(rows, rows), pl.ds(at, size)])

    share_left = left_copy(0, 0, 3 * width + n.hidden)
    share_attention = right_copy(1, 0, 3 * width)
    share_da = right_copy(2, 3 * width, width)
    share_df = right_copy(3, (4 + groups) * width, width)

    def share_dz(group):
        return right_copy(4 + group, pl.multiple_of((4 + group) * width, width), width)

    @pl.when(first)
    def _():
        for cp in own_rows:
            cp.wait()

    @pl.when(last)
    def _():
        hand_up.wait_recv()

    done = set()

    def ready(i):
        if i not in done:
            done.add(i)
            weights[i].wait()

    project(n, ready, w, v, s)
    attend(n, s)
    ready(3)
    attend_out(n, w, v, s)
    attend_norm(n, v, s)
    ready(4)
    go_up(n, w, v, s)
    ready(5)
    go_down(n, w, v, s)
    ffn_norm(n, v, s, y)

    @pl.when(first)
    def _():
        hand_up.start()

    share_left.start()
    results = copies_of([(b, a) for a, b in bucket_rows(n, content_out, query_out, y)], out_sem)
    results_back = copies_of([(b, a) for a, b in bucket_rows(n, content_out, query_out, dx)], out_sem)

    @pl.when(last)
    def _():
        for cp in results:
            cp.start()
        for cp in own_grads:
            cp.wait()

    @pl.when(first)
    def _():
        hand_up.wait_send()
        hand_down.wait_recv()

    slot, slots, finish = sums(me, packed, out, land, arrive, sum_send)
    (ffn, ffn_count), (attention, attention_count) = tiles_of(n, me.core)
    ffn_norm_back(n, v, s, dy, mine_right, smalls, resid)
    share_df.start()
    down_back(n, w, s, mine_right, smalls, lambda group: share_dz(group).start())
    up_back(n, w, dy, mine_right, resid)

    def ffn_grads():
        share_left.wait_recv()
        share_df.wait_recv()
        for group in range(groups):
            share_dz(group).wait_recv()
        weight_grads(n, ffn, ffn_count, 0, left, right, packed)

    pl.when(first)(ffn_grads)
    attend_norm_back(n, v, s, dy, mine_right, smalls, resid)
    share_da.start()
    out_back(n, w, dy, mine_right)
    early = n.micro * n.pairs // UNROLL * EARLY

    def between(outside):
        @pl.when(first)
        def _():
            @pl.loop(0, EARLY)
            def _(i):
                slot(outside * EARLY + i)

    attend_back(n, v, s, dy, mine_right, smalls, table_sum, chosen, between)
    share_attention.start()
    inputs_back(n, w, mine_right, resid, dx)

    @pl.when(last)
    def _():
        hand_down.start()

    table_back(n, smalls, table_sum)
    small_step = small_sums(me, smalls, held, total, small_recv, small_send)
    small_step(-1)

    @pl.when(first)
    def _():
        for cp in results_back:
            cp.start()

    pl.when(last)(ffn_grads)
    share_attention.wait_recv()
    share_da.wait_recv()
    weight_grads(n, attention, attention_count, ffn_count, left, right, packed)
    start = jnp.where(first, early, 0)

    @pl.loop(0, slots - start)
    def _(i):
        slot(start + i)
        for j in range(4):
            pl.when(i == 3 * (j + 1))(functools.partial(small_step, j))

    finish()
    for which in [share_left, share_attention, share_da, share_df] + [share_dz(group) for group in range(groups)]:
        which.wait_send()
    for cp in results:
        cp.wait()

    @pl.when(last)
    def _():
        hand_down.wait_send()


def shaped(shape, dtype=BF16):
    return jax.ShapeDtypeStruct(shape, dtype)


def run_layers(n, content, query, w, v):
    rows, width = n.rows, n.width
    vmem, smem, anywhere = (pl.BlockSpec(memory_space=space) for space in (pltpu.VMEM, pltpu.SMEM, pl.ANY))
    dma = pltpu.SemaphoreType.DMA
    steps = (4 * width + 2 * n.hidden) // (2 * 4 * CHUNK)
    half = (steps, 4, CHUNK, width)
    section, sections = pltpu.VMEM((steps, CHUNK, width), BF16), pltpu.VMEM((steps, 2, CHUNK, width), BF16)
    small_shape = (24, width)
    left, *others = state_shapes(n)
    scratch = [pltpu.VMEM(m.shape[1:], BF16) for m in w]
    scratch += [
        pltpu.VMEM((2 * rows, left[0][1]), BF16),
        pltpu.VMEM((2 * rows, 5 * width + n.hidden), BF16),
        pltpu.VMEM((rows, width), BF16),
        pltpu.VMEM((rows, width), BF16),
        pltpu.VMEM((rows, width), BF16),
        pltpu.VMEM((rows, width), F32),
        pltpu.VMEM((n.heads, n.seq, n.seq), F32),
        pltpu.VMEM((n.micro, n.block, n.seq), BF16),
        pltpu.VMEM(small_shape, F32),
        pltpu.VMEM((2, 4) + small_shape, F32),
        pltpu.VMEM(half, BF16),
    ]
    scratch += [pltpu.VMEM(shape, dtype) for shape, dtype in others]
    scratch += [section, sections, section, section, section, section]
    scratch += [dma((RING,))] * 13
    shares = 4 + n.hidden // width
    scratch += [dma((6,)), dma((2 * n.micro,)), dma((2 * n.micro,)), dma((2 * n.micro,)), dma, dma, dma((shares,)), dma((shares,)), dma((4,)), dma((4,)), dma((11,))]
    return pl.pallas_call(
        functools.partial(whole_kernel, n),
        out_shape=[shaped(content.shape), shaped(query.shape), shaped((2,) + half), shaped(small_shape, F32)],
        in_specs=[anywhere] * 8 + [vmem] * 10 + [smem, vmem],
        out_specs=[anywhere] * 3 + [vmem],
        scratch_shapes=scratch,
        compiler_params=pltpu.CompilerParams(collective_id=1, has_side_effects=True, vmem_limit_bytes=VMEM_LIMIT),
    )(content, query, *w, *v)


def unpack_kernel(n, packed, smalls, *refs):
    grads, refs = Weights(*(ref.at[0] for ref in refs[:6])), refs[6:]
    vectors, table, (block, wide, in_sem, out_sem) = refs[:9], refs[9], refs[10:]
    width = n.width
    groups = n.hidden // width
    places = []
    for core in range(2):
        places += [grads.down.at[pl.ds((core * groups // 2 + i) * width, width)] for i in range(groups // 2)]
        places += [grads.up.at[:, pl.ds((core * groups // 2 + i) * width, width)] for i in range(groups // 2)]
        places += [grads.value, grads.out] if core else [grads.query, grads.key]
    count, steps = block.shape[:2]
    loads = [pltpu.make_async_copy(packed.at[i // (count // 2), pl.ds(i % (count // 2) * steps, steps)], block.at[i], in_sem.at[i]) for i in range(count)]
    stores = [pltpu.make_async_copy(wide.at[i], place, out_sem.at[i]) for i, place in enumerate(places)]
    for cp in loads:
        cp.start()
    at = 0
    for vector in vectors:
        for part in range(vector.shape[1] // width):
            vector[:, part * width : (part + 1) * width] = smalls[at : at + 1, :]
            at += 1
    for h in range(n.heads):
        table[h] = smalls[12 + h : 13 + h, : n.buckets]
    rows = block.shape[2] * block.shape[3]
    for i in range(count):
        loads[i].wait()

        @pl.loop(0, steps)
        def _(step):
            wide[i, pl.ds(pl.multiple_of(step * rows, rows), rows), :] = block[i, step].astype(F32).reshape(rows, width)

        stores[i].start()
    for cp in stores:
        cp.wait()


def unpack(n, packed, smalls):
    width, hidden = n.width, n.hidden
    square, vector = (1, width, width), (1, width)
    matrices = [square] * 4 + [(1, width, hidden), (1, hidden, width)]
    vectors = [vector] * 5 + [(1, hidden)] + [vector] * 3
    vmem, anywhere = pl.BlockSpec(memory_space=pltpu.VMEM), pl.BlockSpec(memory_space=pl.ANY)
    count = 4 + 2 * hidden // width
    steps = 2 * packed.shape[1] // count
    *made, table = pl.pallas_call(
        functools.partial(unpack_kernel, n),
        out_shape=[shaped(shape, F32) for shape in matrices + vectors + [(n.heads, 1, n.buckets)]],
        in_specs=[anywhere, vmem],
        out_specs=[anywhere] * 6 + [vmem] * 10,
        scratch_shapes=[
            pltpu.VMEM((count, steps) + packed.shape[2:], packed.dtype),
            pltpu.VMEM((count, width, width), F32),
            pltpu.SemaphoreType.DMA((count,)),
            pltpu.SemaphoreType.DMA((count,)),
        ],
        compiler_params=pltpu.CompilerParams(vmem_limit_bytes=VMEM_LIMIT),
    )(packed, smalls)
    return made[:6], made[6:] + [jnp.transpose(table, (1, 2, 0))]


def across_blocks(packed, smalls):
    blocks = lax.axis_size("dp") // 16
    if blocks > 1:
        groups = [[block * 16 + i for block in range(blocks)] for i in range(16)]
        packed = lax.psum(packed.astype(F32), "dp", axis_index_groups=groups)
        smalls = lax.psum(smalls, "dp", axis_index_groups=groups)
    return packed, smalls


def on_device(content_ends, query_ends, w_query, b_query, w_key, w_value, b_value, w_out, b_out, gain_attn, shift_attn, w_up, b_up, w_down, b_down, gain_ffn, shift_ffn, rel_table, doc_lengths, position_order):
    micro, seq = position_order.shape
    n = Sizes(micro, seq, query_ends.shape[1] // micro, content_ends.shape[2], rel_table.shape[2], w_up.shape[2], rel_table.shape[1])
    w = Weights(w_query, w_key, w_value, w_out, w_up, w_down)
    v = Vectors(b_query, b_value, b_out, gain_attn, shift_attn, b_up, b_down, gain_ffn, shift_ffn, jnp.transpose(rel_table, (2, 0, 1)), doc_lengths, position_order)
    content_out, query_out, packed, smalls = run_layers(n, content_ends, query_ends, w, v)
    packed, smalls = across_blocks(packed, smalls)
    g, d = unpack(n, packed, smalls)
    return content_out, query_out, g[0], d[0], g[1], g[2], d[1], g[3], d[2], d[3], d[4], g[4], d[5], g[5], d[6], d[7], d[8], d[9]


def solution(mesh):
    rows, matrix, vector, buckets = P("pipe", "dp", None), P("pipe", None, None), P("pipe", None), P("dp", None)
    grads = (matrix, vector, matrix, matrix, vector, matrix, vector, vector, vector, matrix, vector, matrix, vector, vector, vector, matrix)
    return jax.shard_map(on_device, mesh=mesh, in_specs=(rows, rows, *grads, buckets, buckets), out_specs=(rows, rows, *grads), check_vma=False)
```

```python
import functools
import math
from typing import Any, NamedTuple

import jax
import jax.numpy as jnp
from jax import lax
from jax.experimental import pallas as pl
from jax.experimental.pallas import tpu as pltpu
from jax.sharding import PartitionSpec as P

MESH = pl.DeviceIdType.MESH
F32 = jnp.float32
BF16 = jnp.bfloat16
NORM_EPS = 1e-05
NEG_FILL = -1e30
THRESHOLDS = (12, 16, 23, 32, 46, 64, 91)
TILE = 256
LANES = 128
UNROLL = 3
EARLY = 3
LAG = 2
RING = 16
LENT = 8
CHUNK = 16
VMEM_LIMIT = 63 * 2**20


class Sizes(NamedTuple):
    micro: int
    seq: int
    query: int
    width: int
    heads: int
    hidden: int
    buckets: int

    @property
    def block(self):
        return self.seq + self.query

    @property
    def rows(self):
        return self.micro * self.block

    @property
    def pairs(self):
        return self.width // LANES


class Weights(NamedTuple):
    query: Any
    key: Any
    value: Any
    out: Any
    up: Any
    down: Any


class Vectors(NamedTuple):
    b_query: Any
    b_value: Any
    b_out: Any
    gain_attn: Any
    shift_attn: Any
    b_up: Any
    b_down: Any
    gain_ffn: Any
    shift_ffn: Any
    rel_table: Any
    lengths: Any
    order: Any


class State(NamedTuple):
    left: Any
    qkv: Any
    slope: Any
    probs: Any
    norm_attn: Any
    norm_ffn: Any
    spread_attn: Any
    spread_ffn: Any


def state_shapes(n):
    return State(
        ((n.rows, 3 * n.width + n.hidden), BF16),
        ((n.rows, 3 * n.width), BF16),
        ((n.rows, n.hidden), BF16),
        ((n.micro * n.pairs, 2 * n.block, n.seq), F32),
        ((n.rows, n.width), F32),
        ((n.rows, n.width), F32),
        ((n.rows, 1), F32),
        ((n.rows, 1), F32),
    )


def dot(a, b):
    return jnp.dot(a, b, preferred_element_type=F32)


def dot_nt(a, b, precision=None):
    return lax.dot_general(a, b, (((1,), (1,)), ((), ())), precision=precision, preferred_element_type=F32)


def dot_tn(a, b):
    return lax.dot_general(a, b, (((0,), (0,)), ((), ())), preferred_element_type=F32)


def iota(shape, dim):
    return lax.broadcasted_iota(jnp.int32, shape, dim)


def cols(at, size=TILE):
    return pl.ds(pl.multiple_of(at * size, size), size)


def bucket_of(offset):
    distance = jnp.abs(offset)
    bucket = jnp.minimum(distance, 8) + jnp.where(offset < 0, 16, 0)
    for bound_at in THRESHOLDS:
        bucket = bucket + jnp.where(distance >= bound_at, 1, 0)
    return bucket


def place_buckets(n):
    shape = (n.buckets, 2 * n.seq)
    at = iota(shape, 1)
    offset = jnp.where(at < n.seq, -at, 2 * n.seq - at)
    return jnp.where(bucket_of(offset) == iota(shape, 0), 1.0, 0.0)


def to_column(row, n):
    shape = (n.seq, n.seq)
    return jnp.sum(jnp.where(iota(shape, 0) == iota(shape, 1), row, 0.0), axis=1, keepdims=True)


def bias_and_mask(n, v, bias):
    seq, query = n.seq, n.query
    by_head = jnp.concatenate([v.rel_table[h] for h in range(n.heads)], axis=0)
    base = jnp.dot(by_head, place_buckets(n), precision=lax.Precision.HIGHEST, preferred_element_type=F32)
    square = (seq, seq)
    row_at, col_at = iota(square, 0).astype(F32), iota(square, 1).astype(F32)
    visible_from = float(seq - query)
    content_sees, query_sees, chosen = [], [], []
    for b in range(n.micro):
        order_row = v.order[b : b + 1, :].astype(F32)
        order_col = to_column(order_row, n)
        rank_row = jnp.sum(jnp.where(order_col == col_at, row_at, 0.0), axis=0, keepdims=True)
        rank_col = to_column(rank_row, n)
        ends, total = [], jnp.int32(0)
        for d in range(v.lengths.shape[1]):
            total = total + v.lengths[b, d]
            ends.append(total)

        def doc_of(at):
            found = jnp.zeros(at.shape, F32)
            for end in ends:
                found = found + jnp.where(at >= end.astype(F32), 1.0, 0.0)
            return found

        doc_row = doc_of(iota((1, seq), 1).astype(F32))
        doc_col = doc_of(iota((seq, 1), 0).astype(F32))
        unmasked = rank_row < visible_from
        content_sees.append((doc_col == doc_row) & (unmasked | (rank_row <= rank_col)))
        place = order_col[seq - query :]
        at_place = place == iota((query, seq), 1).astype(F32)
        rank = visible_from + iota((query, 1), 0).astype(F32)
        query_sees.append((doc_of(place) == doc_row) & (unmasked | (rank_row < rank) | at_place))
        chosen.append(jnp.where(at_place, 1.0, 0.0).astype(BF16))
    for h in range(n.heads):
        spread = jnp.broadcast_to(base[h : h + 1, :], (seq, 2 * seq))
        table = pltpu.roll(spread, 0, 1, stride=1, stride_axis=0)[:, :seq]
        high = table.astype(BF16)
        rest = table - high.astype(F32)
        middle = rest.astype(BF16)
        low = (rest - middle.astype(F32)).astype(BF16)
        for b in range(n.micro):
            of_query = dot(chosen[b], high) + dot(chosen[b], middle) + dot(chosen[b], low)
            start = (h % 2) * n.block
            bias[b * n.pairs + h // 2, start : start + seq, :] = jnp.where(content_sees[b], table, NEG_FILL)
            bias[b * n.pairs + h // 2, start + seq : start + n.block, :] = jnp.where(query_sees[b], of_query, NEG_FILL)


def half_masks():
    at = iota((1, LANES), 1)
    return jnp.where(at < LANES // 2, 1.0, 0.0).astype(BF16), jnp.where(at < LANES // 2, 0.0, 1.0).astype(BF16)


def both_heads(values):
    first, second = half_masks()
    return jnp.concatenate([values * first, values * second], axis=0)


def side_by_side(stacked):
    half = stacked.shape[0] // 2
    return jnp.concatenate([stacked[:half], stacked[half:]], axis=1)


def block_rows(n, b):
    return pl.ds(pl.multiple_of(b * n.block, 16), n.block)


def norm_rows(n, b, summed, normed_ref, spread_ref, gain, shift, write):
    step = n.block // 3
    for at in range(0, n.block, step):
        rows = pl.ds(pl.multiple_of(b * n.block + at, 16), step)
        r = summed[rows, :]
        centered = r - jnp.mean(r, axis=1, keepdims=True)
        spread = lax.rsqrt(jnp.mean(centered * centered, axis=1, keepdims=True) + NORM_EPS)
        normed = centered * spread
        normed_ref[rows, :] = normed
        spread_ref[rows, :] = spread
        write(rows, (normed * gain + shift).astype(BF16))


def norm_back(n, grad_of, normed_ref, spread_ref, gain, write):
    step = n.block // 3

    def body(i, sums):
        rows = pl.ds(pl.multiple_of(i * step, step), step)
        grad = grad_of(rows)
        normed = normed_ref[rows, :]
        scaled = grad * gain
        inner = jnp.mean(scaled * normed, axis=1, keepdims=True)
        back = spread_ref[rows, :] * (scaled - jnp.mean(scaled, axis=1, keepdims=True) - normed * inner)
        write(rows, back)
        low = back.astype(BF16).astype(F32)
        return (
            sums[0] + jnp.sum(grad * normed, axis=0, keepdims=True),
            sums[1] + jnp.sum(grad, axis=0, keepdims=True),
            sums[2] + jnp.sum(low, axis=0, keepdims=True),
        )

    zero = jnp.zeros((1, n.width), F32)
    return lax.fori_loop(0, n.rows // step, body, (zero, zero, zero), unroll=3)


def project(n, b, ready, w, v, s):
    width, tiles = n.width, n.width // TILE
    rows = block_rows(n, b)
    for i, matrix in enumerate((w.query, w.key, w.value)):
        ready(i)
        for t in range(tiles):
            at = slice(t * TILE, (t + 1) * TILE)
            product = dot(s.left[rows, :width], matrix[:, at])
            if i == 0:
                product = product + v.b_query[:, at]
            if i == 2:
                product = product + v.b_value[:, at]
            s.qkv[rows, i * width + t * TILE : i * width + (t + 1) * TILE] = product.astype(BF16)


def attend(n, b, s):
    factor = (LANES // 2) ** -0.5
    rows, keys = block_rows(n, b), pl.ds(pl.multiple_of(b * n.block, 16), n.seq)
    for pair in range(n.pairs):
        it = b * n.pairs + pair

        def lanes(part):
            return slice((part * n.pairs + pair) * LANES, (part * n.pairs + pair + 1) * LANES)

        q = both_heads(s.qkv[rows, lanes(0)])
        val = both_heads(s.qkv[keys, lanes(2)])
        scores = dot_nt(q, s.qkv[keys, lanes(1)]) * factor + s.probs[it]
        powers = jnp.exp(scores - jnp.max(scores, axis=1, keepdims=True))
        probs = powers / jnp.sum(powers, axis=1, keepdims=True)
        s.probs[it] = probs
        s.left[rows, lanes(1)] = dot(side_by_side(probs.astype(BF16)), val).astype(BF16)


def attend_out(n, b, w, v, s, summed):
    width = n.width
    rows = block_rows(n, b)
    for t in range(width // TILE):
        at = slice(t * TILE, (t + 1) * TILE)
        product = dot(s.left[rows, width : 2 * width], w.out[:, at])
        summed[rows, at] = s.left[rows, at].astype(F32) + product + v.b_out[:, at]


def attend_norm(n, b, v, s, summed, copy):
    width = n.width

    def keep_h1(rows, value):
        s.left[rows, 2 * width : 3 * width] = value
        copy[rows, :] = value

    norm_rows(n, b, summed, s.norm_attn, s.spread_attn, v.gain_attn[...], v.shift_attn[...], keep_h1)


def go_up(n, b, w, v, s, h1):
    width, tiles, left_u = n.width, n.width // TILE, 3 * (n.width // TILE)
    step = n.block // 3
    c = (2 / math.pi) ** 0.5
    staged = s.norm_ffn

    def bend(t, i):
        for at in range(0, n.block, step):
            rows = pl.ds(pl.multiple_of(b * n.block + at, 16), step)
            z = staged[rows, i * TILE : (i + 1) * TILE] + v.b_up[:, cols(t)]
            square = z * z
            half = 0.5 + 0.5 * jnp.tanh(z * (c + 0.044715 * c * square))
            value = z * half
            s.left[rows, cols(left_u + t)] = value.astype(BF16)
            s.slope[rows, cols(t)] = (half + value * (1.0 - half) * (2.0 * c + 0.26829 * c * square)).astype(BF16)

    @pl.loop(0, n.hidden // width, unroll=True)
    def _(group):
        for i in range(tiles):
            staged[block_rows(n, b), i * TILE : (i + 1) * TILE] = dot(h1[block_rows(n, b), :], w.up[:, cols(group * tiles + i)])
            if i:
                bend(group * tiles + i - 1, i - 1)
        bend(group * tiles + tiles - 1, tiles - 1)


def go_down(n, b, w, v, s, summed):
    width = n.width
    rows = block_rows(n, b)
    for t in range(width // TILE):
        at = slice(t * TILE, (t + 1) * TILE)
        h1_at = slice(2 * width + t * TILE, 2 * width + (t + 1) * TILE)
        product = dot(s.left[rows, 3 * width :], w.down[:, at])
        summed[rows, at] = s.left[rows, h1_at].astype(F32) + product + v.b_down[:, at]


def ffn_norm(n, b, v, s, summed, y):
    def keep_y(rows, value):
        y[rows, :] = value

    norm_rows(n, b, summed, s.norm_ffn, s.spread_ffn, v.gain_ffn[...], v.shift_ffn[...], keep_y)


def ffn_norm_back(n, v, s, dy, right, smalls, resid, copy):
    width = n.width
    df_cols = slice(4 * width + n.hidden, 5 * width + n.hidden)

    def keep_df(rows, value):
        resid[rows, :] = value
        right[rows, df_cols] = copy[rows, :] = value.astype(BF16)

    gain, shift, low = norm_back(n, lambda rows: dy[rows, :].astype(F32), s.norm_ffn, s.spread_ffn, v.gain_ffn[...], keep_df)
    smalls[10:11, :], smalls[11:12, :], smalls[9:10, :] = gain, shift, low


def down_back(n, w, s, right, smalls, df, sent):
    width, tiles = n.width, n.width // TILE
    step = n.block // 3
    staged = s.norm_ffn

    def bend(group, i):
        t = group * tiles + i
        total = jnp.zeros((8, TILE), F32)
        for at in range(0, n.rows, step):
            rows = slice(at, at + step)
            dz = (staged[rows, i * TILE : (i + 1) * TILE] * s.slope[rows, cols(t)].astype(F32)).astype(BF16)
            right[rows, cols(4 * tiles + t)] = dz
            total = total + jnp.sum(dz.astype(F32).reshape(step // 8, 8, TILE), axis=0)
        smalls[pl.ds(5 + group, 1), cols(i)] = jnp.sum(total, axis=0, keepdims=True)

    @pl.loop(0, n.hidden // width, unroll=True)
    def _(group):
        for i in range(tiles):
            staged[:, i * TILE : (i + 1) * TILE] = dot_nt(df[...], w.down[cols(group * tiles + i), :])
            if i:
                bend(group, i - 1)
        bend(group, tiles - 1)
        sent(group)


def up_back(n, w, dy, right, resid):
    width, tiles = n.width, n.width // TILE

    @pl.loop(0, tiles, unroll=True)
    def _(t):
        spread = dot_nt(right[:, 4 * width : 4 * width + n.hidden], w.up[cols(t), :])
        dy[:, cols(t)] = (spread + resid[:, cols(t)]).astype(BF16)


def attend_norm_back(n, v, s, dy, right, smalls, resid):
    width = n.width

    def keep_da(rows, value):
        resid[rows, :] = value
        right[rows, 3 * width : 4 * width] = value.astype(BF16)

    gain, shift, low = norm_back(n, lambda rows: dy[rows, :].astype(F32), s.norm_attn, s.spread_attn, v.gain_attn[...], keep_da)
    smalls[3:4, :], smalls[4:5, :], smalls[2:3, :] = gain, shift, low


def out_back(n, w, dy, right):
    width, tiles = n.width, n.width // TILE

    @pl.loop(0, tiles, unroll=True)
    def _(t):
        dy[:, cols(t)] = dot_nt(right[:, 3 * width : 4 * width], w.out[cols(t), :]).astype(BF16)


def attend_back(n, v, s, dy, right, smalls, table_sum, chosen, between):
    width = n.width
    factor = (LANES // 2) ** -0.5
    table_sum[...] = jnp.zeros(table_sum.shape, F32)
    square = (n.seq, n.seq)
    same = jnp.where(iota(square, 0) + iota(square, 1) == n.seq - 1, 1.0, 0.0).astype(BF16)
    for b in range(n.micro):
        place = v.order[b : b + 1, n.seq - n.query :]
        chosen[b, :, : n.seq] = same
        chosen[b, :, n.seq :] = jnp.where(place == n.seq - 1 - iota((n.seq, n.query), 0), 1.0, 0.0).astype(BF16)

    @pl.loop(0, n.micro)
    def _(b):
        start = b * n.block
        rows, keys = block_rows(n, b), pl.ds(pl.multiple_of(start, 16), n.seq)
        rest = pl.ds(pl.multiple_of(start + n.seq, 16), n.query)
        for pair in range(n.pairs):
            q_at, k_at, v_at = (slice((part * n.pairs + pair) * LANES, (part * n.pairs + pair + 1) * LANES) for part in range(3))
            grad = both_heads(dy[rows, q_at])
            q = both_heads(s.qkv[rows, q_at])
            k = both_heads(s.qkv[keys, k_at])
            val = s.qkv[keys, v_at]
            probs = s.probs[b * n.pairs + pair]
            grad_probs = dot_nt(grad, val)
            inner = jnp.sum(probs * grad_probs, axis=1, keepdims=True)
            grad_scores = (probs * (grad_probs - inner)).astype(BF16)
            right[rows, q_at] = (dot(side_by_side(grad_scores), k) * factor).astype(BF16)
            right[keys, k_at] = (dot_tn(grad_scores, q) * factor).astype(BF16)
            right[keys, v_at] = dot_tn(probs.astype(BF16), grad).astype(BF16)
            none = jnp.zeros((n.query, LANES), BF16)
            right[rest, k_at] = none
            right[rest, v_at] = none
            for half in range(2):
                of_head = grad_scores[half * n.block : (half + 1) * n.block]
                table_sum[2 * pair + half] += dot(chosen[b], of_head)
        between(b)

    smalls[0:1, :] = jnp.sum(right[:, :width].astype(F32), axis=0, keepdims=True)
    smalls[1:2, :] = jnp.sum(right[:, 2 * width : 3 * width].astype(F32), axis=0, keepdims=True)


def table_back(n, smalls, table_sum):
    by_place = []
    for h in range(n.heads):
        wide = jnp.concatenate([table_sum[h], jnp.zeros((n.seq, n.seq), F32)], axis=1)
        turned = pltpu.roll(wide, n.seq + 1, 1, stride=1, stride_axis=0)
        by_place.append(jnp.sum(turned, axis=0, keepdims=True))
    by_place = jnp.concatenate(by_place, axis=0)
    smalls[12 : 12 + n.heads, : n.buckets] = dot_nt(by_place, place_buckets(n), lax.Precision.HIGHEST)


def inputs_back(n, w, right, resid, dx):
    width, tiles = n.width, n.width // TILE

    @pl.loop(0, tiles, unroll=True)
    def _(t):
        total = resid[:, cols(t)]
        for i, matrix in enumerate((w.query, w.key, w.value)):
            total = total + dot_nt(right[:, i * width : (i + 1) * width], matrix[cols(t), :])
        dx[:, cols(t)] = total.astype(BF16)


def tiles_of(n, core):
    tiles, groups = n.width // TILE, n.hidden // n.width
    down = groups * tiles // 2

    def ffn(i):
        is_down = i < down
        up = i - down
        left = jnp.where(is_down, 3 * tiles + core * down + i, 2 * tiles + up % tiles)
        return left, jnp.where(is_down, 4 + groups, 4 + core * (groups // 2) + up // tiles)

    def attention(i):
        group = i // tiles
        return i % tiles + jnp.where(core * group == 1, tiles, 0), 2 * core + group

    return (ffn, 2 * down), (attention, 2 * tiles)


def weight_grads(n, of, count, first, left, right, packed):
    per = TILE // packed.shape[2] // packed.shape[1]
    by = math.gcd(count, UNROLL)

    @pl.loop(0, count // by)
    def _(outside):
        for inside in range(by):
            i = outside * by + inside
            left_tile, group = of(i)
            rhs = right[:, pl.ds(pl.multiple_of(group * n.width, n.width), n.width)]
            product = dot_tn(left[:, cols(left_tile)], rhs).astype(BF16)
            packed[pl.ds(first + i * per, per)] = product.reshape((per,) + packed.shape[1:])


class Landing(NamedTuple):
    from_y: Any
    end_b: Any
    end_a: Any
    mid_a: Any
    mid_b: Any
    rung_b: Any


class Arrival(NamedTuple):
    y: Any
    end_b: Any
    end_a: Any
    mid_a: Any
    mid_b: Any
    rung: Any
    own_a: Any
    own_b: Any
    end_final: Any
    y_final: Any
    mid_final: Any
    end_both: Any
    sibling: Any
    back: Any


class Place(NamedTuple):
    core: Any
    y: Any
    mine: Any
    other: Any
    is_end: Any
    is_mid: Any
    sibling: Any
    y_peer: Any
    z_in: Any
    z_out: Any
    z_mid: Any
    across: Any
    doubling: Any


def find_place():
    pipe, index = lax.axis_index("pipe"), lax.axis_index("dp")
    base, local = index // 16 * 16, index % 16
    z, y, core = local // 4, local // 2 % 2, local % 2

    def at(zz, yy, cc):
        return (pipe, base + zz * 4 + yy * 2 + cc)

    return Place(
        core,
        y,
        z + 1,
        4 - z,
        (z == 0) | (z == 3),
        (z == 1) | (z == 2),
        at(z, y, 1 - core),
        at(z, 1 - y, core),
        at(jnp.where(z == 0, 1, 2), y, core),
        at(jnp.where(z == 1, 0, 3), y, core),
        at(3 - z, y, core),
        (1 - pipe, index),
        [(pipe, base + jnp.bitwise_xor(local, 1 << j)) for j in range(4)],
    )


def greet_all(me):
    barrier = pltpu.get_barrier_semaphore()
    for device in me.doubling + [me.across]:
        pl.semaphore_signal(barrier, inc=1, device_id=device, device_id_type=MESH)

    @pl.when(me.is_mid)
    def _():
        pl.semaphore_signal(barrier, inc=1, device_id=me.z_mid, device_id_type=MESH)


def all_here(me):
    barrier = pltpu.get_barrier_semaphore()
    pl.when(me.is_mid)(lambda: pl.semaphore_wait(barrier, 6))
    pl.when(me.is_end)(lambda: pl.semaphore_wait(barrier, 5))


def remote(src, dst, send, recv, device):
    return pltpu.make_async_remote_copy(src_ref=src, dst_ref=dst, send_sem=send, recv_sem=recv, device_id=device, device_id_type=MESH)


def wait_for(ref, sem):
    pltpu.make_async_copy(ref, ref, sem).wait()


def added(a, b):
    return (a.astype(F32) + b.astype(F32)).astype(BF16)


def sums(me, first, last, borrowed, packed, out, land, sem, send, lent_sem):
    steps = packed.shape[0] - LENT
    own = jnp.where(first, steps - LENT, steps + LENT)
    lent = remote(packed.at[pl.ds(steps - LENT, LENT)], packed.at[pl.ds(borrowed, LENT)], lent_sem.at[0], lent_sem.at[1], me.across)
    c, y, mine, other = me.core, me.y, me.mine, me.other
    both = pl.ds(2, 2)

    def is_lent(k):
        return last & (k >= borrowed) & (k < borrowed + LENT)

    def row(k):
        moved = jnp.where(k < borrowed + LENT, steps + k - borrowed, k - LENT)
        return jnp.where(last & (k >= borrowed), moved, k)

    def s0(k):
        pl.when(last & (k == borrowed))(lent.wait_recv)
        remote(packed.at[k, 1 - y], land.from_y.at[k], send.at[0], sem.y.at[jnp.bitwise_and(k, RING - 1)], me.y_peer).start()

        @pl.when(me.is_end)
        def _():
            remote(packed.at[k, both], land.end_b.at[k], send.at[1], sem.end_b.at[jnp.bitwise_and(k, RING - 1)], me.z_in).start()

    def s1(k):
        wait_for(land.from_y.at[k], sem.y.at[jnp.bitwise_and(k, RING - 1)])
        packed[k, y] = added(packed[k, y], land.from_y[k])

        @pl.when(me.is_end)
        def _():
            remote(packed.at[k, y], land.end_a.at[k], send.at[2], sem.end_a.at[jnp.bitwise_and(k, RING - 1)], me.z_in).start()

        @pl.when(me.is_mid)
        def _():
            wait_for(land.end_b.at[k], sem.end_b.at[jnp.bitwise_and(k, RING - 1)])
            packed[k, both] = added(packed[k, both], land.end_b[k])
            remote(packed.at[k, other], land.mid_b.at[k], send.at[3], sem.mid_b.at[jnp.bitwise_and(k, RING - 1)], me.z_mid).start()

    def s2(k):
        @pl.when(me.is_mid)
        def _():
            wait_for(land.end_a.at[k], sem.end_a.at[jnp.bitwise_and(k, RING - 1)])
            packed[k, y] = added(packed[k, y], land.end_a[k])
            remote(packed.at[k, y], land.mid_a.at[k], send.at[4], sem.mid_a.at[jnp.bitwise_and(k, RING - 1)], me.z_mid).start()
            wait_for(land.mid_b.at[k], sem.mid_b.at[jnp.bitwise_and(k, RING - 1)])
            packed[k, mine] = added(packed[k, mine], land.mid_b[k])
            remote(packed.at[k, mine], land.rung_b.at[k], send.at[5], sem.rung.at[jnp.bitwise_and(k, RING - 1)], me.y_peer).start()

    def s3(k):
        o = row(k)
        @pl.when(me.is_mid)
        def _():
            wait_for(land.mid_a.at[k], sem.mid_a.at[jnp.bitwise_and(k, RING - 1)])
            total = land.from_y.at[k]
            total[...] = added(packed[k, y], land.mid_a[k])
            remote(total, out.at[c, o, y], send.at[6], sem.end_final.at[jnp.bitwise_and(k, RING - 1)], me.z_out).start()
            remote(total, out.at[c, o, y], send.at[7], sem.y_final.at[jnp.bitwise_and(k, RING - 1)], me.y_peer).start()
            pltpu.make_async_copy(total, out.at[c, o, y], sem.own_a.at[jnp.bitwise_and(k, RING - 1)]).start()
            wait_for(land.rung_b.at[k], sem.rung.at[jnp.bitwise_and(k, RING - 1)])
            total = land.end_a.at[k]
            total[...] = added(packed[k, mine], land.rung_b[k])
            remote(total, out.at[c, o, mine], send.at[8], sem.mid_final.at[jnp.bitwise_and(k, RING - 1)], me.z_mid).start()
            pltpu.make_async_copy(total, out.at[c, o, mine], sem.own_b.at[jnp.bitwise_and(k, RING - 1)]).start()

    def s4(k):
        o = row(k)
        @pl.when(me.is_end)
        def _():
            wait_for(out.at[c, o, y], sem.end_final.at[jnp.bitwise_and(k, RING - 1)])
            remote(out.at[c, o, y], out.at[c, o, y], send.at[7], sem.y_final.at[jnp.bitwise_and(k, RING - 1)], me.y_peer).start()

        @pl.when(me.is_mid)
        def _():
            wait_for(out.at[c, o, other], sem.mid_final.at[jnp.bitwise_and(k, RING - 1)])
            wait_for(out.at[c, o, mine], sem.own_b.at[jnp.bitwise_and(k, RING - 1)])
            remote(out.at[c, o, both], out.at[c, o, both], send.at[9], sem.end_both.at[jnp.bitwise_and(k, RING - 1)], me.z_out).start()

    def s5(k):
        o = row(k)
        @pl.when(k < own)
        def _():
            wait_for(out.at[c, o, 1 - y], sem.y_final.at[jnp.bitwise_and(k, RING - 1)])

            @pl.when(me.is_end)
            def _():
                wait_for(out.at[c, o, both], sem.end_both.at[jnp.bitwise_and(k, RING - 1)])

            @pl.when(me.is_mid)
            def _():
                wait_for(out.at[c, o, y], sem.own_a.at[jnp.bitwise_and(k, RING - 1)])

        @pl.when(k >= own)
        def _():
            wait_for(out.at[c, o], sem.back.at[jnp.bitwise_and(k, RING - 1)])

        @pl.when(jnp.logical_not(is_lent(k)))
        def _():
            remote(out.at[c, o], out.at[c, o], send.at[10], sem.sibling.at[jnp.bitwise_and(k, RING - 1)], me.sibling).start()

        @pl.when(is_lent(k))
        def _():
            home = k - borrowed + steps - LENT
            remote(out.at[c, o], out.at[c, home], send.at[11], sem.back.at[jnp.bitwise_and(home, RING - 1)], me.across).start()

    def s6(k):
        o = row(k)

        @pl.when(jnp.logical_not(is_lent(k)))
        def _():
            wait_for(out.at[1 - c, o], sem.sibling.at[jnp.bitwise_and(k, RING - 1)])

    stages = (s0, s1, s2, s3, s4, s5, s6)
    everything = jnp.where(first, steps, steps + LENT)
    limits = (own,) * 5 + (everything,) * 2

    def slot(t):
        for i, stage in enumerate(stages):
            k = t - i * LAG

            @pl.when((k >= 0) & (k < limits[i]))
            def _():
                stage(jnp.clip(k, 0, steps + LENT - 1))

    def all_sent(count):
        section, sections = land.from_y.at[pl.ds(0, count)], land.end_b.at[pl.ds(0, count)]
        wait_for(section, send.at[0])
        wait_for(section, send.at[7])

        @pl.when(me.is_end)
        def _():
            wait_for(sections, send.at[1])
            wait_for(section, send.at[2])

        @pl.when(me.is_mid)
        def _():
            for which in (3, 4, 5, 6, 8):
                wait_for(section, send.at[which])
            wait_for(sections, send.at[9])

    def finish():
        wait_for(packed.at[pl.ds(0, steps)], send.at[10])

        @pl.when(first)
        def _():
            all_sent(steps - LENT)
            lent.wait_send()

        @pl.when(last)
        def _():
            all_sent(steps + LENT)
            wait_for(packed.at[pl.ds(steps, LENT)], send.at[11])

    return slot, steps + LENT + (len(stages) - 1) * LAG, lent.start, finish


def small_sums(me, smalls, held, total, recv, send):
    def source(j):
        return smalls if j == 0 else held.at[1, j - 1]

    def copy(j):
        return remote(source(j), held.at[0, j], send.at[j], recv.at[j], me.doubling[j])

    def step(j):
        if j >= 0:
            copy(j).wait()
            summed = source(j)[...] + held[0, j]
            if j == 3:
                total[...] = summed
            else:
                held[1, j] = summed
        if j < 3:
            copy(j + 1).start()

    return step


def copies_of(pairs, sems):
    return [pltpu.make_async_copy(src, dst, sems.at[i]) for i, (src, dst) in enumerate(pairs)]


def bucket_rows(n, content, query, wide):
    pairs = []
    for b in range(n.micro):
        pairs.append((content.at[0, pl.ds(b * n.seq, n.seq)], wide.at[pl.ds(b * n.block, n.seq)]))
        pairs.append((query.at[0, pl.ds(b * n.query, n.query)], wide.at[pl.ds(b * n.block + n.seq, n.query)]))
    return pairs


def whole_kernel(n, *refs):
    content, query, *refs = refs
    w_hbm, refs = Weights(*refs[:6]), refs[6:]
    v, refs = Vectors(*refs[:12]), refs[12:]
    content_out, query_out, out, total, *refs = refs
    w, refs = Weights(*refs[:6]), refs[6:]
    left, right, y, dx, dy, resid, table_sum, chosen, smalls, held, packed, *refs = refs
    s, refs = State(left.at[pl.ds(0, n.rows)], *refs[:7]), refs[7:]
    land, refs = Landing(*refs[:6]), refs[6:]
    arrive, refs = Arrival(*refs[:14]), refs[14:]
    w_sem, in_sem, grad_sem, out_sem, pipe_send, pipe_recv, core_send, core_recv, small_send, small_recv, sum_send, lent_sem = refs
    width, rows = n.width, n.rows
    inputs = s.left.at[:, pl.ds(0, width)]
    mine_right = right.at[pl.ds(0, rows)]
    groups = n.hidden // width
    first, last = lax.axis_index("pipe") == 0, lax.axis_index("pipe") == 1
    me = find_place()

    weights = copies_of([(a.at[0], b) for a, b in zip(w_hbm, w)], w_sem)
    own_rows = copies_of(bucket_rows(n, content, query, inputs), in_sem)
    own_grads = copies_of(bucket_rows(n, content, query, dy), in_sem)

    @pl.when(first)
    def _():
        for cp in own_rows:
            cp.start()

    @pl.when(last)
    def _():
        for cp in own_grads:
            cp.start()

    greet_all(me)
    for cp in weights[:3]:
        cp.start()
    bias_and_mask(n, v, s.probs)
    for cp in weights[3:]:
        cp.start()
    hand_down = remote(dx, dy, pipe_send.at[n.micro], pipe_recv.at[n.micro], me.across)

    def hand_up(b):
        return remote(y.at[block_rows(n, b)], inputs.at[block_rows(n, b)], pipe_send.at[b], pipe_recv.at[b], me.across)


    def to_core(which, src, dst):
        return remote(src, dst, core_send.at[which], core_recv.at[which], me.sibling)

    def left_copy(which, at, size):
        return to_core(which, left.at[pl.ds(0, rows), pl.ds(at, size)], left.at[pl.ds(rows, rows), pl.ds(at, size)])

    def right_copy(which, at, size):
        return to_core(which, right.at[pl.ds(0, rows), pl.ds(at, size)], right.at[pl.ds(rows, rows), pl.ds(at, size)])

    share_left = left_copy(0, 0, 3 * width + n.hidden)
    share_attention = right_copy(1, 0, 3 * width)
    share_da = right_copy(2, 3 * width, width)
    share_df = right_copy(3, (4 + groups) * width, width)

    def share_dz(group):
        return right_copy(4 + group, pl.multiple_of((4 + group) * width, width), width)

    @pl.loop(0, n.micro)
    def _(b):
        @pl.when(first & (b == 0))
        def _():
            for cp in own_rows:
                cp.wait()

        @pl.when(last)
        def _():
            hand_up(b).wait_recv()

        def at_first(i):
            pl.when(b == 0)(weights[i].wait)

        project(n, b, at_first, w, v, s)
        attend(n, b, s)
        at_first(3)
        attend_out(n, b, w, v, s, resid)
        attend_norm(n, b, v, s, resid, y)
        at_first(4)
        go_up(n, b, w, v, s, y)
        at_first(5)
        go_down(n, b, w, v, s, resid)
        ffn_norm(n, b, v, s, resid, y)

        pl.when(b == 0)(lambda: all_here(me))

        @pl.when(first)
        def _():
            hand_up(b).start()

    share_left.start()
    results = copies_of([(b, a) for a, b in bucket_rows(n, content_out, query_out, y)], out_sem)
    results_back = copies_of([(b, a) for a, b in bucket_rows(n, content_out, query_out, dx)], out_sem)

    @pl.when(last)
    def _():
        for cp in results:
            cp.start()
        for cp in own_grads:
            cp.wait()

    @pl.when(first)
    def _():
        for b in range(n.micro):
            hand_up(b).wait_send()
        hand_down.wait_recv()

    borrowed = n.hidden // (4 * CHUNK)
    slot, slots, lend, finish = sums(me, first, last, borrowed, packed, out, land, arrive, sum_send, lent_sem)
    (ffn, ffn_count), (attention, attention_count) = tiles_of(n, me.core)
    ffn_norm_back(n, v, s, dy, mine_right, smalls, resid, dx)
    share_df.start()
    down_back(n, w, s, mine_right, smalls, dx, lambda group: share_dz(group).start())
    up_back(n, w, dy, mine_right, resid)

    def ffn_grads():
        share_left.wait_recv()
        share_df.wait_recv()
        for group in range(groups):
            share_dz(group).wait_recv()
        weight_grads(n, ffn, ffn_count, 0, left, right, packed)

    pl.when(first)(ffn_grads)
    attend_norm_back(n, v, s, dy, mine_right, smalls, resid)
    share_da.start()
    out_back(n, w, dy, mine_right)
    early = n.micro * EARLY

    def between(b):
        @pl.when(first)
        def _():
            @pl.loop(0, EARLY)
            def _(i):
                slot(b * EARLY + i)

    attend_back(n, v, s, dy, mine_right, smalls, table_sum, chosen, between)
    share_attention.start()
    inputs_back(n, w, mine_right, resid, dx)

    @pl.when(last)
    def _():
        hand_down.start()

    table_back(n, smalls, table_sum)
    small_step = small_sums(me, smalls, held, total, small_recv, small_send)
    small_step(-1)

    @pl.when(first)
    def _():
        for cp in results_back:
            cp.start()

    pl.when(last)(ffn_grads)
    share_attention.wait_recv()
    share_da.wait_recv()
    weight_grads(n, attention, attention_count, borrowed + jnp.where(last, LENT, 0), left, right, packed)
    pl.when(first)(lend)
    start = jnp.where(first, early, 0)

    @pl.loop(0, slots - start)
    def _(i):
        slot(start + i)
        for j in range(4):
            pl.when(i == 3 * (j + 1))(functools.partial(small_step, j))

    finish()
    for which in [share_left, share_attention, share_da, share_df] + [share_dz(group) for group in range(groups)]:
        which.wait_send()
    for cp in results:
        cp.wait()

    @pl.when(last)
    def _():
        hand_down.wait_send()


def shaped(shape, dtype=BF16):
    return jax.ShapeDtypeStruct(shape, dtype)


def run_layers(n, content, query, w, v):
    rows, width = n.rows, n.width
    vmem, smem, anywhere = (pl.BlockSpec(memory_space=space) for space in (pltpu.VMEM, pltpu.SMEM, pl.ANY))
    dma = pltpu.SemaphoreType.DMA
    steps = (4 * width + 2 * n.hidden) // (2 * 4 * CHUNK)
    chunks = steps + LENT
    half = (chunks, 4, CHUNK, width)
    section, sections = pltpu.VMEM((chunks, CHUNK, width), BF16), pltpu.VMEM((chunks, 2, CHUNK, width), BF16)
    small_shape = (24, width)
    left, *others = state_shapes(n)
    scratch = [pltpu.VMEM(m.shape[1:], BF16) for m in w]
    scratch += [
        pltpu.VMEM((2 * rows, left[0][1]), BF16),
        pltpu.VMEM((2 * rows, 5 * width + n.hidden), BF16),
        pltpu.VMEM((rows, width), BF16),
        pltpu.VMEM((rows, width), BF16),
        pltpu.VMEM((rows, width), BF16),
        pltpu.VMEM((rows, width), F32),
        pltpu.VMEM((n.heads, n.seq, n.seq), F32),
        pltpu.VMEM((n.micro, n.seq, n.block), BF16),
        pltpu.VMEM(small_shape, F32),
        pltpu.VMEM((2, 4) + small_shape, F32),
        pltpu.VMEM(half, BF16),
    ]
    scratch += [pltpu.VMEM(shape, dtype) for shape, dtype in others]
    scratch += [section, sections, section, section, section, section]
    scratch += [dma((RING,))] * 14
    shares = 4 + n.hidden // width
    scratch += [dma((6,)), dma((2 * n.micro,)), dma((2 * n.micro,)), dma((2 * n.micro,)), dma((n.micro + 1,)), dma((n.micro + 1,)), dma((shares,)), dma((shares,)), dma((4,)), dma((4,)), dma((12,)), dma((2,))]
    return pl.pallas_call(
        functools.partial(whole_kernel, n),
        out_shape=[shaped(content.shape), shaped(query.shape), shaped((2,) + half), shaped(small_shape, F32)],
        in_specs=[anywhere] * 8 + [vmem] * 10 + [smem, vmem],
        out_specs=[anywhere] * 3 + [vmem],
        scratch_shapes=scratch,
        compiler_params=pltpu.CompilerParams(collective_id=1, has_side_effects=True, vmem_limit_bytes=VMEM_LIMIT),
    )(content, query, *w, *v)


def unpack_kernel(n, packed, smalls, *refs):
    grads, refs = Weights(*(ref.at[0] for ref in refs[:6])), refs[6:]
    vectors, table, (block, wide, in_sem, out_sem) = refs[:9], refs[9], refs[10:]
    width = n.width
    groups = n.hidden // width
    places = []
    for core in range(2):
        places += [grads.down.at[pl.ds((core * groups // 2 + i) * width, width)] for i in range(groups // 2)]
        places += [grads.up.at[:, pl.ds((core * groups // 2 + i) * width, width)] for i in range(groups // 2)]
        places += [grads.value, grads.out] if core else [grads.query, grads.key]
    count, steps = block.shape[:2]
    loads = [pltpu.make_async_copy(packed.at[i // (count // 2), pl.ds(i % (count // 2) * steps, steps)], block.at[i], in_sem.at[i]) for i in range(count)]
    stores = [pltpu.make_async_copy(wide.at[i], place, out_sem.at[i]) for i, place in enumerate(places)]
    for cp in loads:
        cp.start()
    for i, vector in enumerate(vectors):
        for part in range(vector.shape[1] // width):
            at = part + (i if i <= 5 else i + 3)
            vector[:, part * width : (part + 1) * width] = smalls[at : at + 1, :]
    for h in range(n.heads):
        table[h] = smalls[12 + h : 13 + h, : n.buckets]
    rows = block.shape[2] * block.shape[3]
    for i in range(count):
        loads[i].wait()

        @pl.loop(0, steps)
        def _(step):
            wide[i, pl.ds(pl.multiple_of(step * rows, rows), rows), :] = block[i, step].astype(F32).reshape(rows, width)

        stores[i].start()
    for cp in stores:
        cp.wait()


def unpack(n, packed, smalls):
    width, hidden = n.width, n.hidden
    square, vector = (1, width, width), (1, width)
    matrices = [square] * 4 + [(1, width, hidden), (1, hidden, width)]
    vectors = [vector] * 5 + [(1, hidden)] + [vector] * 3
    vmem, anywhere = pl.BlockSpec(memory_space=pltpu.VMEM), pl.BlockSpec(memory_space=pl.ANY)
    count = 4 + 2 * hidden // width
    steps = 2 * (packed.shape[1] - LENT) // count
    *made, table = pl.pallas_call(
        functools.partial(unpack_kernel, n),
        out_shape=[shaped(shape, F32) for shape in matrices + vectors + [(n.heads, 1, n.buckets)]],
        in_specs=[anywhere, vmem],
        out_specs=[anywhere] * 6 + [vmem] * 10,
        scratch_shapes=[
            pltpu.VMEM((count, steps) + packed.shape[2:], packed.dtype),
            pltpu.VMEM((count, width, width), F32),
            pltpu.SemaphoreType.DMA((count,)),
            pltpu.SemaphoreType.DMA((count,)),
        ],
        compiler_params=pltpu.CompilerParams(vmem_limit_bytes=VMEM_LIMIT),
    )(packed, smalls)
    return made[:6], made[6:] + [jnp.transpose(table, (1, 2, 0))]


def across_blocks(packed, smalls):
    blocks = lax.axis_size("dp") // 16
    if blocks > 1:
        groups = [[block * 16 + i for block in range(blocks)] for i in range(16)]
        packed = lax.psum(packed.astype(F32), "dp", axis_index_groups=groups)
        smalls = lax.psum(smalls, "dp", axis_index_groups=groups)
    return packed, smalls


def on_device(content_ends, query_ends, w_query, b_query, w_key, w_value, b_value, w_out, b_out, gain_attn, shift_attn, w_up, b_up, w_down, b_down, gain_ffn, shift_ffn, rel_table, doc_lengths, position_order):
    micro, seq = position_order.shape
    n = Sizes(micro, seq, query_ends.shape[1] // micro, content_ends.shape[2], rel_table.shape[2], w_up.shape[2], rel_table.shape[1])
    w = Weights(w_query, w_key, w_value, w_out, w_up, w_down)
    v = Vectors(b_query, b_value, b_out, gain_attn, shift_attn, b_up, b_down, gain_ffn, shift_ffn, jnp.transpose(rel_table, (2, 0, 1)), doc_lengths, position_order)
    content_out, query_out, packed, smalls = run_layers(n, content_ends, query_ends, w, v)
    packed, smalls = across_blocks(packed, smalls)
    g, d = unpack(n, packed, smalls)
    return content_out, query_out, g[0], d[0], g[1], g[2], d[1], g[3], d[2], d[3], d[4], g[4], d[5], g[5], d[6], d[7], d[8], d[9]


def solution(mesh):
    rows, matrix, vector, buckets = P("pipe", "dp", None), P("pipe", None, None), P("pipe", None), P("dp", None)
    grads = (matrix, vector, matrix, matrix, vector, matrix, vector, vector, vector, matrix, vector, matrix, vector, vector, vector, matrix)
    return jax.shard_map(on_device, mesh=mesh, in_specs=(rows, rows, *grads, buckets, buckets), out_specs=(rows, rows, *grads), check_vma=False)
```

```python
import functools
import math
from typing import Any, NamedTuple

import jax
import jax.numpy as jnp
from jax import lax
from jax.experimental import pallas as pl
from jax.experimental.pallas import tpu as pltpu
from jax.sharding import PartitionSpec as P

MESH = pl.DeviceIdType.MESH
F32 = jnp.float32
BF16 = jnp.bfloat16
NORM_EPS = 1e-05
NEG_FILL = -1e30
THRESHOLDS = (12, 16, 23, 32, 46, 64, 91)
TILE = 256
LANES = 128
UNROLL = 3
AHEAD = 4
EARLY = 3
BESIDE = 1
OFFSETS = (0, 3, 6, 8, 10, 13, 16)
RING = 16
LENT = 8
CHUNK = 16
VMEM_LIMIT = 63 * 2**20


class Sizes(NamedTuple):
    micro: int
    seq: int
    query: int
    width: int
    heads: int
    hidden: int
    buckets: int

    @property
    def block(self):
        return self.seq + self.query

    @property
    def rows(self):
        return self.micro * self.block

    @property
    def pairs(self):
        return self.width // LANES


class Weights(NamedTuple):
    query: Any
    key: Any
    value: Any
    out: Any
    up: Any
    down: Any


class Vectors(NamedTuple):
    b_query: Any
    b_value: Any
    b_out: Any
    gain_attn: Any
    shift_attn: Any
    b_up: Any
    b_down: Any
    gain_ffn: Any
    shift_ffn: Any
    rel_table: Any
    lengths: Any
    order: Any


class State(NamedTuple):
    left: Any
    qkv: Any
    slope: Any
    probs: Any
    norm_attn: Any
    norm_ffn: Any
    spread_attn: Any
    spread_ffn: Any


def state_shapes(n):
    return State(
        ((n.rows, 3 * n.width + n.hidden), BF16),
        ((n.rows, 3 * n.width), BF16),
        ((n.rows, n.hidden), BF16),
        ((n.micro * n.pairs, 2 * n.block, n.seq), F32),
        ((n.rows, n.width), F32),
        ((n.rows, n.width), F32),
        ((n.rows, 1), F32),
        ((n.rows, 1), F32),
    )


def dot(a, b):
    return jnp.dot(a, b, preferred_element_type=F32)


def dot_nt(a, b, precision=None):
    return lax.dot_general(a, b, (((1,), (1,)), ((), ())), precision=precision, preferred_element_type=F32)


def dot_tn(a, b):
    return lax.dot_general(a, b, (((0,), (0,)), ((), ())), preferred_element_type=F32)


def iota(shape, dim):
    return lax.broadcasted_iota(jnp.int32, shape, dim)


def cols(at, size=TILE):
    return pl.ds(pl.multiple_of(at * size, size), size)


def bucket_of(offset):
    distance = jnp.abs(offset)
    bucket = jnp.minimum(distance, 8) + jnp.where(offset < 0, 16, 0)
    for bound_at in THRESHOLDS:
        bucket = bucket + jnp.where(distance >= bound_at, 1, 0)
    return bucket


def place_buckets(n):
    shape = (n.buckets, 2 * n.seq)
    at = iota(shape, 1)
    offset = jnp.where(at < n.seq, -at, 2 * n.seq - at)
    return jnp.where(bucket_of(offset) == iota(shape, 0), 1.0, 0.0)


def to_column(row, n):
    shape = (n.seq, n.seq)
    return jnp.sum(jnp.where(iota(shape, 0) == iota(shape, 1), row, 0.0), axis=1, keepdims=True)


def bias_and_mask(n, v, bias):
    seq, query = n.seq, n.query
    by_head = jnp.concatenate([v.rel_table[h] for h in range(n.heads)], axis=0)
    base = jnp.dot(by_head, place_buckets(n), precision=lax.Precision.HIGHEST, preferred_element_type=F32)
    square = (seq, seq)
    row_at, col_at = iota(square, 0).astype(F32), iota(square, 1).astype(F32)
    visible_from = float(seq - query)
    content_sees, query_sees, chosen = [], [], []
    for b in range(n.micro):
        order_row = v.order[b : b + 1, :].astype(F32)
        order_col = to_column(order_row, n)
        rank_row = jnp.sum(jnp.where(order_col == col_at, row_at, 0.0), axis=0, keepdims=True)
        rank_col = to_column(rank_row, n)
        ends, total = [], jnp.int32(0)
        for d in range(v.lengths.shape[1]):
            total = total + v.lengths[b, d]
            ends.append(total)

        def doc_of(at):
            found = jnp.zeros(at.shape, F32)
            for end in ends:
                found = found + jnp.where(at >= end.astype(F32), 1.0, 0.0)
            return found

        doc_row = doc_of(iota((1, seq), 1).astype(F32))
        doc_col = doc_of(iota((seq, 1), 0).astype(F32))
        unmasked = rank_row < visible_from
        content_sees.append((doc_col == doc_row) & (unmasked | (rank_row <= rank_col)))
        place = order_col[seq - query :]
        at_place = place == iota((query, seq), 1).astype(F32)
        rank = visible_from + iota((query, 1), 0).astype(F32)
        query_sees.append((doc_of(place) == doc_row) & (unmasked | (rank_row < rank) | at_place))
        chosen.append(jnp.where(at_place, 1.0, 0.0).astype(BF16))
    for h in range(n.heads):
        spread = jnp.broadcast_to(base[h : h + 1, :], (seq, 2 * seq))
        table = pltpu.roll(spread, 0, 1, stride=1, stride_axis=0)[:, :seq]
        high = table.astype(BF16)
        rest = table - high.astype(F32)
        middle = rest.astype(BF16)
        low = (rest - middle.astype(F32)).astype(BF16)
        for b in range(n.micro):
            of_query = dot(chosen[b], high) + dot(chosen[b], middle) + dot(chosen[b], low)
            start = (h % 2) * n.block
            bias[b * n.pairs + h // 2, start : start + seq, :] = jnp.where(content_sees[b], table, NEG_FILL)
            bias[b * n.pairs + h // 2, start + seq : start + n.block, :] = jnp.where(query_sees[b], of_query, NEG_FILL)


def half_masks():
    at = iota((1, LANES), 1)
    return jnp.where(at < LANES // 2, 1.0, 0.0).astype(BF16), jnp.where(at < LANES // 2, 0.0, 1.0).astype(BF16)


def both_heads(values):
    first, second = half_masks()
    return jnp.concatenate([values * first, values * second], axis=0)


def side_by_side(stacked):
    half = stacked.shape[0] // 2
    return jnp.concatenate([stacked[:half], stacked[half:]], axis=1)


def block_rows(n, b):
    return pl.ds(pl.multiple_of(b * n.block, 16), n.block)


def norm_rows(n, b, summed, normed_ref, spread_ref, gain, shift, write):
    step = n.block // 3
    for at in range(0, n.block, step):
        rows = pl.ds(pl.multiple_of(b * n.block + at, 16), step)
        r = summed[rows, :]
        centered = r - jnp.mean(r, axis=1, keepdims=True)
        spread = lax.rsqrt(jnp.mean(centered * centered, axis=1, keepdims=True) + NORM_EPS)
        normed = centered * spread
        normed_ref[rows, :] = normed
        spread_ref[rows, :] = spread
        write(rows, (normed * gain + shift).astype(BF16))


def norm_back(n, grad_of, normed_ref, spread_ref, gain, write):
    step = n.block // 3

    def body(i, sums):
        rows = pl.ds(pl.multiple_of(i * step, step), step)
        grad = grad_of(rows)
        normed = normed_ref[rows, :]
        scaled = grad * gain
        inner = jnp.mean(scaled * normed, axis=1, keepdims=True)
        back = spread_ref[rows, :] * (scaled - jnp.mean(scaled, axis=1, keepdims=True) - normed * inner)
        write(rows, back)
        low = back.astype(BF16).astype(F32)
        return (
            sums[0] + jnp.sum(grad * normed, axis=0, keepdims=True),
            sums[1] + jnp.sum(grad, axis=0, keepdims=True),
            sums[2] + jnp.sum(low, axis=0, keepdims=True),
        )

    zero = jnp.zeros((1, n.width), F32)
    return lax.fori_loop(0, n.rows // step, body, (zero, zero, zero), unroll=3)


def project(n, b, ready, w, v, s):
    width, tiles = n.width, n.width // TILE
    rows = block_rows(n, b)
    for i, matrix in enumerate((w.query, w.key, w.value)):
        ready(i)
        for t in range(tiles):
            at = slice(t * TILE, (t + 1) * TILE)
            product = dot(s.left[rows, :width], matrix[:, at])
            if i == 0:
                product = product + v.b_query[:, at]
            if i == 2:
                product = product + v.b_value[:, at]
            s.qkv[rows, i * width + t * TILE : i * width + (t + 1) * TILE] = product.astype(BF16)


def attend(n, b, s):
    factor = (LANES // 2) ** -0.5
    rows, keys = block_rows(n, b), pl.ds(pl.multiple_of(b * n.block, 16), n.seq)
    for pair in range(n.pairs):
        it = b * n.pairs + pair

        def lanes(part):
            return slice((part * n.pairs + pair) * LANES, (part * n.pairs + pair + 1) * LANES)

        q = both_heads(s.qkv[rows, lanes(0)])
        val = both_heads(s.qkv[keys, lanes(2)])
        scores = dot_nt(q, s.qkv[keys, lanes(1)]) * factor + s.probs[it]
        powers = jnp.exp(scores - jnp.max(scores, axis=1, keepdims=True))
        probs = powers / jnp.sum(powers, axis=1, keepdims=True)
        s.probs[it] = probs
        s.left[rows, lanes(1)] = dot(side_by_side(probs.astype(BF16)), val).astype(BF16)


def attend_out(n, b, w, v, s, summed):
    width = n.width
    rows = block_rows(n, b)
    for t in range(width // TILE):
        at = slice(t * TILE, (t + 1) * TILE)
        product = dot(s.left[rows, width : 2 * width], w.out[:, at])
        summed[rows, at] = s.left[rows, at].astype(F32) + product + v.b_out[:, at]


def attend_norm(n, b, v, s, summed, copy):
    width = n.width

    def keep_h1(rows, value):
        s.left[rows, 2 * width : 3 * width] = value
        copy[rows, :] = value

    norm_rows(n, b, summed, s.norm_attn, s.spread_attn, v.gain_attn[...], v.shift_attn[...], keep_h1)


def go_up(n, b, w, v, s, h1):
    width, tiles, left_u = n.width, n.width // TILE, 3 * (n.width // TILE)
    step = n.block // 3
    c = (2 / math.pi) ** 0.5
    staged = s.norm_ffn

    def bend(t, i):
        for at in range(0, n.block, step):
            rows = pl.ds(pl.multiple_of(b * n.block + at, 16), step)
            z = staged[rows, i * TILE : (i + 1) * TILE] + v.b_up[:, cols(t)]
            square = z * z
            half = 0.5 + 0.5 * jnp.tanh(z * (c + 0.044715 * c * square))
            value = z * half
            s.left[rows, cols(left_u + t)] = value.astype(BF16)
            s.slope[rows, cols(t)] = (half + value * (1.0 - half) * (2.0 * c + 0.26829 * c * square)).astype(BF16)

    @pl.loop(0, n.hidden // width, unroll=True)
    def _(group):
        for i in range(tiles):
            staged[block_rows(n, b), i * TILE : (i + 1) * TILE] = dot(h1[block_rows(n, b), :], w.up[:, cols(group * tiles + i)])
            if i:
                bend(group * tiles + i - 1, i - 1)
        bend(group * tiles + tiles - 1, tiles - 1)


def go_down(n, b, w, v, s, summed):
    width = n.width
    rows = block_rows(n, b)
    for t in range(width // TILE):
        at = slice(t * TILE, (t + 1) * TILE)
        h1_at = slice(2 * width + t * TILE, 2 * width + (t + 1) * TILE)
        product = dot(s.left[rows, 3 * width :], w.down[:, at])
        summed[rows, at] = s.left[rows, h1_at].astype(F32) + product + v.b_down[:, at]


def ffn_norm(n, b, v, s, summed, y):
    def keep_y(rows, value):
        y[rows, :] = value

    norm_rows(n, b, summed, s.norm_ffn, s.spread_ffn, v.gain_ffn[...], v.shift_ffn[...], keep_y)


def ffn_norm_back(n, v, s, dy, right, smalls, resid, copy):
    width = n.width
    df_cols = slice(4 * width + n.hidden, 5 * width + n.hidden)

    def keep_df(rows, value):
        resid[rows, :] = value
        right[rows, df_cols] = copy[rows, :] = value.astype(BF16)

    gain, shift, low = norm_back(n, lambda rows: dy[rows, :].astype(F32), s.norm_ffn, s.spread_ffn, v.gain_ffn[...], keep_df)
    smalls[10:11, :], smalls[11:12, :], smalls[9:10, :] = gain, shift, low


def down_back(n, w, s, right, smalls, df, sent):
    width, tiles = n.width, n.width // TILE
    step = n.block // 3
    staged = s.norm_ffn

    def bend(group, i):
        t = group * tiles + i
        total = jnp.zeros((8, TILE), F32)
        for at in range(0, n.rows, step):
            rows = slice(at, at + step)
            dz = (staged[rows, i * TILE : (i + 1) * TILE] * s.slope[rows, cols(t)].astype(F32)).astype(BF16)
            right[rows, cols(4 * tiles + t)] = dz
            total = total + jnp.sum(dz.astype(F32).reshape(step // 8, 8, TILE), axis=0)
        smalls[pl.ds(5 + group, 1), cols(i)] = jnp.sum(total, axis=0, keepdims=True)

    @pl.loop(0, n.hidden // width, unroll=True)
    def _(group):
        for i in range(tiles):
            staged[:, i * TILE : (i + 1) * TILE] = dot_nt(df[...], w.down[cols(group * tiles + i), :])
            if i:
                bend(group, i - 1)
        bend(group, tiles - 1)
        sent(group)


def up_back(n, w, dy, right, resid):
    width, tiles = n.width, n.width // TILE

    @pl.loop(0, tiles, unroll=True)
    def _(t):
        spread = dot_nt(right[:, 4 * width : 4 * width + n.hidden], w.up[cols(t), :])
        dy[:, cols(t)] = (spread + resid[:, cols(t)]).astype(BF16)


def attend_norm_back(n, v, s, dy, right, smalls, resid):
    width = n.width

    def keep_da(rows, value):
        resid[rows, :] = value
        right[rows, 3 * width : 4 * width] = value.astype(BF16)

    gain, shift, low = norm_back(n, lambda rows: dy[rows, :].astype(F32), s.norm_attn, s.spread_attn, v.gain_attn[...], keep_da)
    smalls[3:4, :], smalls[4:5, :], smalls[2:3, :] = gain, shift, low


def out_back(n, w, dy, right):
    width, tiles = n.width, n.width // TILE

    @pl.loop(0, tiles, unroll=True)
    def _(t):
        dy[:, cols(t)] = dot_nt(right[:, 3 * width : 4 * width], w.out[cols(t), :]).astype(BF16)


def attend_back(n, v, s, dy, right, smalls, table_sum, chosen, between):
    width = n.width
    factor = (LANES // 2) ** -0.5
    table_sum[...] = jnp.zeros(table_sum.shape, F32)
    square = (n.seq, n.seq)
    same = jnp.where(iota(square, 0) + iota(square, 1) == n.seq - 1, 1.0, 0.0).astype(BF16)
    for b in range(n.micro):
        place = v.order[b : b + 1, n.seq - n.query :]
        chosen[b, :, : n.seq] = same
        chosen[b, :, n.seq :] = jnp.where(place == n.seq - 1 - iota((n.seq, n.query), 0), 1.0, 0.0).astype(BF16)

    @pl.loop(0, n.micro)
    def _(b):
        start = b * n.block
        rows, keys = block_rows(n, b), pl.ds(pl.multiple_of(start, 16), n.seq)
        rest = pl.ds(pl.multiple_of(start + n.seq, 16), n.query)
        for pair in range(n.pairs):
            q_at, k_at, v_at = (slice((part * n.pairs + pair) * LANES, (part * n.pairs + pair + 1) * LANES) for part in range(3))
            grad = both_heads(dy[rows, q_at])
            q = both_heads(s.qkv[rows, q_at])
            k = both_heads(s.qkv[keys, k_at])
            val = s.qkv[keys, v_at]
            probs = s.probs[b * n.pairs + pair]
            grad_probs = dot_nt(grad, val)
            inner = jnp.sum(probs * grad_probs, axis=1, keepdims=True)
            grad_scores = (probs * (grad_probs - inner)).astype(BF16)
            beside = side_by_side(grad_scores)
            right[rows, q_at] = (dot(beside, k) * factor).astype(BF16)
            right[keys, k_at] = (dot_tn(grad_scores, q) * factor).astype(BF16)
            right[keys, v_at] = dot_tn(probs.astype(BF16), grad).astype(BF16)
            none = jnp.zeros((n.query, LANES), BF16)
            right[rest, k_at] = none
            right[rest, v_at] = none
            of_heads = dot(chosen[b], beside)
            table_sum[2 * pair] += of_heads[:, : n.seq]
            table_sum[2 * pair + 1] += of_heads[:, n.seq :]
        between(b)

    smalls[0:1, :] = jnp.sum(right[:, :width].astype(F32), axis=0, keepdims=True)
    smalls[1:2, :] = jnp.sum(right[:, 2 * width : 3 * width].astype(F32), axis=0, keepdims=True)


def table_back(n, smalls, table_sum):
    by_place = []
    for h in range(n.heads):
        wide = jnp.concatenate([table_sum[h], jnp.zeros((n.seq, n.seq), F32)], axis=1)
        turned = pltpu.roll(wide, n.seq + 1, 1, stride=1, stride_axis=0)
        by_place.append(jnp.sum(turned, axis=0, keepdims=True))
    by_place = jnp.concatenate(by_place, axis=0)
    smalls[12 : 12 + n.heads, : n.buckets] = dot_nt(by_place, place_buckets(n), lax.Precision.HIGHEST)


def inputs_back(n, w, right, resid, dx):
    width, tiles = n.width, n.width // TILE

    @pl.loop(0, tiles, unroll=True)
    def _(t):
        total = resid[:, cols(t)]
        for i, matrix in enumerate((w.query, w.key, w.value)):
            total = total + dot_nt(right[:, i * width : (i + 1) * width], matrix[cols(t), :])
        dx[:, cols(t)] = total.astype(BF16)


def tiles_of(n, core):
    tiles, groups = n.width // TILE, n.hidden // n.width
    down = groups * tiles // 2

    def ffn(i):
        is_down = i < down
        up = i - down
        left = jnp.where(is_down, 3 * tiles + core * down + i, 2 * tiles + up % tiles)
        return left, jnp.where(is_down, 4 + groups, 4 + core * (groups // 2) + up // tiles)

    def attention(i):
        group = i // tiles
        return i % tiles + jnp.where(core * group == 1, tiles, 0), 2 * core + group

    return (ffn, 2 * down), (attention, 2 * tiles)


def weight_grads(n, of, count, first, left, right, packed, between):
    per = TILE // packed.shape[2] // packed.shape[1]
    by = math.gcd(count, UNROLL)

    @pl.loop(0, count // by)
    def _(outside):
        for inside in range(by):
            i = outside * by + inside
            left_tile, group = of(i)
            rhs = right[:, pl.ds(pl.multiple_of(group * n.width, n.width), n.width)]
            product = dot_tn(left[:, cols(left_tile)], rhs).astype(BF16)
            packed[pl.ds(first + i * per, per)] = product.reshape((per,) + packed.shape[1:])
        between(outside)


class Landing(NamedTuple):
    from_y: Any
    end_b: Any
    end_a: Any
    mid_a: Any
    mid_b: Any
    rung_b: Any


class Arrival(NamedTuple):
    y: Any
    end_b: Any
    end_a: Any
    mid_a: Any
    mid_b: Any
    rung: Any
    own_a: Any
    own_b: Any
    end_final: Any
    y_final: Any
    mid_final: Any
    end_both: Any
    sibling: Any
    back: Any


class Place(NamedTuple):
    core: Any
    y: Any
    mine: Any
    other: Any
    is_end: Any
    is_mid: Any
    sibling: Any
    y_peer: Any
    z_in: Any
    z_out: Any
    z_mid: Any
    across: Any
    doubling: Any


def find_place():
    pipe, index = lax.axis_index("pipe"), lax.axis_index("dp")
    base, local = index // 16 * 16, index % 16
    z, y, core = local // 4, local // 2 % 2, local % 2

    def at(zz, yy, cc):
        return (pipe, base + zz * 4 + yy * 2 + cc)

    return Place(
        core,
        y,
        z + 1,
        4 - z,
        (z == 0) | (z == 3),
        (z == 1) | (z == 2),
        at(z, y, 1 - core),
        at(z, 1 - y, core),
        at(jnp.where(z == 0, 1, 2), y, core),
        at(jnp.where(z == 1, 0, 3), y, core),
        at(3 - z, y, core),
        (1 - pipe, index),
        [(pipe, base + jnp.bitwise_xor(local, 1 << j)) for j in range(4)],
    )


def greet_all(me):
    barrier = pltpu.get_barrier_semaphore()
    for device in me.doubling + [me.across]:
        pl.semaphore_signal(barrier, inc=1, device_id=device, device_id_type=MESH)

    @pl.when(me.is_mid)
    def _():
        pl.semaphore_signal(barrier, inc=1, device_id=me.z_mid, device_id_type=MESH)


def all_here(me):
    barrier = pltpu.get_barrier_semaphore()
    pl.when(me.is_mid)(lambda: pl.semaphore_wait(barrier, 6))
    pl.when(me.is_end)(lambda: pl.semaphore_wait(barrier, 5))


def remote(src, dst, send, recv, device):
    return pltpu.make_async_remote_copy(src_ref=src, dst_ref=dst, send_sem=send, recv_sem=recv, device_id=device, device_id_type=MESH)


def wait_for(ref, sem):
    pltpu.make_async_copy(ref, ref, sem).wait()


def added(a, b):
    return (a.astype(F32) + b.astype(F32)).astype(BF16)


def sums(me, first, last, borrowed, packed, out, land, sem, send, lent_sem):
    steps = packed.shape[0] - LENT
    own = jnp.where(first, steps - LENT, steps + LENT)
    lent = remote(packed.at[pl.ds(steps - LENT, LENT)], packed.at[pl.ds(borrowed, LENT)], lent_sem.at[0], lent_sem.at[1], me.across)
    c, y, mine, other = me.core, me.y, me.mine, me.other
    both = pl.ds(2, 2)

    def is_lent(k):
        return last & (k >= borrowed) & (k < borrowed + LENT)

    def row(k):
        moved = jnp.where(k < borrowed + LENT, steps + k - borrowed, k - LENT)
        return jnp.where(last & (k >= borrowed), moved, k)

    def s0(k):
        pl.when(last & (k == borrowed))(lent.wait_recv)
        remote(packed.at[k, 1 - y], land.from_y.at[k], send.at[0], sem.y.at[jnp.bitwise_and(k, RING - 1)], me.y_peer).start()

        @pl.when(me.is_end)
        def _():
            remote(packed.at[k, both], land.end_b.at[k], send.at[1], sem.end_b.at[jnp.bitwise_and(k, RING - 1)], me.z_in).start()

    def s1(k):
        wait_for(land.from_y.at[k], sem.y.at[jnp.bitwise_and(k, RING - 1)])
        packed[k, y] = added(packed[k, y], land.from_y[k])

        @pl.when(me.is_end)
        def _():
            remote(packed.at[k, y], land.end_a.at[k], send.at[2], sem.end_a.at[jnp.bitwise_and(k, RING - 1)], me.z_in).start()

        @pl.when(me.is_mid)
        def _():
            wait_for(land.end_b.at[k], sem.end_b.at[jnp.bitwise_and(k, RING - 1)])
            packed[k, both] = added(packed[k, both], land.end_b[k])
            remote(packed.at[k, other], land.mid_b.at[k], send.at[3], sem.mid_b.at[jnp.bitwise_and(k, RING - 1)], me.z_mid).start()

    def s2(k):
        @pl.when(me.is_mid)
        def _():
            wait_for(land.end_a.at[k], sem.end_a.at[jnp.bitwise_and(k, RING - 1)])
            packed[k, y] = added(packed[k, y], land.end_a[k])
            remote(packed.at[k, y], land.mid_a.at[k], send.at[4], sem.mid_a.at[jnp.bitwise_and(k, RING - 1)], me.z_mid).start()
            wait_for(land.mid_b.at[k], sem.mid_b.at[jnp.bitwise_and(k, RING - 1)])
            packed[k, mine] = added(packed[k, mine], land.mid_b[k])
            remote(packed.at[k, mine], land.rung_b.at[k], send.at[5], sem.rung.at[jnp.bitwise_and(k, RING - 1)], me.y_peer).start()

    def s3(k):
        o = row(k)
        @pl.when(me.is_mid)
        def _():
            wait_for(land.mid_a.at[k], sem.mid_a.at[jnp.bitwise_and(k, RING - 1)])
            total = land.from_y.at[k]
            total[...] = added(packed[k, y], land.mid_a[k])
            remote(total, out.at[c, o, y], send.at[6], sem.end_final.at[jnp.bitwise_and(k, RING - 1)], me.z_out).start()
            remote(total, out.at[c, o, y], send.at[7], sem.y_final.at[jnp.bitwise_and(k, RING - 1)], me.y_peer).start()
            pltpu.make_async_copy(total, out.at[c, o, y], sem.own_a.at[jnp.bitwise_and(k, RING - 1)]).start()
            wait_for(land.rung_b.at[k], sem.rung.at[jnp.bitwise_and(k, RING - 1)])
            total = land.end_a.at[k]
            total[...] = added(packed[k, mine], land.rung_b[k])
            remote(total, out.at[c, o, mine], send.at[8], sem.mid_final.at[jnp.bitwise_and(k, RING - 1)], me.z_mid).start()
            pltpu.make_async_copy(total, out.at[c, o, mine], sem.own_b.at[jnp.bitwise_and(k, RING - 1)]).start()

    def s4(k):
        o = row(k)
        @pl.when(me.is_end)
        def _():
            wait_for(out.at[c, o, y], sem.end_final.at[jnp.bitwise_and(k, RING - 1)])
            remote(out.at[c, o, y], out.at[c, o, y], send.at[7], sem.y_final.at[jnp.bitwise_and(k, RING - 1)], me.y_peer).start()

        @pl.when(me.is_mid)
        def _():
            wait_for(out.at[c, o, other], sem.mid_final.at[jnp.bitwise_and(k, RING - 1)])
            wait_for(out.at[c, o, mine], sem.own_b.at[jnp.bitwise_and(k, RING - 1)])
            remote(out.at[c, o, both], out.at[c, o, both], send.at[9], sem.end_both.at[jnp.bitwise_and(k, RING - 1)], me.z_out).start()

    def s5(k):
        o = row(k)
        @pl.when(k < own)
        def _():
            wait_for(out.at[c, o, 1 - y], sem.y_final.at[jnp.bitwise_and(k, RING - 1)])

            @pl.when(me.is_end)
            def _():
                wait_for(out.at[c, o, both], sem.end_both.at[jnp.bitwise_and(k, RING - 1)])

            @pl.when(me.is_mid)
            def _():
                wait_for(out.at[c, o, y], sem.own_a.at[jnp.bitwise_and(k, RING - 1)])

        @pl.when(k >= own)
        def _():
            wait_for(out.at[c, o], sem.back.at[jnp.bitwise_and(k, RING - 1)])

        @pl.when(jnp.logical_not(is_lent(k)))
        def _():
            remote(out.at[c, o], out.at[c, o], send.at[10], sem.sibling.at[jnp.bitwise_and(k, RING - 1)], me.sibling).start()

        @pl.when(is_lent(k))
        def _():
            home = k - borrowed + steps - LENT
            remote(out.at[c, o], out.at[c, home], send.at[11], sem.back.at[jnp.bitwise_and(home, RING - 1)], me.across).start()

    def s6(k):
        o = row(k)

        @pl.when(jnp.logical_not(is_lent(k)))
        def _():
            wait_for(out.at[1 - c, o], sem.sibling.at[jnp.bitwise_and(k, RING - 1)])

    stages = (s0, s1, s2, s3, s4, s5, s6)
    everything = jnp.where(first, steps, steps + LENT)
    limits = (own,) * 5 + (everything,) * 2

    def slot(t):
        for i, stage in enumerate(stages):
            k = t - OFFSETS[i]

            @pl.when((k >= 0) & (k < limits[i]))
            def _():
                stage(jnp.clip(k, 0, steps + LENT - 1))

    def all_sent(count):
        section, sections = land.from_y.at[pl.ds(0, count)], land.end_b.at[pl.ds(0, count)]
        wait_for(section, send.at[0])
        wait_for(section, send.at[7])

        @pl.when(me.is_end)
        def _():
            wait_for(sections, send.at[1])
            wait_for(section, send.at[2])

        @pl.when(me.is_mid)
        def _():
            for which in (3, 4, 5, 6, 8):
                wait_for(section, send.at[which])
            wait_for(sections, send.at[9])

    def finish():
        wait_for(packed.at[pl.ds(0, steps)], send.at[10])

        @pl.when(first)
        def _():
            all_sent(steps - LENT)
            lent.wait_send()

        @pl.when(last)
        def _():
            all_sent(steps + LENT)
            wait_for(packed.at[pl.ds(steps, LENT)], send.at[11])

    return slot, steps + LENT + OFFSETS[-1], lent.start, finish


def small_sums(me, smalls, held, total, recv, send):
    def source(j):
        return smalls if j == 0 else held.at[1, j - 1]

    def copy(j):
        return remote(source(j), held.at[0, j], send.at[j], recv.at[j], me.doubling[j])

    def step(j):
        if j >= 0:
            copy(j).wait()
            summed = source(j)[...] + held[0, j]
            if j == 3:
                total[...] = summed
            else:
                held[1, j] = summed
        if j < 3:
            copy(j + 1).start()

    return step


def copies_of(pairs, sems):
    return [pltpu.make_async_copy(src, dst, sems.at[i]) for i, (src, dst) in enumerate(pairs)]


def bucket_rows(n, content, query, wide):
    pairs = []
    for b in range(n.micro):
        pairs.append((content.at[0, pl.ds(b * n.seq, n.seq)], wide.at[pl.ds(b * n.block, n.seq)]))
        pairs.append((query.at[0, pl.ds(b * n.query, n.query)], wide.at[pl.ds(b * n.block + n.seq, n.query)]))
    return pairs


def whole_kernel(n, *refs):
    content, query, *refs = refs
    w_hbm, refs = Weights(*refs[:6]), refs[6:]
    v, refs = Vectors(*refs[:12]), refs[12:]
    content_out, query_out, out, total, *refs = refs
    w, refs = Weights(*refs[:6]), refs[6:]
    left, right, y, dx, dy, resid, table_sum, chosen, smalls, held, packed, *refs = refs
    s, refs = State(left.at[pl.ds(0, n.rows)], *refs[:7]), refs[7:]
    land, refs = Landing(*refs[:6]), refs[6:]
    arrive, refs = Arrival(*refs[:14]), refs[14:]
    w_sem, in_sem, grad_sem, out_sem, pipe_send, pipe_recv, core_send, core_recv, small_send, small_recv, sum_send, lent_sem = refs
    width, rows = n.width, n.rows
    inputs = s.left.at[:, pl.ds(0, width)]
    mine_right = right.at[pl.ds(0, rows)]
    groups = n.hidden // width
    first, last = lax.axis_index("pipe") == 0, lax.axis_index("pipe") == 1
    me = find_place()

    weights = copies_of([(a.at[0], b) for a, b in zip(w_hbm, w)], w_sem)
    own_rows = copies_of(bucket_rows(n, content, query, inputs), in_sem)
    own_grads = copies_of(bucket_rows(n, content, query, dy), in_sem)

    @pl.when(first)
    def _():
        for cp in own_rows:
            cp.start()

    @pl.when(last)
    def _():
        for cp in own_grads:
            cp.start()

    greet_all(me)
    for cp in weights[:3]:
        cp.start()
    bias_and_mask(n, v, s.probs)
    for cp in weights[3:]:
        cp.start()
    hand_down = remote(dx, dy, pipe_send.at[n.micro], pipe_recv.at[n.micro], me.across)

    def hand_up(b):
        return remote(y.at[block_rows(n, b)], inputs.at[block_rows(n, b)], pipe_send.at[b], pipe_recv.at[b], me.across)


    def to_core(which, src, dst):
        return remote(src, dst, core_send.at[which], core_recv.at[which], me.sibling)

    def left_copy(which, at, size):
        return to_core(which, left.at[pl.ds(0, rows), pl.ds(at, size)], left.at[pl.ds(rows, rows), pl.ds(at, size)])

    def right_copy(which, at, size):
        return to_core(which, right.at[pl.ds(0, rows), pl.ds(at, size)], right.at[pl.ds(rows, rows), pl.ds(at, size)])

    share_left = left_copy(0, 0, 3 * width + n.hidden)
    share_attention = right_copy(1, 0, 3 * width)
    share_da = right_copy(2, 3 * width, width)
    share_df = right_copy(3, (4 + groups) * width, width)

    def share_dz(group):
        return right_copy(4 + group, pl.multiple_of((4 + group) * width, width), width)

    @pl.loop(0, n.micro)
    def _(b):
        @pl.when(first & (b == 0))
        def _():
            for cp in own_rows:
                cp.wait()

        @pl.when(last)
        def _():
            hand_up(b).wait_recv()

        def at_first(i):
            pl.when(b == 0)(weights[i].wait)

        project(n, b, at_first, w, v, s)
        attend(n, b, s)
        at_first(3)
        attend_out(n, b, w, v, s, resid)
        attend_norm(n, b, v, s, resid, y)
        at_first(4)
        go_up(n, b, w, v, s, y)
        at_first(5)
        go_down(n, b, w, v, s, resid)
        ffn_norm(n, b, v, s, resid, y)

        pl.when(b == 0)(lambda: all_here(me))

        @pl.when(first)
        def _():
            hand_up(b).start()

    share_left.start()
    results = copies_of([(b, a) for a, b in bucket_rows(n, content_out, query_out, y)], out_sem)
    results_back = copies_of([(b, a) for a, b in bucket_rows(n, content_out, query_out, dx)], out_sem)

    @pl.when(last)
    def _():
        for cp in results:
            cp.start()
        for cp in own_grads:
            cp.wait()

    @pl.when(first)
    def _():
        for b in range(n.micro):
            hand_up(b).wait_send()
        hand_down.wait_recv()

    borrowed = n.hidden // (4 * CHUNK)
    slot, slots, lend, finish = sums(me, first, last, borrowed, packed, out, land, arrive, sum_send, lent_sem)
    (ffn, ffn_count), (attention, attention_count) = tiles_of(n, me.core)
    ffn_norm_back(n, v, s, dy, mine_right, smalls, resid, dx)
    share_df.start()
    down_back(n, w, s, mine_right, smalls, dx, lambda group: share_dz(group).start())
    up_back(n, w, dy, mine_right, resid)

    ffn_steps, attention_steps = (count // math.gcd(count, UNROLL) for count in (ffn_count, attention_count))
    at_attend = ffn_steps * BESIDE
    at_attention = at_attend + jnp.where(first, n.micro * EARLY, 0)
    start = at_attention + attention_steps * BESIDE

    def some_slots(at, count):
        @pl.loop(0, count)
        def _(i):
            slot(at + i)

    def after_ffn(outside):
        some_slots(outside * BESIDE, BESIDE)

    def after_attention(outside):
        some_slots(at_attention + outside * BESIDE, BESIDE)

    def ffn_grads():
        share_left.wait_recv()
        share_df.wait_recv()
        for group in range(groups):
            share_dz(group).wait_recv()
        weight_grads(n, ffn, ffn_count, 0, left, right, packed, after_ffn)

    pl.when(first)(ffn_grads)
    attend_norm_back(n, v, s, dy, mine_right, smalls, resid)
    share_da.start()
    out_back(n, w, dy, mine_right)
    def between(b):
        @pl.when(first)
        def _():
            some_slots(at_attend + b * EARLY, EARLY)

    attend_back(n, v, s, dy, mine_right, smalls, table_sum, chosen, between)
    share_attention.start()
    inputs_back(n, w, mine_right, resid, dx)

    @pl.when(last)
    def _():
        hand_down.start()

    small_step = small_sums(me, smalls, held, total, small_recv, small_send)

    @pl.when(first)
    def _():
        for cp in results_back:
            cp.start()

    pl.when(last)(ffn_grads)
    share_attention.wait_recv()
    share_da.wait_recv()
    weight_grads(n, attention, attention_count, borrowed + jnp.where(last, LENT, 0), left, right, packed, after_attention)
    pl.when(first)(lend)
    table_back(n, smalls, table_sum)
    small_step(-1)

    @pl.loop(0, slots - start)
    def _(i):
        slot(start + i)
        for j in range(4):
            pl.when(i == 3 * (j + 1))(functools.partial(small_step, j))

    finish()
    for which in [share_left, share_attention, share_da, share_df] + [share_dz(group) for group in range(groups)]:
        which.wait_send()
    for cp in results:
        cp.wait()

    @pl.when(last)
    def _():
        hand_down.wait_send()


def shaped(shape, dtype=BF16):
    return jax.ShapeDtypeStruct(shape, dtype)


def run_layers(n, content, query, w, v):
    rows, width = n.rows, n.width
    vmem, smem, anywhere = (pl.BlockSpec(memory_space=space) for space in (pltpu.VMEM, pltpu.SMEM, pl.ANY))
    dma = pltpu.SemaphoreType.DMA
    steps = (4 * width + 2 * n.hidden) // (2 * 4 * CHUNK)
    chunks = steps + LENT
    half = (chunks, 4, CHUNK, width)
    section, sections = pltpu.VMEM((chunks, CHUNK, width), BF16), pltpu.VMEM((chunks, 2, CHUNK, width), BF16)
    small_shape = (24, width)
    left, *others = state_shapes(n)
    scratch = [pltpu.VMEM(m.shape[1:], BF16) for m in w]
    scratch += [
        pltpu.VMEM((2 * rows, left[0][1]), BF16),
        pltpu.VMEM((2 * rows, 5 * width + n.hidden), BF16),
        pltpu.VMEM((rows, width), BF16),
        pltpu.VMEM((rows, width), BF16),
        pltpu.VMEM((rows, width), BF16),
        pltpu.VMEM((rows, width), F32),
        pltpu.VMEM((n.heads, n.seq, n.seq), F32),
        pltpu.VMEM((n.micro, n.seq, n.block), BF16),
        pltpu.VMEM(small_shape, F32),
        pltpu.VMEM((2, 4) + small_shape, F32),
        pltpu.VMEM(half, BF16),
    ]
    scratch += [pltpu.VMEM(shape, dtype) for shape, dtype in others]
    scratch += [section, sections, section, section, section, section]
    scratch += [dma((RING,))] * 14
    shares = 4 + n.hidden // width
    scratch += [dma((6,)), dma((2 * n.micro,)), dma((2 * n.micro,)), dma((2 * n.micro,)), dma((n.micro + 1,)), dma((n.micro + 1,)), dma((shares,)), dma((shares,)), dma((4,)), dma((4,)), dma((12,)), dma((2,))]
    return pl.pallas_call(
        functools.partial(whole_kernel, n),
        out_shape=[shaped(content.shape), shaped(query.shape), shaped((2,) + half), shaped(small_shape, F32)],
        in_specs=[anywhere] * 8 + [vmem] * 10 + [smem, vmem],
        out_specs=[anywhere] * 3 + [vmem],
        scratch_shapes=scratch,
        compiler_params=pltpu.CompilerParams(collective_id=1, has_side_effects=True, vmem_limit_bytes=VMEM_LIMIT),
    )(content, query, *w, *v)


def unpack_kernel(n, packed, smalls, content, query, *refs):
    (content_out, query_out), refs = refs[:2], refs[2:]
    grads, refs = Weights(*(ref.at[0] for ref in refs[:6])), refs[6:]
    vectors, table, (block, wide, in_sem, out_sem, row_sem, held_content, held_query) = refs[:9], refs[9], refs[10:]
    width = n.width
    groups = n.hidden // width
    places = []
    for core in range(2):
        places += [grads.down.at[pl.ds((core * groups // 2 + i) * width, width)] for i in range(groups // 2)]
        places += [grads.up.at[:, pl.ds((core * groups // 2 + i) * width, width)] for i in range(groups // 2)]
        places += [grads.value, grads.out] if core else [grads.query, grads.key]
    count, steps = block.shape[:2]
    loads = [pltpu.make_async_copy(packed.at[i // (count // 2), pl.ds(i % (count // 2) * steps, steps)], block.at[i], in_sem.at[i]) for i in range(count)]
    stores = [pltpu.make_async_copy(wide.at[i], place, out_sem.at[i]) for i, place in enumerate(places)]
    rows_in = copies_of([(content, held_content), (query, held_query)], row_sem)
    rows_back = copies_of([(held_content, content_out), (held_query, query_out)], row_sem)
    for cp in rows_in:
        cp.start()
    for cp in loads[:AHEAD]:
        cp.start()
    for i, vector in enumerate(vectors):
        for part in range(vector.shape[1] // width):
            at = part + (i if i <= 5 else i + 3)
            vector[:, part * width : (part + 1) * width] = smalls[at : at + 1, :]
    for h in range(n.heads):
        table[h] = smalls[12 + h : 13 + h, : n.buckets]
    rows = block.shape[2] * block.shape[3]
    for i in range(count):
        loads[i].wait()
        if i + AHEAD < count:
            loads[i + AHEAD].start()

        @pl.loop(0, steps)
        def _(step):
            wide[i, pl.ds(pl.multiple_of(step * rows, rows), rows), :] = block[i, step].astype(F32).reshape(rows, width)

        stores[i].start()
        if i == 0:
            for back, cp in zip(rows_back, rows_in):
                cp.wait()
                back.start()
    for cp in stores + rows_back:
        cp.wait()


def unpack(n, packed, smalls, content, query):
    width, hidden = n.width, n.hidden
    square, vector = (1, width, width), (1, width)
    matrices = [square] * 4 + [(1, width, hidden), (1, hidden, width)]
    vectors = [vector] * 5 + [(1, hidden)] + [vector] * 3
    vmem, anywhere = pl.BlockSpec(memory_space=pltpu.VMEM), pl.BlockSpec(memory_space=pl.ANY)
    count = 4 + 2 * hidden // width
    steps = 2 * (packed.shape[1] - LENT) // count
    content, query, *made, table = pl.pallas_call(
        functools.partial(unpack_kernel, n),
        out_shape=[shaped(content.shape), shaped(query.shape)] + [shaped(shape, F32) for shape in matrices + vectors + [(n.heads, 1, n.buckets)]],
        in_specs=[anywhere, vmem, anywhere, anywhere],
        out_specs=[anywhere] * 8 + [vmem] * 10,
        scratch_shapes=[
            pltpu.VMEM((count, steps) + packed.shape[2:], packed.dtype),
            pltpu.VMEM((count, width, width), F32),
            pltpu.SemaphoreType.DMA((count,)),
            pltpu.SemaphoreType.DMA((count,)),
            pltpu.SemaphoreType.DMA((2,)),
            pltpu.VMEM(content.shape, BF16),
            pltpu.VMEM(query.shape, BF16),
        ],
        compiler_params=pltpu.CompilerParams(vmem_limit_bytes=VMEM_LIMIT),
    )(packed, smalls, content, query)
    return content, query, made[:6], made[6:] + [jnp.transpose(table, (1, 2, 0))]


def across_blocks(packed, smalls):
    blocks = lax.axis_size("dp") // 16
    if blocks > 1:
        groups = [[block * 16 + i for block in range(blocks)] for i in range(16)]
        packed = lax.psum(packed.astype(F32), "dp", axis_index_groups=groups)
        smalls = lax.psum(smalls, "dp", axis_index_groups=groups)
    return packed, smalls


def on_device(content_ends, query_ends, w_query, b_query, w_key, w_value, b_value, w_out, b_out, gain_attn, shift_attn, w_up, b_up, w_down, b_down, gain_ffn, shift_ffn, rel_table, doc_lengths, position_order):
    micro, seq = position_order.shape
    n = Sizes(micro, seq, query_ends.shape[1] // micro, content_ends.shape[2], rel_table.shape[2], w_up.shape[2], rel_table.shape[1])
    w = Weights(w_query, w_key, w_value, w_out, w_up, w_down)
    v = Vectors(b_query, b_value, b_out, gain_attn, shift_attn, b_up, b_down, gain_ffn, shift_ffn, jnp.transpose(rel_table, (2, 0, 1)), doc_lengths, position_order)
    content_out, query_out, packed, smalls = run_layers(n, content_ends, query_ends, w, v)
    packed, smalls = across_blocks(packed, smalls)
    content_out, query_out, g, d = unpack(n, packed, smalls, content_out, query_out)
    return content_out, query_out, g[0], d[0], g[1], g[2], d[1], g[3], d[2], d[3], d[4], g[4], d[5], g[5], d[6], d[7], d[8], d[9]


def solution(mesh):
    rows, matrix, vector, buckets = P("pipe", "dp", None), P("pipe", None, None), P("pipe", None), P("dp", None)
    grads = (matrix, vector, matrix, matrix, vector, matrix, vector, vector, vector, matrix, vector, matrix, vector, vector, vector, matrix)
    return jax.shard_map(on_device, mesh=mesh, in_specs=(rows, rows, *grads, buckets, buckets), out_specs=(rows, rows, *grads), check_vma=False)
```

```python
import functools
import math
from typing import Any, NamedTuple

import jax
import jax.numpy as jnp
from jax import lax
from jax.experimental import pallas as pl
from jax.experimental.pallas import tpu as pltpu
from jax.sharding import PartitionSpec as P

MESH = pl.DeviceIdType.MESH
F32 = jnp.float32
BF16 = jnp.bfloat16
NORM_EPS = 1e-05
NEG_FILL = -1e30
THRESHOLDS = (12, 16, 23, 32, 46, 64, 91)
TILE = 256
LANES = 128
UNROLL = 1
AHEAD = 4
EARLY = 3
BESIDE = 1
OFFSETS = (0, 3, 6, 8, 10, 13, 16)
RING = 16
LENT = 8
CHUNK = 16
VMEM_LIMIT = 63 * 2**20


class Sizes(NamedTuple):
    micro: int
    seq: int
    query: int
    width: int
    heads: int
    hidden: int
    buckets: int

    @property
    def block(self):
        return self.seq + self.query

    @property
    def rows(self):
        return self.micro * self.block

    @property
    def pairs(self):
        return self.width // LANES


class Weights(NamedTuple):
    query: Any
    key: Any
    value: Any
    out: Any
    up: Any
    down: Any


class Vectors(NamedTuple):
    b_query: Any
    b_value: Any
    b_out: Any
    gain_attn: Any
    shift_attn: Any
    b_up: Any
    b_down: Any
    gain_ffn: Any
    shift_ffn: Any
    rel_table: Any
    lengths: Any
    order: Any


class State(NamedTuple):
    left: Any
    qkv: Any
    slope: Any
    probs: Any
    norm_attn: Any
    norm_ffn: Any
    spread_attn: Any
    spread_ffn: Any


def state_shapes(n):
    return State(
        ((n.rows, 3 * n.width + n.hidden), BF16),
        ((n.rows, 3 * n.width), BF16),
        ((n.rows, n.hidden), BF16),
        ((n.micro * n.pairs, 2 * n.block, n.seq), F32),
        ((n.rows, n.width), F32),
        ((n.rows, n.width), F32),
        ((n.rows, 1), F32),
        ((n.rows, 1), F32),
    )


def dot(a, b):
    return jnp.dot(a, b, preferred_element_type=F32)


def dot_nt(a, b, precision=None):
    return lax.dot_general(a, b, (((1,), (1,)), ((), ())), precision=precision, preferred_element_type=F32)


def dot_tn(a, b):
    return lax.dot_general(a, b, (((0,), (0,)), ((), ())), preferred_element_type=F32)


def iota(shape, dim):
    return lax.broadcasted_iota(jnp.int32, shape, dim)


def cols(at, size=TILE):
    return pl.ds(pl.multiple_of(at * size, size), size)


def bucket_of(offset):
    distance = jnp.abs(offset)
    bucket = jnp.minimum(distance, 8) + jnp.where(offset < 0, 16, 0)
    for bound_at in THRESHOLDS:
        bucket = bucket + jnp.where(distance >= bound_at, 1, 0)
    return bucket


def place_buckets(n):
    shape = (n.buckets, 2 * n.seq)
    at = iota(shape, 1)
    offset = jnp.where(at < n.seq, -at, 2 * n.seq - at)
    return jnp.where(bucket_of(offset) == iota(shape, 0), 1.0, 0.0)


def to_column(row, n):
    shape = (n.seq, n.seq)
    return jnp.sum(jnp.where(iota(shape, 0) == iota(shape, 1), row, 0.0), axis=1, keepdims=True)


def bias_and_mask(n, v, bias):
    seq, query = n.seq, n.query
    by_head = jnp.concatenate([v.rel_table[h] for h in range(n.heads)], axis=0)
    base = jnp.dot(by_head, place_buckets(n), precision=lax.Precision.HIGHEST, preferred_element_type=F32)
    square = (seq, seq)
    row_at, col_at = iota(square, 0).astype(F32), iota(square, 1).astype(F32)
    visible_from = float(seq - query)
    content_sees, query_sees, chosen = [], [], []
    for b in range(n.micro):
        order_row = v.order[b : b + 1, :].astype(F32)
        order_col = to_column(order_row, n)
        rank_row = jnp.sum(jnp.where(order_col == col_at, row_at, 0.0), axis=0, keepdims=True)
        rank_col = to_column(rank_row, n)
        ends, total = [], jnp.int32(0)
        for d in range(v.lengths.shape[1]):
            total = total + v.lengths[b, d]
            ends.append(total)

        def doc_of(at):
            found = jnp.zeros(at.shape, F32)
            for end in ends:
                found = found + jnp.where(at >= end.astype(F32), 1.0, 0.0)
            return found

        doc_row = doc_of(iota((1, seq), 1).astype(F32))
        doc_col = doc_of(iota((seq, 1), 0).astype(F32))
        unmasked = rank_row < visible_from
        content_sees.append((doc_col == doc_row) & (unmasked | (rank_row <= rank_col)))
        place = order_col[seq - query :]
        at_place = place == iota((query, seq), 1).astype(F32)
        rank = visible_from + iota((query, 1), 0).astype(F32)
        query_sees.append((doc_of(place) == doc_row) & (unmasked | (rank_row < rank) | at_place))
        chosen.append(jnp.where(at_place, 1.0, 0.0).astype(BF16))
    for h in range(n.heads):
        spread = jnp.broadcast_to(base[h : h + 1, :], (seq, 2 * seq))
        table = pltpu.roll(spread, 0, 1, stride=1, stride_axis=0)[:, :seq]
        high = table.astype(BF16)
        rest = table - high.astype(F32)
        middle = rest.astype(BF16)
        low = (rest - middle.astype(F32)).astype(BF16)
        for b in range(n.micro):
            of_query = dot(chosen[b], high) + dot(chosen[b], middle) + dot(chosen[b], low)
            start = (h % 2) * n.block
            bias[b * n.pairs + h // 2, start : start + seq, :] = jnp.where(content_sees[b], table, NEG_FILL)
            bias[b * n.pairs + h // 2, start + seq : start + n.block, :] = jnp.where(query_sees[b], of_query, NEG_FILL)


def half_masks():
    at = iota((1, LANES), 1)
    return jnp.where(at < LANES // 2, 1.0, 0.0).astype(BF16), jnp.where(at < LANES // 2, 0.0, 1.0).astype(BF16)


def both_heads(values):
    first, second = half_masks()
    return jnp.concatenate([values * first, values * second], axis=0)


def side_by_side(stacked):
    half = stacked.shape[0] // 2
    return jnp.concatenate([stacked[:half], stacked[half:]], axis=1)


def block_rows(n, b):
    return pl.ds(pl.multiple_of(b * n.block, 16), n.block)


def norm_rows(n, b, summed, normed_ref, spread_ref, gain, shift, write):
    step = n.block // 3
    for at in range(0, n.block, step):
        rows = pl.ds(pl.multiple_of(b * n.block + at, 16), step)
        r = summed[rows, :]
        centered = r - jnp.mean(r, axis=1, keepdims=True)
        spread = lax.rsqrt(jnp.mean(centered * centered, axis=1, keepdims=True) + NORM_EPS)
        normed = centered * spread
        normed_ref[rows, :] = normed
        spread_ref[rows, :] = spread
        write(rows, (normed * gain + shift).astype(BF16))


def norm_back(n, grad_of, normed_ref, spread_ref, gain, write):
    step = n.block // 3

    def body(i, sums):
        rows = pl.ds(pl.multiple_of(i * step, step), step)
        grad = grad_of(rows)
        normed = normed_ref[rows, :]
        scaled = grad * gain
        inner = jnp.mean(scaled * normed, axis=1, keepdims=True)
        back = spread_ref[rows, :] * (scaled - jnp.mean(scaled, axis=1, keepdims=True) - normed * inner)
        write(rows, back)
        low = back.astype(BF16).astype(F32)
        return (
            sums[0] + jnp.sum(grad * normed, axis=0, keepdims=True),
            sums[1] + jnp.sum(grad, axis=0, keepdims=True),
            sums[2] + jnp.sum(low, axis=0, keepdims=True),
        )

    zero = jnp.zeros((1, n.width), F32)
    return lax.fori_loop(0, n.rows // step, body, (zero, zero, zero), unroll=3)


def project(n, b, ready, w, v, s):
    width, tiles = n.width, n.width // TILE
    rows = block_rows(n, b)
    for i, matrix in enumerate((w.query, w.key, w.value)):
        ready(i)
        for t in range(tiles):
            at = slice(t * TILE, (t + 1) * TILE)
            product = dot(s.left[rows, :width], matrix[:, at])
            if i == 0:
                product = product + v.b_query[:, at]
            if i == 2:
                product = product + v.b_value[:, at]
            s.qkv[rows, i * width + t * TILE : i * width + (t + 1) * TILE] = product.astype(BF16)


def attend(n, b, s):
    factor = (LANES // 2) ** -0.5
    rows, keys = block_rows(n, b), pl.ds(pl.multiple_of(b * n.block, 16), n.seq)
    for pair in range(n.pairs):
        it = b * n.pairs + pair

        def lanes(part):
            return slice((part * n.pairs + pair) * LANES, (part * n.pairs + pair + 1) * LANES)

        q = both_heads(s.qkv[rows, lanes(0)])
        val = both_heads(s.qkv[keys, lanes(2)])
        scores = dot_nt(q, s.qkv[keys, lanes(1)]) * factor + s.probs[it]
        powers = jnp.exp(scores - jnp.max(scores, axis=1, keepdims=True))
        probs = powers / jnp.sum(powers, axis=1, keepdims=True)
        s.probs[it] = probs
        s.left[rows, lanes(1)] = dot(side_by_side(probs.astype(BF16)), val).astype(BF16)


def attend_out(n, b, w, v, s, summed):
    width = n.width
    rows = block_rows(n, b)
    for t in range(width // TILE):
        at = slice(t * TILE, (t + 1) * TILE)
        product = dot(s.left[rows, width : 2 * width], w.out[:, at])
        summed[rows, at] = s.left[rows, at].astype(F32) + product + v.b_out[:, at]


def attend_norm(n, b, v, s, summed, copy):
    width = n.width

    def keep_h1(rows, value):
        s.left[rows, 2 * width : 3 * width] = value
        copy[rows, :] = value

    norm_rows(n, b, summed, s.norm_attn, s.spread_attn, v.gain_attn[...], v.shift_attn[...], keep_h1)


def go_up(n, b, w, v, s, h1):
    width, tiles, left_u = n.width, n.width // TILE, 3 * (n.width // TILE)
    step = n.block // 3
    c = (2 / math.pi) ** 0.5
    staged = s.norm_ffn

    def bend(t, i):
        for at in range(0, n.block, step):
            rows = pl.ds(pl.multiple_of(b * n.block + at, 16), step)
            z = staged[rows, i * TILE : (i + 1) * TILE] + v.b_up[:, cols(t)]
            square = z * z
            half = 0.5 + 0.5 * jnp.tanh(z * (c + 0.044715 * c * square))
            value = z * half
            s.left[rows, cols(left_u + t)] = value.astype(BF16)
            s.slope[rows, cols(t)] = (half + value * (1.0 - half) * (2.0 * c + 0.26829 * c * square)).astype(BF16)

    @pl.loop(0, n.hidden // width, unroll=True)
    def _(group):
        for i in range(tiles):
            staged[block_rows(n, b), i * TILE : (i + 1) * TILE] = dot(h1[block_rows(n, b), :], w.up[:, cols(group * tiles + i)])
            if i:
                bend(group * tiles + i - 1, i - 1)
        bend(group * tiles + tiles - 1, tiles - 1)


def go_down(n, b, w, v, s, summed):
    width = n.width
    rows = block_rows(n, b)
    for t in range(width // TILE):
        at = slice(t * TILE, (t + 1) * TILE)
        h1_at = slice(2 * width + t * TILE, 2 * width + (t + 1) * TILE)
        product = dot(s.left[rows, 3 * width :], w.down[:, at])
        summed[rows, at] = s.left[rows, h1_at].astype(F32) + product + v.b_down[:, at]


def ffn_norm(n, b, v, s, summed, y):
    def keep_y(rows, value):
        y[rows, :] = value

    norm_rows(n, b, summed, s.norm_ffn, s.spread_ffn, v.gain_ffn[...], v.shift_ffn[...], keep_y)


def ffn_norm_back(n, v, s, dy, right, smalls, resid, copy):
    width = n.width
    df_cols = slice(4 * width + n.hidden, 5 * width + n.hidden)

    def keep_df(rows, value):
        resid[rows, :] = value
        right[rows, df_cols] = copy[rows, :] = value.astype(BF16)

    gain, shift, low = norm_back(n, lambda rows: dy[rows, :].astype(F32), s.norm_ffn, s.spread_ffn, v.gain_ffn[...], keep_df)
    smalls[10:11, :], smalls[11:12, :], smalls[9:10, :] = gain, shift, low


def down_back(n, w, s, right, smalls, df, sent):
    width, tiles = n.width, n.width // TILE
    step = n.block // 3
    staged = s.norm_ffn

    def bend(group, i):
        t = group * tiles + i
        total = jnp.zeros((8, TILE), F32)
        for at in range(0, n.rows, step):
            rows = slice(at, at + step)
            dz = (staged[rows, i * TILE : (i + 1) * TILE] * s.slope[rows, cols(t)].astype(F32)).astype(BF16)
            right[rows, cols(4 * tiles + t)] = dz
            total = total + jnp.sum(dz.astype(F32).reshape(step // 8, 8, TILE), axis=0)
        smalls[pl.ds(5 + group, 1), cols(i)] = jnp.sum(total, axis=0, keepdims=True)

    @pl.loop(0, n.hidden // width, unroll=True)
    def _(group):
        for i in range(tiles):
            staged[:, i * TILE : (i + 1) * TILE] = dot_nt(df[...], w.down[cols(group * tiles + i), :])
            if i:
                bend(group, i - 1)
        bend(group, tiles - 1)
        sent(group)


def up_back(n, w, dy, right, resid):
    width, tiles = n.width, n.width // TILE

    @pl.loop(0, tiles, unroll=True)
    def _(t):
        spread = dot_nt(right[:, 4 * width : 4 * width + n.hidden], w.up[cols(t), :])
        dy[:, cols(t)] = (spread + resid[:, cols(t)]).astype(BF16)


def attend_norm_back(n, v, s, dy, right, smalls, resid):
    width = n.width

    def keep_da(rows, value):
        resid[rows, :] = value
        right[rows, 3 * width : 4 * width] = value.astype(BF16)

    gain, shift, low = norm_back(n, lambda rows: dy[rows, :].astype(F32), s.norm_attn, s.spread_attn, v.gain_attn[...], keep_da)
    smalls[3:4, :], smalls[4:5, :], smalls[2:3, :] = gain, shift, low


def out_back(n, w, dy, right):
    width, tiles = n.width, n.width // TILE

    @pl.loop(0, tiles, unroll=True)
    def _(t):
        dy[:, cols(t)] = dot_nt(right[:, 3 * width : 4 * width], w.out[cols(t), :]).astype(BF16)


def attend_back(n, v, s, dy, right, smalls, table_sum, chosen, between):
    width = n.width
    factor = (LANES // 2) ** -0.5
    table_sum[...] = jnp.zeros(table_sum.shape, F32)
    square = (n.seq, n.seq)
    same = jnp.where(iota(square, 0) + iota(square, 1) == n.seq - 1, 1.0, 0.0).astype(BF16)
    for b in range(n.micro):
        place = v.order[b : b + 1, n.seq - n.query :]
        chosen[b, :, : n.seq] = same
        chosen[b, :, n.seq :] = jnp.where(place == n.seq - 1 - iota((n.seq, n.query), 0), 1.0, 0.0).astype(BF16)

    @pl.loop(0, n.micro)
    def _(b):
        start = b * n.block
        rows, keys = block_rows(n, b), pl.ds(pl.multiple_of(start, 16), n.seq)
        rest = pl.ds(pl.multiple_of(start + n.seq, 16), n.query)
        for pair in range(n.pairs):
            q_at, k_at, v_at = (slice((part * n.pairs + pair) * LANES, (part * n.pairs + pair + 1) * LANES) for part in range(3))
            grad = both_heads(dy[rows, q_at])
            q = both_heads(s.qkv[rows, q_at])
            k = both_heads(s.qkv[keys, k_at])
            val = s.qkv[keys, v_at]
            probs = s.probs[b * n.pairs + pair]
            grad_probs = dot_nt(grad, val)
            inner = jnp.sum(probs * grad_probs, axis=1, keepdims=True)
            grad_scores = (probs * (grad_probs - inner)).astype(BF16)
            beside = side_by_side(grad_scores)
            right[rows, q_at] = (dot(beside, k) * factor).astype(BF16)
            right[keys, k_at] = (dot_tn(grad_scores, q) * factor).astype(BF16)
            right[keys, v_at] = dot_tn(probs.astype(BF16), grad).astype(BF16)
            none = jnp.zeros((n.query, LANES), BF16)
            right[rest, k_at] = none
            right[rest, v_at] = none
            of_heads = dot(chosen[b], beside)
            table_sum[2 * pair] += of_heads[:, : n.seq]
            table_sum[2 * pair + 1] += of_heads[:, n.seq :]
        between(b)

    smalls[0:1, :] = jnp.sum(right[:, :width].astype(F32), axis=0, keepdims=True)
    smalls[1:2, :] = jnp.sum(right[:, 2 * width : 3 * width].astype(F32), axis=0, keepdims=True)


def table_back(n, smalls, table_sum):
    by_place = []
    for h in range(n.heads):
        wide = jnp.concatenate([table_sum[h], jnp.zeros((n.seq, n.seq), F32)], axis=1)
        turned = pltpu.roll(wide, n.seq + 1, 1, stride=1, stride_axis=0)
        by_place.append(jnp.sum(turned, axis=0, keepdims=True))
    by_place = jnp.concatenate(by_place, axis=0)
    smalls[12 : 12 + n.heads, : n.buckets] = dot_nt(by_place, place_buckets(n), lax.Precision.HIGHEST)


def inputs_back(n, w, right, resid, dx):
    width, tiles = n.width, n.width // TILE

    @pl.loop(0, tiles, unroll=True)
    def _(t):
        total = resid[:, cols(t)]
        for i, matrix in enumerate((w.query, w.key, w.value)):
            total = total + dot_nt(right[:, i * width : (i + 1) * width], matrix[cols(t), :])
        dx[:, cols(t)] = total.astype(BF16)


def tiles_of(n, core):
    tiles, groups = n.width // TILE, n.hidden // n.width
    down = groups * tiles // 2

    def ffn(i):
        is_down = i < down
        up = i - down
        left = jnp.where(is_down, 3 * tiles + core * down + i, 2 * tiles + up % tiles)
        return left, jnp.where(is_down, 4 + groups, 4 + core * (groups // 2) + up // tiles)

    def attention(i):
        group = i // tiles
        return i % tiles + jnp.where(core * group == 1, tiles, 0), 2 * core + group

    return (ffn, 2 * down), (attention, 2 * tiles)


def weight_grads(n, of, count, first, left, right, packed, between):
    per = TILE // packed.shape[2] // packed.shape[1]
    by = math.gcd(count, UNROLL)

    @pl.loop(0, count // by)
    def _(outside):
        for inside in range(by):
            i = outside * by + inside
            left_tile, group = of(i)
            rhs = right[:, pl.ds(pl.multiple_of(group * n.width, n.width), n.width)]
            product = dot_tn(left[:, cols(left_tile)], rhs).astype(BF16)
            packed[pl.ds(first + i * per, per)] = product.reshape((per,) + packed.shape[1:])
        between(outside)


class Landing(NamedTuple):
    from_y: Any
    end_b: Any
    end_a: Any
    mid_a: Any
    mid_b: Any
    rung_b: Any


class Arrival(NamedTuple):
    y: Any
    end_b: Any
    end_a: Any
    mid_a: Any
    mid_b: Any
    rung: Any
    own_a: Any
    own_b: Any
    end_final: Any
    y_final: Any
    mid_final: Any
    end_both: Any
    sibling: Any
    back: Any


class Place(NamedTuple):
    core: Any
    y: Any
    mine: Any
    other: Any
    is_end: Any
    is_mid: Any
    sibling: Any
    y_peer: Any
    z_in: Any
    z_out: Any
    z_mid: Any
    across: Any
    doubling: Any


def find_place():
    pipe, index = lax.axis_index("pipe"), lax.axis_index("dp")
    base, local = index // 16 * 16, index % 16
    z, y, core = local // 4, local // 2 % 2, local % 2

    def at(zz, yy, cc):
        return (pipe, base + zz * 4 + yy * 2 + cc)

    return Place(
        core,
        y,
        z + 1,
        4 - z,
        (z == 0) | (z == 3),
        (z == 1) | (z == 2),
        at(z, y, 1 - core),
        at(z, 1 - y, core),
        at(jnp.where(z == 0, 1, 2), y, core),
        at(jnp.where(z == 1, 0, 3), y, core),
        at(3 - z, y, core),
        (1 - pipe, index),
        [(pipe, base + jnp.bitwise_xor(local, 1 << j)) for j in range(4)],
    )


def greet_all(me):
    barrier = pltpu.get_barrier_semaphore()
    for device in me.doubling + [me.across]:
        pl.semaphore_signal(barrier, inc=1, device_id=device, device_id_type=MESH)

    @pl.when(me.is_mid)
    def _():
        pl.semaphore_signal(barrier, inc=1, device_id=me.z_mid, device_id_type=MESH)


def all_here(me):
    barrier = pltpu.get_barrier_semaphore()
    pl.when(me.is_mid)(lambda: pl.semaphore_wait(barrier, 6))
    pl.when(me.is_end)(lambda: pl.semaphore_wait(barrier, 5))


def remote(src, dst, send, recv, device):
    return pltpu.make_async_remote_copy(src_ref=src, dst_ref=dst, send_sem=send, recv_sem=recv, device_id=device, device_id_type=MESH)


def wait_for(ref, sem):
    pltpu.make_async_copy(ref, ref, sem).wait()


def added(a, b):
    return (a.astype(F32) + b.astype(F32)).astype(BF16)


def sums(me, first, last, borrowed, packed, out, land, sem, send, lent_sem):
    steps = packed.shape[0] - LENT
    own = jnp.where(first, steps - LENT, steps + LENT)
    lent = remote(packed.at[pl.ds(steps - LENT, LENT)], packed.at[pl.ds(borrowed, LENT)], lent_sem.at[0], lent_sem.at[1], me.across)
    c, y, mine, other = me.core, me.y, me.mine, me.other
    both = pl.ds(2, 2)

    def is_lent(k):
        return last & (k >= borrowed) & (k < borrowed + LENT)

    def row(k):
        moved = jnp.where(k < borrowed + LENT, steps + k - borrowed, k - LENT)
        return jnp.where(last & (k >= borrowed), moved, k)

    def s0(k):
        pl.when(last & (k == borrowed))(lent.wait_recv)
        remote(packed.at[k, 1 - y], land.from_y.at[k], send.at[0], sem.y.at[jnp.bitwise_and(k, RING - 1)], me.y_peer).start()

        @pl.when(me.is_end)
        def _():
            remote(packed.at[k, both], land.end_b.at[k], send.at[1], sem.end_b.at[jnp.bitwise_and(k, RING - 1)], me.z_in).start()

    def s1(k):
        wait_for(land.from_y.at[k], sem.y.at[jnp.bitwise_and(k, RING - 1)])
        packed[k, y] = added(packed[k, y], land.from_y[k])

        @pl.when(me.is_end)
        def _():
            remote(packed.at[k, y], land.end_a.at[k], send.at[2], sem.end_a.at[jnp.bitwise_and(k, RING - 1)], me.z_in).start()

        @pl.when(me.is_mid)
        def _():
            wait_for(land.end_b.at[k], sem.end_b.at[jnp.bitwise_and(k, RING - 1)])
            packed[k, both] = added(packed[k, both], land.end_b[k])
            remote(packed.at[k, other], land.mid_b.at[k], send.at[3], sem.mid_b.at[jnp.bitwise_and(k, RING - 1)], me.z_mid).start()

    def s2(k):
        @pl.when(me.is_mid)
        def _():
            wait_for(land.end_a.at[k], sem.end_a.at[jnp.bitwise_and(k, RING - 1)])
            packed[k, y] = added(packed[k, y], land.end_a[k])
            remote(packed.at[k, y], land.mid_a.at[k], send.at[4], sem.mid_a.at[jnp.bitwise_and(k, RING - 1)], me.z_mid).start()
            wait_for(land.mid_b.at[k], sem.mid_b.at[jnp.bitwise_and(k, RING - 1)])
            packed[k, mine] = added(packed[k, mine], land.mid_b[k])
            remote(packed.at[k, mine], land.rung_b.at[k], send.at[5], sem.rung.at[jnp.bitwise_and(k, RING - 1)], me.y_peer).start()

    def s3(k):
        o = row(k)
        @pl.when(me.is_mid)
        def _():
            wait_for(land.mid_a.at[k], sem.mid_a.at[jnp.bitwise_and(k, RING - 1)])
            total = land.from_y.at[k]
            total[...] = added(packed[k, y], land.mid_a[k])
            remote(total, out.at[c, o, y], send.at[6], sem.end_final.at[jnp.bitwise_and(k, RING - 1)], me.z_out).start()
            remote(total, out.at[c, o, y], send.at[7], sem.y_final.at[jnp.bitwise_and(k, RING - 1)], me.y_peer).start()
            pltpu.make_async_copy(total, out.at[c, o, y], sem.own_a.at[jnp.bitwise_and(k, RING - 1)]).start()
            wait_for(land.rung_b.at[k], sem.rung.at[jnp.bitwise_and(k, RING - 1)])
            total = land.end_a.at[k]
            total[...] = added(packed[k, mine], land.rung_b[k])
            remote(total, out.at[c, o, mine], send.at[8], sem.mid_final.at[jnp.bitwise_and(k, RING - 1)], me.z_mid).start()
            pltpu.make_async_copy(total, out.at[c, o, mine], sem.own_b.at[jnp.bitwise_and(k, RING - 1)]).start()

    def s4(k):
        o = row(k)
        @pl.when(me.is_end)
        def _():
            wait_for(out.at[c, o, y], sem.end_final.at[jnp.bitwise_and(k, RING - 1)])
            remote(out.at[c, o, y], out.at[c, o, y], send.at[7], sem.y_final.at[jnp.bitwise_and(k, RING - 1)], me.y_peer).start()

        @pl.when(me.is_mid)
        def _():
            wait_for(out.at[c, o, other], sem.mid_final.at[jnp.bitwise_and(k, RING - 1)])
            wait_for(out.at[c, o, mine], sem.own_b.at[jnp.bitwise_and(k, RING - 1)])
            remote(out.at[c, o, both], out.at[c, o, both], send.at[9], sem.end_both.at[jnp.bitwise_and(k, RING - 1)], me.z_out).start()

    def s5(k):
        o = row(k)
        @pl.when(k < own)
        def _():
            wait_for(out.at[c, o, 1 - y], sem.y_final.at[jnp.bitwise_and(k, RING - 1)])

            @pl.when(me.is_end)
            def _():
                wait_for(out.at[c, o, both], sem.end_both.at[jnp.bitwise_and(k, RING - 1)])

            @pl.when(me.is_mid)
            def _():
                wait_for(out.at[c, o, y], sem.own_a.at[jnp.bitwise_and(k, RING - 1)])

        @pl.when(k >= own)
        def _():
            wait_for(out.at[c, o], sem.back.at[jnp.bitwise_and(k, RING - 1)])

        @pl.when(jnp.logical_not(is_lent(k)))
        def _():
            remote(out.at[c, o], out.at[c, o], send.at[10], sem.sibling.at[jnp.bitwise_and(k, RING - 1)], me.sibling).start()

        @pl.when(is_lent(k))
        def _():
            home = k - borrowed + steps - LENT
            remote(out.at[c, o], out.at[c, home], send.at[11], sem.back.at[jnp.bitwise_and(home, RING - 1)], me.across).start()

    def s6(k):
        o = row(k)

        @pl.when(jnp.logical_not(is_lent(k)))
        def _():
            wait_for(out.at[1 - c, o], sem.sibling.at[jnp.bitwise_and(k, RING - 1)])

    stages = (s0, s1, s2, s3, s4, s5, s6)
    everything = jnp.where(first, steps, steps + LENT)
    limits = (own,) * 5 + (everything,) * 2

    def slot(t):
        for i, stage in enumerate(stages):
            k = t - OFFSETS[i]

            @pl.when((k >= 0) & (k < limits[i]))
            def _():
                stage(jnp.clip(k, 0, steps + LENT - 1))

    def all_sent(count):
        section, sections = land.from_y.at[pl.ds(0, count)], land.end_b.at[pl.ds(0, count)]
        wait_for(section, send.at[0])
        wait_for(section, send.at[7])

        @pl.when(me.is_end)
        def _():
            wait_for(sections, send.at[1])
            wait_for(section, send.at[2])

        @pl.when(me.is_mid)
        def _():
            for which in (3, 4, 5, 6, 8):
                wait_for(section, send.at[which])
            wait_for(sections, send.at[9])

    def finish():
        wait_for(packed.at[pl.ds(0, steps)], send.at[10])

        @pl.when(first)
        def _():
            all_sent(steps - LENT)
            lent.wait_send()

        @pl.when(last)
        def _():
            all_sent(steps + LENT)
            wait_for(packed.at[pl.ds(steps, LENT)], send.at[11])

    return slot, steps + LENT + OFFSETS[-1], lent.start, finish


def small_sums(me, smalls, held, total, recv, send):
    def source(j):
        return smalls if j == 0 else held.at[1, j - 1]

    def copy(j):
        return remote(source(j), held.at[0, j], send.at[j], recv.at[j], me.doubling[j])

    def step(j):
        if j >= 0:
            copy(j).wait()
            summed = source(j)[...] + held[0, j]
            if j == 3:
                total[...] = summed
            else:
                held[1, j] = summed
        if j < 3:
            copy(j + 1).start()

    return step


def copies_of(pairs, sems):
    return [pltpu.make_async_copy(src, dst, sems.at[i]) for i, (src, dst) in enumerate(pairs)]


def bucket_rows(n, content, query, wide):
    pairs = []
    for b in range(n.micro):
        pairs.append((content.at[0, pl.ds(b * n.seq, n.seq)], wide.at[pl.ds(b * n.block, n.seq)]))
        pairs.append((query.at[0, pl.ds(b * n.query, n.query)], wide.at[pl.ds(b * n.block + n.seq, n.query)]))
    return pairs


def whole_kernel(n, *refs):
    content, query, *refs = refs
    w_hbm, refs = Weights(*refs[:6]), refs[6:]
    v, refs = Vectors(*refs[:12]), refs[12:]
    content_out, query_out, out, total, *refs = refs
    w, refs = Weights(*refs[:6]), refs[6:]
    left, right, y, dx, dy, resid, table_sum, chosen, smalls, held, packed, *refs = refs
    s, refs = State(left.at[pl.ds(0, n.rows)], *refs[:7]), refs[7:]
    land, refs = Landing(*refs[:6]), refs[6:]
    arrive, refs = Arrival(*refs[:14]), refs[14:]
    w_sem, in_sem, grad_sem, out_sem, pipe_send, pipe_recv, core_send, core_recv, small_send, small_recv, sum_send, lent_sem = refs
    width, rows = n.width, n.rows
    inputs = s.left.at[:, pl.ds(0, width)]
    mine_right = right.at[pl.ds(0, rows)]
    groups = n.hidden // width
    first, last = lax.axis_index("pipe") == 0, lax.axis_index("pipe") == 1
    me = find_place()

    weights = copies_of([(a.at[0], b) for a, b in zip(w_hbm, w)], w_sem)
    own_rows = copies_of(bucket_rows(n, content, query, inputs), in_sem)
    own_grads = copies_of(bucket_rows(n, content, query, dy), in_sem)

    @pl.when(first)
    def _():
        for cp in own_rows:
            cp.start()

    @pl.when(last)
    def _():
        for cp in own_grads:
            cp.start()

    greet_all(me)
    for cp in weights[:3]:
        cp.start()
    bias_and_mask(n, v, s.probs)
    for cp in weights[3:]:
        cp.start()
    hand_down = remote(dx, dy, pipe_send.at[n.micro], pipe_recv.at[n.micro], me.across)

    def hand_up(b):
        return remote(y.at[block_rows(n, b)], inputs.at[block_rows(n, b)], pipe_send.at[b], pipe_recv.at[b], me.across)


    def to_core(which, src, dst):
        return remote(src, dst, core_send.at[which], core_recv.at[which], me.sibling)

    def left_copy(which, at, size):
        return to_core(which, left.at[pl.ds(0, rows), pl.ds(at, size)], left.at[pl.ds(rows, rows), pl.ds(at, size)])

    def right_copy(which, at, size):
        return to_core(which, right.at[pl.ds(0, rows), pl.ds(at, size)], right.at[pl.ds(rows, rows), pl.ds(at, size)])

    share_left = left_copy(0, 0, 3 * width + n.hidden)
    share_attention = right_copy(1, 0, 3 * width)
    share_da = right_copy(2, 3 * width, width)
    share_df = right_copy(3, (4 + groups) * width, width)

    def share_dz(group):
        return right_copy(4 + group, pl.multiple_of((4 + group) * width, width), width)

    @pl.loop(0, n.micro)
    def _(b):
        @pl.when(first & (b == 0))
        def _():
            for cp in own_rows:
                cp.wait()

        @pl.when(last)
        def _():
            hand_up(b).wait_recv()

        def at_first(i):
            pl.when(b == 0)(weights[i].wait)

        project(n, b, at_first, w, v, s)
        attend(n, b, s)
        at_first(3)
        attend_out(n, b, w, v, s, resid)
        attend_norm(n, b, v, s, resid, y)
        at_first(4)
        go_up(n, b, w, v, s, y)
        at_first(5)
        go_down(n, b, w, v, s, resid)
        ffn_norm(n, b, v, s, resid, y)

        pl.when(b == 0)(lambda: all_here(me))

        @pl.when(first)
        def _():
            hand_up(b).start()

    share_left.start()
    results = copies_of([(b, a) for a, b in bucket_rows(n, content_out, query_out, y)], out_sem)
    results_back = copies_of([(b, a) for a, b in bucket_rows(n, content_out, query_out, dx)], out_sem)

    @pl.when(last)
    def _():
        for cp in results:
            cp.start()
        for cp in own_grads:
            cp.wait()

    @pl.when(first)
    def _():
        for b in range(n.micro):
            hand_up(b).wait_send()
        hand_down.wait_recv()

    borrowed = n.hidden // (4 * CHUNK)
    slot, slots, lend, finish = sums(me, first, last, borrowed, packed, out, land, arrive, sum_send, lent_sem)
    (ffn, ffn_count), (attention, attention_count) = tiles_of(n, me.core)
    ffn_norm_back(n, v, s, dy, mine_right, smalls, resid, dx)
    share_df.start()
    down_back(n, w, s, mine_right, smalls, dx, lambda group: share_dz(group).start())

    ffn_steps, attention_steps = (count // math.gcd(ffn_count // 2, UNROLL) for count in (ffn_count, attention_count))
    at_attend = ffn_steps * BESIDE
    at_attention = at_attend + jnp.where(first, n.micro * EARLY, 0)
    start = at_attention + attention_steps * BESIDE

    def some_slots(at, count):
        @pl.loop(0, count)
        def _(i):
            slot(at + i)

    def after_ffn(outside):
        some_slots(outside * BESIDE, BESIDE)

    def after_attention(outside):
        some_slots(at_attention + outside * BESIDE, BESIDE)

    def ffn_grads():
        share_left.wait_recv()
        share_df.wait_recv()
        half = ffn_count // 2
        weight_grads(n, ffn, half, 0, left, right, packed, after_ffn)
        for group in range(groups):
            share_dz(group).wait_recv()
        per = TILE // (4 * CHUNK)
        weight_grads(n, lambda i: ffn(half + i), half, half * per, left, right, packed, lambda i: after_ffn(ffn_steps // 2 + i))

    pl.when(first)(ffn_grads)
    up_back(n, w, dy, mine_right, resid)
    attend_norm_back(n, v, s, dy, mine_right, smalls, resid)
    share_da.start()
    out_back(n, w, dy, mine_right)
    def between(b):
        @pl.when(first)
        def _():
            some_slots(at_attend + b * EARLY, EARLY)

    attend_back(n, v, s, dy, mine_right, smalls, table_sum, chosen, between)
    share_attention.start()
    inputs_back(n, w, mine_right, resid, dx)

    @pl.when(last)
    def _():
        hand_down.start()

    small_step = small_sums(me, smalls, held, total, small_recv, small_send)

    @pl.when(first)
    def _():
        for cp in results_back:
            cp.start()

    pl.when(last)(ffn_grads)
    share_attention.wait_recv()
    share_da.wait_recv()
    weight_grads(n, attention, attention_count, borrowed + jnp.where(last, LENT, 0), left, right, packed, after_attention)
    pl.when(first)(lend)
    table_back(n, smalls, table_sum)
    small_step(-1)

    @pl.loop(0, slots - start)
    def _(i):
        slot(start + i)
        for j in range(4):
            pl.when(i == 3 * (j + 1))(functools.partial(small_step, j))

    finish()
    for which in [share_left, share_attention, share_da, share_df] + [share_dz(group) for group in range(groups)]:
        which.wait_send()
    for cp in results:
        cp.wait()

    @pl.when(last)
    def _():
        hand_down.wait_send()


def shaped(shape, dtype=BF16):
    return jax.ShapeDtypeStruct(shape, dtype)


def run_layers(n, content, query, w, v):
    rows, width = n.rows, n.width
    vmem, smem, anywhere = (pl.BlockSpec(memory_space=space) for space in (pltpu.VMEM, pltpu.SMEM, pl.ANY))
    dma = pltpu.SemaphoreType.DMA
    steps = (4 * width + 2 * n.hidden) // (2 * 4 * CHUNK)
    chunks = steps + LENT
    half = (chunks, 4, CHUNK, width)
    section, sections = pltpu.VMEM((chunks, CHUNK, width), BF16), pltpu.VMEM((chunks, 2, CHUNK, width), BF16)
    small_shape = (24, width)
    left, *others = state_shapes(n)
    scratch = [pltpu.VMEM(m.shape[1:], BF16) for m in w]
    scratch += [
        pltpu.VMEM((2 * rows, left[0][1]), BF16),
        pltpu.VMEM((2 * rows, 5 * width + n.hidden), BF16),
        pltpu.VMEM((rows, width), BF16),
        pltpu.VMEM((rows, width), BF16),
        pltpu.VMEM((rows, width), BF16),
        pltpu.VMEM((rows, width), F32),
        pltpu.VMEM((n.heads, n.seq, n.seq), F32),
        pltpu.VMEM((n.micro, n.seq, n.block), BF16),
        pltpu.VMEM(small_shape, F32),
        pltpu.VMEM((2, 4) + small_shape, F32),
        pltpu.VMEM(half, BF16),
    ]
    scratch += [pltpu.VMEM(shape, dtype) for shape, dtype in others]
    scratch += [section, sections, section, section, section, section]
    scratch += [dma((RING,))] * 14
    shares = 4 + n.hidden // width
    scratch += [dma((6,)), dma((2 * n.micro,)), dma((2 * n.micro,)), dma((2 * n.micro,)), dma((n.micro + 1,)), dma((n.micro + 1,)), dma((shares,)), dma((shares,)), dma((4,)), dma((4,)), dma((12,)), dma((2,))]
    return pl.pallas_call(
        functools.partial(whole_kernel, n),
        out_shape=[shaped(content.shape), shaped(query.shape), shaped((2,) + half), shaped(small_shape, F32)],
        in_specs=[anywhere] * 8 + [vmem] * 10 + [smem, vmem],
        out_specs=[anywhere] * 3 + [vmem],
        scratch_shapes=scratch,
        compiler_params=pltpu.CompilerParams(collective_id=1, has_side_effects=True, vmem_limit_bytes=VMEM_LIMIT),
    )(content, query, *w, *v)


def unpack_kernel(n, packed, smalls, content, query, *refs):
    (content_out, query_out), refs = refs[:2], refs[2:]
    grads, refs = Weights(*(ref.at[0] for ref in refs[:6])), refs[6:]
    vectors, table, (block, wide, in_sem, out_sem, row_sem, held_content, held_query) = refs[:9], refs[9], refs[10:]
    width = n.width
    groups = n.hidden // width
    places = []
    for core in range(2):
        places += [grads.down.at[pl.ds((core * groups // 2 + i) * width, width)] for i in range(groups // 2)]
        places += [grads.up.at[:, pl.ds((core * groups // 2 + i) * width, width)] for i in range(groups // 2)]
        places += [grads.value, grads.out] if core else [grads.query, grads.key]
    count, steps = block.shape[:2]
    loads = [pltpu.make_async_copy(packed.at[i // (count // 2), pl.ds(i % (count // 2) * steps, steps)], block.at[i], in_sem.at[i]) for i in range(count)]
    stores = [pltpu.make_async_copy(wide.at[i], place, out_sem.at[i]) for i, place in enumerate(places)]
    rows_in = copies_of([(content, held_content), (query, held_query)], row_sem)
    rows_back = copies_of([(held_content, content_out), (held_query, query_out)], row_sem)
    for cp in rows_in:
        cp.start()
    for cp in loads[:AHEAD]:
        cp.start()
    for i, vector in enumerate(vectors):
        for part in range(vector.shape[1] // width):
            at = part + (i if i <= 5 else i + 3)
            vector[:, part * width : (part + 1) * width] = smalls[at : at + 1, :]
    for h in range(n.heads):
        table[h] = smalls[12 + h : 13 + h, : n.buckets]
    rows = block.shape[2] * block.shape[3]
    for i in range(count):
        loads[i].wait()
        if i + AHEAD < count:
            loads[i + AHEAD].start()

        @pl.loop(0, steps)
        def _(step):
            wide[i, pl.ds(pl.multiple_of(step * rows, rows), rows), :] = block[i, step].astype(F32).reshape(rows, width)

        stores[i].start()
        if i == 0:
            for back, cp in zip(rows_back, rows_in):
                cp.wait()
                back.start()
    for cp in stores + rows_back:
        cp.wait()


def unpack(n, packed, smalls, content, query):
    width, hidden = n.width, n.hidden
    square, vector = (1, width, width), (1, width)
    matrices = [square] * 4 + [(1, width, hidden), (1, hidden, width)]
    vectors = [vector] * 5 + [(1, hidden)] + [vector] * 3
    vmem, anywhere = pl.BlockSpec(memory_space=pltpu.VMEM), pl.BlockSpec(memory_space=pl.ANY)
    count = 4 + 2 * hidden // width
    steps = 2 * (packed.shape[1] - LENT) // count
    content, query, *made, table = pl.pallas_call(
        functools.partial(unpack_kernel, n),
        out_shape=[shaped(content.shape), shaped(query.shape)] + [shaped(shape, F32) for shape in matrices + vectors + [(n.heads, 1, n.buckets)]],
        in_specs=[anywhere, vmem, anywhere, anywhere],
        out_specs=[anywhere] * 8 + [vmem] * 10,
        scratch_shapes=[
            pltpu.VMEM((count, steps) + packed.shape[2:], packed.dtype),
            pltpu.VMEM((count, width, width), F32),
            pltpu.SemaphoreType.DMA((count,)),
            pltpu.SemaphoreType.DMA((count,)),
            pltpu.SemaphoreType.DMA((2,)),
            pltpu.VMEM(content.shape, BF16),
            pltpu.VMEM(query.shape, BF16),
        ],
        compiler_params=pltpu.CompilerParams(vmem_limit_bytes=VMEM_LIMIT),
    )(packed, smalls, content, query)
    return content, query, made[:6], made[6:] + [jnp.transpose(table, (1, 2, 0))]


def across_blocks(packed, smalls):
    blocks = lax.axis_size("dp") // 16
    if blocks > 1:
        groups = [[block * 16 + i for block in range(blocks)] for i in range(16)]
        packed = lax.psum(packed.astype(F32), "dp", axis_index_groups=groups)
        smalls = lax.psum(smalls, "dp", axis_index_groups=groups)
    return packed, smalls


def on_device(content_ends, query_ends, w_query, b_query, w_key, w_value, b_value, w_out, b_out, gain_attn, shift_attn, w_up, b_up, w_down, b_down, gain_ffn, shift_ffn, rel_table, doc_lengths, position_order):
    micro, seq = position_order.shape
    n = Sizes(micro, seq, query_ends.shape[1] // micro, content_ends.shape[2], rel_table.shape[2], w_up.shape[2], rel_table.shape[1])
    w = Weights(w_query, w_key, w_value, w_out, w_up, w_down)
    v = Vectors(b_query, b_value, b_out, gain_attn, shift_attn, b_up, b_down, gain_ffn, shift_ffn, jnp.transpose(rel_table, (2, 0, 1)), doc_lengths, position_order)
    content_out, query_out, packed, smalls = run_layers(n, content_ends, query_ends, w, v)
    packed, smalls = across_blocks(packed, smalls)
    content_out, query_out, g, d = unpack(n, packed, smalls, content_out, query_out)
    return content_out, query_out, g[0], d[0], g[1], g[2], d[1], g[3], d[2], d[3], d[4], g[4], d[5], g[5], d[6], d[7], d[8], d[9]


def solution(mesh):
    rows, matrix, vector, buckets = P("pipe", "dp", None), P("pipe", None, None), P("pipe", None), P("dp", None)
    grads = (matrix, vector, matrix, matrix, vector, matrix, vector, vector, vector, matrix, vector, matrix, vector, vector, vector, matrix)
    return jax.shard_map(on_device, mesh=mesh, in_specs=(rows, rows, *grads, buckets, buckets), out_specs=(rows, rows, *grads), check_vma=False)
```

```python
import functools
import math
from typing import Any, NamedTuple

import jax
import jax.numpy as jnp
from jax import lax
from jax.experimental import pallas as pl
from jax.experimental.pallas import tpu as pltpu
from jax.sharding import PartitionSpec as P

MESH = pl.DeviceIdType.MESH
F32 = jnp.float32
BF16 = jnp.bfloat16
NORM_EPS = 1e-05
NEG_FILL = -1e30
THRESHOLDS = (12, 16, 23, 32, 46, 64, 91)
TILE = 256
LANES = 128
UNROLL = 1
AHEAD = 4
EARLY = 3
BESIDE = 1
OFFSETS = (0, 3, 6, 8, 10, 13, 16)
RING = 16
LENT = 8
CHUNK = 16
VMEM_LIMIT = 63 * 2**20


class Sizes(NamedTuple):
    micro: int
    seq: int
    query: int
    width: int
    heads: int
    hidden: int
    buckets: int

    @property
    def block(self):
        return self.seq + self.query

    @property
    def rows(self):
        return self.micro * self.block

    @property
    def pairs(self):
        return self.width // LANES


class Weights(NamedTuple):
    query: Any
    key: Any
    value: Any
    out: Any
    up: Any
    down: Any


class Vectors(NamedTuple):
    b_query: Any
    b_value: Any
    b_out: Any
    gain_attn: Any
    shift_attn: Any
    b_up: Any
    b_down: Any
    gain_ffn: Any
    shift_ffn: Any
    rel_table: Any
    lengths: Any
    order: Any


class State(NamedTuple):
    left: Any
    qkv: Any
    slope: Any
    probs: Any
    norm_attn: Any
    norm_ffn: Any
    spread_attn: Any
    spread_ffn: Any


def state_shapes(n):
    return State(
        ((n.rows, 3 * n.width + n.hidden), BF16),
        ((n.rows, 3 * n.width), BF16),
        ((n.rows, n.hidden), BF16),
        ((n.micro * n.pairs, 2 * n.block, n.seq), F32),
        ((n.rows, n.width), F32),
        ((n.rows, n.width), F32),
        ((n.rows, 1), F32),
        ((n.rows, 1), F32),
    )


def dot(a, b):
    return jnp.dot(a, b, preferred_element_type=F32)


def dot_nt(a, b, precision=None):
    return lax.dot_general(a, b, (((1,), (1,)), ((), ())), precision=precision, preferred_element_type=F32)


def dot_tn(a, b):
    return lax.dot_general(a, b, (((0,), (0,)), ((), ())), preferred_element_type=F32)


def iota(shape, dim):
    return lax.broadcasted_iota(jnp.int32, shape, dim)


def cols(at, size=TILE):
    return pl.ds(pl.multiple_of(at * size, size), size)


def bucket_of(offset):
    distance = jnp.abs(offset)
    bucket = jnp.minimum(distance, 8) + jnp.where(offset < 0, 16, 0)
    for bound_at in THRESHOLDS:
        bucket = bucket + jnp.where(distance >= bound_at, 1, 0)
    return bucket


def place_buckets(n):
    shape = (n.buckets, 2 * n.seq)
    at = iota(shape, 1)
    offset = jnp.where(at < n.seq, -at, 2 * n.seq - at)
    return jnp.where(bucket_of(offset) == iota(shape, 0), 1.0, 0.0)


def to_column(row, n):
    shape = (n.seq, n.seq)
    return jnp.sum(jnp.where(iota(shape, 0) == iota(shape, 1), row, 0.0), axis=1, keepdims=True)


def bias_and_mask(n, v, bias):
    seq, query = n.seq, n.query
    by_head = jnp.concatenate([v.rel_table[h] for h in range(n.heads)], axis=0)
    base = jnp.dot(by_head, place_buckets(n), precision=lax.Precision.HIGHEST, preferred_element_type=F32)
    square = (seq, seq)
    row_at, col_at = iota(square, 0).astype(F32), iota(square, 1).astype(F32)
    visible_from = float(seq - query)
    content_sees, query_sees, chosen = [], [], []
    for b in range(n.micro):
        order_row = v.order[b : b + 1, :].astype(F32)
        order_col = to_column(order_row, n)
        rank_row = jnp.sum(jnp.where(order_col == col_at, row_at, 0.0), axis=0, keepdims=True)
        rank_col = to_column(rank_row, n)
        ends, total = [], jnp.int32(0)
        for d in range(v.lengths.shape[1]):
            total = total + v.lengths[b, d]
            ends.append(total)

        def doc_of(at):
            found = jnp.zeros(at.shape, F32)
            for end in ends:
                found = found + jnp.where(at >= end.astype(F32), 1.0, 0.0)
            return found

        doc_row = doc_of(iota((1, seq), 1).astype(F32))
        doc_col = doc_of(iota((seq, 1), 0).astype(F32))
        unmasked = rank_row < visible_from
        content_sees.append((doc_col == doc_row) & (unmasked | (rank_row <= rank_col)))
        place = order_col[seq - query :]
        at_place = place == iota((query, seq), 1).astype(F32)
        rank = visible_from + iota((query, 1), 0).astype(F32)
        query_sees.append((doc_of(place) == doc_row) & (unmasked | (rank_row < rank) | at_place))
        chosen.append(jnp.where(at_place, 1.0, 0.0).astype(BF16))
    for h in range(n.heads):
        spread = jnp.broadcast_to(base[h : h + 1, :], (seq, 2 * seq))
        table = pltpu.roll(spread, 0, 1, stride=1, stride_axis=0)[:, :seq]
        high = table.astype(BF16)
        rest = table - high.astype(F32)
        middle = rest.astype(BF16)
        low = (rest - middle.astype(F32)).astype(BF16)
        for b in range(n.micro):
            of_query = dot(chosen[b], high) + dot(chosen[b], middle) + dot(chosen[b], low)
            start = (h % 2) * n.block
            bias[b * n.pairs + h // 2, start : start + seq, :] = jnp.where(content_sees[b], table, NEG_FILL)
            bias[b * n.pairs + h // 2, start + seq : start + n.block, :] = jnp.where(query_sees[b], of_query, NEG_FILL)


def half_masks():
    at = iota((1, LANES), 1)
    return jnp.where(at < LANES // 2, 1.0, 0.0).astype(BF16), jnp.where(at < LANES // 2, 0.0, 1.0).astype(BF16)


def both_heads(values):
    first, second = half_masks()
    return jnp.concatenate([values * first, values * second], axis=0)


def side_by_side(stacked):
    half = stacked.shape[0] // 2
    return jnp.concatenate([stacked[:half], stacked[half:]], axis=1)


def block_rows(n, b):
    return pl.ds(pl.multiple_of(b * n.block, 16), n.block)


def norm_rows(n, b, summed, normed_ref, spread_ref, gain, shift, write):
    step = n.block // 3
    for at in range(0, n.block, step):
        rows = pl.ds(pl.multiple_of(b * n.block + at, 16), step)
        r = summed[rows, :]
        centered = r - jnp.mean(r, axis=1, keepdims=True)
        spread = lax.rsqrt(jnp.mean(centered * centered, axis=1, keepdims=True) + NORM_EPS)
        normed = centered * spread
        normed_ref[rows, :] = normed
        spread_ref[rows, :] = spread
        write(rows, (normed * gain + shift).astype(BF16))


def norm_back(n, grad_of, normed_ref, spread_ref, gain, write):
    step = n.block // 3

    def body(i, sums):
        rows = pl.ds(pl.multiple_of(i * step, step), step)
        grad = grad_of(rows)
        normed = normed_ref[rows, :]
        scaled = grad * gain
        inner = jnp.mean(scaled * normed, axis=1, keepdims=True)
        back = spread_ref[rows, :] * (scaled - jnp.mean(scaled, axis=1, keepdims=True) - normed * inner)
        write(rows, back)
        low = back.astype(BF16).astype(F32)
        return (
            sums[0] + jnp.sum(grad * normed, axis=0, keepdims=True),
            sums[1] + jnp.sum(grad, axis=0, keepdims=True),
            sums[2] + jnp.sum(low, axis=0, keepdims=True),
        )

    zero = jnp.zeros((1, n.width), F32)
    return lax.fori_loop(0, n.rows // step, body, (zero, zero, zero), unroll=3)


def project(n, b, ready, w, v, s):
    width, tiles = n.width, n.width // TILE
    rows = block_rows(n, b)
    for i, matrix in enumerate((w.query, w.key, w.value)):
        ready(i)
        for t in range(tiles):
            at = slice(t * TILE, (t + 1) * TILE)
            product = dot(s.left[rows, :width], matrix[:, at])
            if i == 0:
                product = product + v.b_query[:, at]
            if i == 2:
                product = product + v.b_value[:, at]
            s.qkv[rows, i * width + t * TILE : i * width + (t + 1) * TILE] = product.astype(BF16)


def attend(n, b, s):
    factor = (LANES // 2) ** -0.5
    rows, keys = block_rows(n, b), pl.ds(pl.multiple_of(b * n.block, 16), n.seq)
    for pair in range(n.pairs):
        it = b * n.pairs + pair

        def lanes(part):
            return slice((part * n.pairs + pair) * LANES, (part * n.pairs + pair + 1) * LANES)

        q = both_heads(s.qkv[rows, lanes(0)])
        val = both_heads(s.qkv[keys, lanes(2)])
        scores = dot_nt(q, s.qkv[keys, lanes(1)]) * factor + s.probs[it]
        powers = jnp.exp(scores - jnp.max(scores, axis=1, keepdims=True))
        probs = powers / jnp.sum(powers, axis=1, keepdims=True)
        s.probs[it] = probs
        s.left[rows, lanes(1)] = dot(side_by_side(probs.astype(BF16)), val).astype(BF16)


def attend_out(n, b, w, v, s, summed):
    width = n.width
    rows = block_rows(n, b)
    for t in range(width // TILE):
        at = slice(t * TILE, (t + 1) * TILE)
        product = dot(s.left[rows, width : 2 * width], w.out[:, at])
        summed[rows, at] = s.left[rows, at].astype(F32) + product + v.b_out[:, at]


def attend_norm(n, b, v, s, summed, copy):
    width = n.width

    def keep_h1(rows, value):
        s.left[rows, 2 * width : 3 * width] = value
        copy[rows, :] = value

    norm_rows(n, b, summed, s.norm_attn, s.spread_attn, v.gain_attn[...], v.shift_attn[...], keep_h1)


def go_up(n, b, w, v, s, h1):
    width, tiles, left_u = n.width, n.width // TILE, 3 * (n.width // TILE)
    step = n.block // 3
    c = (2 / math.pi) ** 0.5
    staged = s.norm_ffn

    def bend(t, i):
        for at in range(0, n.block, step):
            rows = pl.ds(pl.multiple_of(b * n.block + at, 16), step)
            z = staged[rows, i * TILE : (i + 1) * TILE] + v.b_up[:, cols(t)]
            square = z * z
            half = 0.5 + 0.5 * jnp.tanh(z * (c + 0.044715 * c * square))
            value = z * half
            s.left[rows, cols(left_u + t)] = value.astype(BF16)
            s.slope[rows, cols(t)] = (half + value * (1.0 - half) * (2.0 * c + 0.26829 * c * square)).astype(BF16)

    @pl.loop(0, n.hidden // width, unroll=True)
    def _(group):
        for i in range(tiles):
            staged[block_rows(n, b), i * TILE : (i + 1) * TILE] = dot(h1[block_rows(n, b), :], w.up[:, cols(group * tiles + i)])
            if i:
                bend(group * tiles + i - 1, i - 1)
        bend(group * tiles + tiles - 1, tiles - 1)


def go_down(n, b, w, v, s, summed):
    width = n.width
    rows = block_rows(n, b)
    for t in range(width // TILE):
        at = slice(t * TILE, (t + 1) * TILE)
        h1_at = slice(2 * width + t * TILE, 2 * width + (t + 1) * TILE)
        product = dot(s.left[rows, 3 * width :], w.down[:, at])
        summed[rows, at] = s.left[rows, h1_at].astype(F32) + product + v.b_down[:, at]


def ffn_norm(n, b, v, s, summed, y):
    def keep_y(rows, value):
        y[rows, :] = value

    norm_rows(n, b, summed, s.norm_ffn, s.spread_ffn, v.gain_ffn[...], v.shift_ffn[...], keep_y)


def ffn_norm_back(n, v, s, dy, right, smalls, resid, copy):
    width = n.width
    df_cols = slice(4 * width + n.hidden, 5 * width + n.hidden)

    def keep_df(rows, value):
        resid[rows, :] = value
        right[rows, df_cols] = copy[rows, :] = value.astype(BF16)

    gain, shift, low = norm_back(n, lambda rows: dy[rows, :].astype(F32), s.norm_ffn, s.spread_ffn, v.gain_ffn[...], keep_df)
    smalls[10:11, :], smalls[11:12, :], smalls[9:10, :] = gain, shift, low


def down_back(n, w, s, right, smalls, df, sent):
    width, tiles = n.width, n.width // TILE
    step = n.block // 3
    staged = s.norm_ffn

    def bend(group, i):
        t = group * tiles + i
        total = jnp.zeros((8, TILE), F32)
        for at in range(0, n.rows, step):
            rows = slice(at, at + step)
            dz = (staged[rows, i * TILE : (i + 1) * TILE] * s.slope[rows, cols(t)].astype(F32)).astype(BF16)
            right[rows, cols(4 * tiles + t)] = dz
            total = total + jnp.sum(dz.astype(F32).reshape(step // 8, 8, TILE), axis=0)
        smalls[pl.ds(5 + group, 1), cols(i)] = jnp.sum(total, axis=0, keepdims=True)

    @pl.loop(0, n.hidden // width, unroll=True)
    def _(group):
        for i in range(tiles):
            staged[:, i * TILE : (i + 1) * TILE] = dot_nt(df[...], w.down[cols(group * tiles + i), :])
            if i:
                bend(group, i - 1)
        bend(group, tiles - 1)
        sent(group)


def up_back(n, w, dy, right, resid):
    width, tiles = n.width, n.width // TILE

    @pl.loop(0, tiles, unroll=True)
    def _(t):
        spread = dot_nt(right[:, 4 * width : 4 * width + n.hidden], w.up[cols(t), :])
        dy[:, cols(t)] = (spread + resid[:, cols(t)]).astype(BF16)


def attend_norm_back(n, v, s, dy, right, smalls, resid):
    width = n.width

    def keep_da(rows, value):
        resid[rows, :] = value
        right[rows, 3 * width : 4 * width] = value.astype(BF16)

    gain, shift, low = norm_back(n, lambda rows: dy[rows, :].astype(F32), s.norm_attn, s.spread_attn, v.gain_attn[...], keep_da)
    smalls[3:4, :], smalls[4:5, :], smalls[2:3, :] = gain, shift, low


def out_back(n, w, dy, right):
    width, tiles = n.width, n.width // TILE

    @pl.loop(0, tiles, unroll=True)
    def _(t):
        dy[:, cols(t)] = dot_nt(right[:, 3 * width : 4 * width], w.out[cols(t), :]).astype(BF16)


def attend_back(n, v, s, dy, right, smalls, table_sum, chosen, between):
    width = n.width
    factor = (LANES // 2) ** -0.5
    table_sum[...] = jnp.zeros(table_sum.shape, F32)
    square = (n.seq, n.seq)
    same = jnp.where(iota(square, 0) + iota(square, 1) == n.seq - 1, 1.0, 0.0).astype(BF16)
    for b in range(n.micro):
        place = v.order[b : b + 1, n.seq - n.query :]
        chosen[b, :, : n.seq] = same
        chosen[b, :, n.seq :] = jnp.where(place == n.seq - 1 - iota((n.seq, n.query), 0), 1.0, 0.0).astype(BF16)

    @pl.loop(0, n.micro)
    def _(b):
        start = b * n.block
        rows, keys = block_rows(n, b), pl.ds(pl.multiple_of(start, 16), n.seq)
        rest = pl.ds(pl.multiple_of(start + n.seq, 16), n.query)
        for pair in range(n.pairs):
            q_at, k_at, v_at = (slice((part * n.pairs + pair) * LANES, (part * n.pairs + pair + 1) * LANES) for part in range(3))
            grad = both_heads(dy[rows, q_at])
            q = both_heads(s.qkv[rows, q_at])
            k = both_heads(s.qkv[keys, k_at])
            val = s.qkv[keys, v_at]
            probs = s.probs[b * n.pairs + pair]
            grad_probs = dot_nt(grad, val)
            inner = jnp.sum(probs * grad_probs, axis=1, keepdims=True)
            grad_scores = (probs * (grad_probs - inner)).astype(BF16)
            beside = side_by_side(grad_scores)
            right[rows, q_at] = (dot(beside, k) * factor).astype(BF16)
            right[keys, k_at] = (dot_tn(grad_scores, q) * factor).astype(BF16)
            right[keys, v_at] = dot_tn(probs.astype(BF16), grad).astype(BF16)
            none = jnp.zeros((n.query, LANES), BF16)
            right[rest, k_at] = none
            right[rest, v_at] = none
            of_heads = dot(chosen[b], beside)
            table_sum[2 * pair] += of_heads[:, : n.seq]
            table_sum[2 * pair + 1] += of_heads[:, n.seq :]
        between(b)

    smalls[0:1, :] = jnp.sum(right[:, :width].astype(F32), axis=0, keepdims=True)
    smalls[1:2, :] = jnp.sum(right[:, 2 * width : 3 * width].astype(F32), axis=0, keepdims=True)


def table_back(n, smalls, table_sum):
    by_place = []
    for h in range(n.heads):
        wide = jnp.concatenate([table_sum[h], jnp.zeros((n.seq, n.seq), F32)], axis=1)
        turned = pltpu.roll(wide, n.seq + 1, 1, stride=1, stride_axis=0)
        by_place.append(jnp.sum(turned, axis=0, keepdims=True))
    by_place = jnp.concatenate(by_place, axis=0)
    smalls[12 : 12 + n.heads, : n.buckets] = dot_nt(by_place, place_buckets(n), lax.Precision.HIGHEST)


def inputs_back(n, w, right, resid, dx):
    width, tiles = n.width, n.width // TILE

    @pl.loop(0, tiles, unroll=True)
    def _(t):
        total = resid[:, cols(t)]
        for i, matrix in enumerate((w.query, w.key, w.value)):
            total = total + dot_nt(right[:, i * width : (i + 1) * width], matrix[cols(t), :])
        dx[:, cols(t)] = total.astype(BF16)


def tiles_of(n, core):
    tiles, groups = n.width // TILE, n.hidden // n.width
    down = groups * tiles // 2

    def ffn(i):
        is_down = i < down
        up = i - down
        left = jnp.where(is_down, 3 * tiles + core * down + i, 2 * tiles + up % tiles)
        return left, jnp.where(is_down, 4 + groups, 4 + core * (groups // 2) + up // tiles)

    def attention(i):
        group = i // tiles
        return i % tiles + jnp.where(core * group == 1, tiles, 0), 2 * core + group

    return (ffn, 2 * down), (attention, 2 * tiles)


def weight_grads(n, of, count, first, left, right, packed, between):
    per = TILE // packed.shape[2] // packed.shape[1]
    by = math.gcd(count, UNROLL)

    @pl.loop(0, count // by)
    def _(outside):
        for inside in range(by):
            i = outside * by + inside
            left_tile, group = of(i)
            rhs = right[:, pl.ds(pl.multiple_of(group * n.width, n.width), n.width)]
            product = dot_tn(left[:, cols(left_tile)], rhs).astype(BF16)
            packed[pl.ds(first + i * per, per)] = product.reshape((per,) + packed.shape[1:])
        between(outside)


class Landing(NamedTuple):
    from_y: Any
    end_b: Any
    end_a: Any
    mid_a: Any
    mid_b: Any
    rung_b: Any


class Arrival(NamedTuple):
    y: Any
    end_b: Any
    end_a: Any
    mid_a: Any
    mid_b: Any
    rung: Any
    own_a: Any
    own_b: Any
    end_final: Any
    y_final: Any
    mid_final: Any
    end_both: Any
    sibling: Any
    back: Any


class Place(NamedTuple):
    core: Any
    y: Any
    mine: Any
    other: Any
    is_end: Any
    is_mid: Any
    sibling: Any
    y_peer: Any
    z_in: Any
    z_out: Any
    z_mid: Any
    across: Any
    doubling: Any


def find_place():
    pipe, index = lax.axis_index("pipe"), lax.axis_index("dp")
    base, local = index // 16 * 16, index % 16
    z, y, core = local // 4, local // 2 % 2, local % 2

    def at(zz, yy, cc):
        return (pipe, base + zz * 4 + yy * 2 + cc)

    return Place(
        core,
        y,
        z + 1,
        4 - z,
        (z == 0) | (z == 3),
        (z == 1) | (z == 2),
        at(z, y, 1 - core),
        at(z, 1 - y, core),
        at(jnp.where(z == 0, 1, 2), y, core),
        at(jnp.where(z == 1, 0, 3), y, core),
        at(3 - z, y, core),
        (1 - pipe, index),
        [(pipe, base + jnp.bitwise_xor(local, 1 << j)) for j in range(4)],
    )


def greet_all(me):
    barrier = pltpu.get_barrier_semaphore()
    for device in me.doubling + [me.across]:
        pl.semaphore_signal(barrier, inc=1, device_id=device, device_id_type=MESH)

    @pl.when(me.is_mid)
    def _():
        pl.semaphore_signal(barrier, inc=1, device_id=me.z_mid, device_id_type=MESH)


def all_here(me):
    barrier = pltpu.get_barrier_semaphore()
    pl.when(me.is_mid)(lambda: pl.semaphore_wait(barrier, 6))
    pl.when(me.is_end)(lambda: pl.semaphore_wait(barrier, 5))


def remote(src, dst, send, recv, device):
    return pltpu.make_async_remote_copy(src_ref=src, dst_ref=dst, send_sem=send, recv_sem=recv, device_id=device, device_id_type=MESH)


def wait_for(ref, sem):
    pltpu.make_async_copy(ref, ref, sem).wait()


def added(a, b):
    return (a.astype(F32) + b.astype(F32)).astype(BF16)


def sums(me, first, last, borrowed, packed, out, land, sem, send, lent_sem):
    steps = packed.shape[0] - LENT
    own = jnp.where(first, steps - LENT, steps + LENT)
    lent = remote(packed.at[pl.ds(steps - LENT, LENT)], packed.at[pl.ds(borrowed, LENT)], lent_sem.at[0], lent_sem.at[1], me.across)
    c, y, mine, other = me.core, me.y, me.mine, me.other
    both = pl.ds(2, 2)

    def is_lent(k):
        return last & (k >= borrowed) & (k < borrowed + LENT)

    def row(k):
        moved = jnp.where(k < borrowed + LENT, steps + k - borrowed, k - LENT)
        return jnp.where(last & (k >= borrowed), moved, k)

    def s0(k):
        pl.when(last & (k == borrowed))(lent.wait_recv)
        remote(packed.at[k, 1 - y], land.from_y.at[k], send.at[0], sem.y.at[jnp.bitwise_and(k, RING // 2 - 1)], me.y_peer).start()

        @pl.when(me.is_end)
        def _():
            remote(packed.at[k, both], land.end_b.at[k], send.at[1], sem.end_b.at[jnp.bitwise_and(k, RING - 1)], me.z_in).start()

    def s1(k):
        wait_for(land.from_y.at[k], sem.y.at[jnp.bitwise_and(k, RING // 2 - 1)])
        packed[k, y] = added(packed[k, y], land.from_y[k])

        @pl.when(me.is_end)
        def _():
            remote(packed.at[k, y], land.end_a.at[k], send.at[2], sem.end_a.at[jnp.bitwise_and(k, RING - 1)], me.z_in).start()

        @pl.when(me.is_mid)
        def _():
            wait_for(land.end_b.at[k], sem.end_b.at[jnp.bitwise_and(k, RING - 1)])
            packed[k, both] = added(packed[k, both], land.end_b[k])
            remote(packed.at[k, other], land.mid_b.at[k], send.at[3], sem.mid_b.at[jnp.bitwise_and(k, RING // 2 - 1)], me.z_mid).start()

    def s2(k):
        @pl.when(me.is_mid)
        def _():
            wait_for(land.end_a.at[k], sem.end_a.at[jnp.bitwise_and(k, RING - 1)])
            packed[k, y] = added(packed[k, y], land.end_a[k])
            remote(packed.at[k, y], land.mid_a.at[k], send.at[4], sem.mid_a.at[jnp.bitwise_and(k, RING // 2 - 1)], me.z_mid).start()
            wait_for(land.mid_b.at[k], sem.mid_b.at[jnp.bitwise_and(k, RING // 2 - 1)])
            packed[k, mine] = added(packed[k, mine], land.mid_b[k])
            remote(packed.at[k, mine], land.rung_b.at[k], send.at[5], sem.rung.at[jnp.bitwise_and(k, RING // 2 - 1)], me.y_peer).start()

    def s3(k):
        o = row(k)
        @pl.when(me.is_mid)
        def _():
            wait_for(land.mid_a.at[k], sem.mid_a.at[jnp.bitwise_and(k, RING // 2 - 1)])
            total = land.from_y.at[k]
            total[...] = added(packed[k, y], land.mid_a[k])
            remote(total, out.at[c, o, y], send.at[6], sem.end_final.at[jnp.bitwise_and(k, RING - 1)], me.z_out).start()
            remote(total, out.at[c, o, y], send.at[7], sem.y_final.at[jnp.bitwise_and(k, RING - 1)], me.y_peer).start()
            pltpu.make_async_copy(total, out.at[c, o, y], sem.own_a.at[jnp.bitwise_and(k, RING // 2 - 1)]).start()
            wait_for(land.rung_b.at[k], sem.rung.at[jnp.bitwise_and(k, RING // 2 - 1)])
            total = land.end_a.at[k]
            total[...] = added(packed[k, mine], land.rung_b[k])
            remote(total, out.at[c, o, mine], send.at[8], sem.mid_final.at[jnp.bitwise_and(k, RING // 2 - 1)], me.z_mid).start()
            pltpu.make_async_copy(total, out.at[c, o, mine], sem.own_b.at[jnp.bitwise_and(k, RING // 2 - 1)]).start()

    def s4(k):
        o = row(k)
        @pl.when(me.is_end)
        def _():
            wait_for(out.at[c, o, y], sem.end_final.at[jnp.bitwise_and(k, RING - 1)])
            remote(out.at[c, o, y], out.at[c, o, y], send.at[7], sem.y_final.at[jnp.bitwise_and(k, RING - 1)], me.y_peer).start()

        @pl.when(me.is_mid)
        def _():
            wait_for(out.at[c, o, other], sem.mid_final.at[jnp.bitwise_and(k, RING // 2 - 1)])
            wait_for(out.at[c, o, mine], sem.own_b.at[jnp.bitwise_and(k, RING // 2 - 1)])
            remote(out.at[c, o, both], out.at[c, o, both], send.at[9], sem.end_both.at[jnp.bitwise_and(k, RING - 1)], me.z_out).start()

    def s5(k):
        o = row(k)
        @pl.when(k < own)
        def _():
            wait_for(out.at[c, o, 1 - y], sem.y_final.at[jnp.bitwise_and(k, RING - 1)])

            @pl.when(me.is_end)
            def _():
                wait_for(out.at[c, o, both], sem.end_both.at[jnp.bitwise_and(k, RING - 1)])

            @pl.when(me.is_mid)
            def _():
                wait_for(out.at[c, o, y], sem.own_a.at[jnp.bitwise_and(k, RING // 2 - 1)])

        @pl.when(k >= own)
        def _():
            wait_for(out.at[c, o], sem.back.at[jnp.bitwise_and(k, RING // 2 - 1)])

        @pl.when(jnp.logical_not(is_lent(k)))
        def _():
            remote(out.at[c, o], out.at[c, o], send.at[10], sem.sibling.at[jnp.bitwise_and(k, RING - 1)], me.sibling).start()

        @pl.when(is_lent(k))
        def _():
            home = k - borrowed + steps - LENT
            remote(out.at[c, o], out.at[c, home], send.at[11], sem.back.at[jnp.bitwise_and(home, RING // 2 - 1)], me.across).start()

    def s6(k):
        o = row(k)

        @pl.when(jnp.logical_not(is_lent(k)))
        def _():
            wait_for(out.at[1 - c, o], sem.sibling.at[jnp.bitwise_and(k, RING - 1)])

    stages = (s0, s1, s2, s3, s4, s5, s6)
    everything = jnp.where(first, steps, steps + LENT)
    limits = (own,) * 5 + (everything,) * 2

    def slot(t):
        for i, stage in enumerate(stages):
            k = t - OFFSETS[i]

            @pl.when((k >= 0) & (k < limits[i]))
            def _():
                stage(jnp.clip(k, 0, steps + LENT - 1))

    def all_sent(count):
        section, sections = land.from_y.at[pl.ds(0, count)], land.end_b.at[pl.ds(0, count)]
        wait_for(section, send.at[0])
        wait_for(section, send.at[7])

        @pl.when(me.is_end)
        def _():
            wait_for(sections, send.at[1])
            wait_for(section, send.at[2])

        @pl.when(me.is_mid)
        def _():
            for which in (3, 4, 5, 6, 8):
                wait_for(section, send.at[which])
            wait_for(sections, send.at[9])

    def finish():
        wait_for(packed.at[pl.ds(0, steps)], send.at[10])

        @pl.when(first)
        def _():
            all_sent(steps - LENT)
            lent.wait_send()

        @pl.when(last)
        def _():
            all_sent(steps + LENT)
            wait_for(packed.at[pl.ds(steps, LENT)], send.at[11])

    return slot, steps + LENT + OFFSETS[-1], lent.start, finish


def small_sums(me, smalls, held, total, recv, send):
    def source(j):
        return smalls if j == 0 else held.at[1, j - 1]

    def copy(j):
        return remote(source(j), held.at[0, j], send.at[j], recv.at[j], me.doubling[j])

    def step(j):
        if j >= 0:
            copy(j).wait()
            summed = source(j)[...] + held[0, j]
            if j == 3:
                total[...] = summed
            else:
                held[1, j] = summed
        if j < 3:
            copy(j + 1).start()

    return step


def copies_of(pairs, sems):
    return [pltpu.make_async_copy(src, dst, sems.at[i]) for i, (src, dst) in enumerate(pairs)]


def bucket_rows(n, content, query, wide):
    pairs = []
    for b in range(n.micro):
        pairs.append((content.at[0, pl.ds(b * n.seq, n.seq)], wide.at[pl.ds(b * n.block, n.seq)]))
        pairs.append((query.at[0, pl.ds(b * n.query, n.query)], wide.at[pl.ds(b * n.block + n.seq, n.query)]))
    return pairs


def whole_kernel(n, *refs):
    content, query, *refs = refs
    w_hbm, refs = Weights(*refs[:6]), refs[6:]
    v, refs = Vectors(*refs[:12]), refs[12:]
    content_out, query_out, out, total, *refs = refs
    w, refs = Weights(*refs[:6]), refs[6:]
    left, right, y, dx, dy, resid, table_sum, chosen, smalls, held, packed, *refs = refs
    s, refs = State(left.at[pl.ds(0, n.rows)], *refs[:7]), refs[7:]
    land, refs = Landing(*refs[:6]), refs[6:]
    arrive, refs = Arrival(*refs[:14]), refs[14:]
    w_sem, in_sem, grad_sem, out_sem, pipe_send, pipe_recv, core_send, core_recv, small_send, small_recv, sum_send, lent_sem = refs
    width, rows = n.width, n.rows
    inputs = s.left.at[:, pl.ds(0, width)]
    mine_right = right.at[pl.ds(0, rows)]
    groups = n.hidden // width
    first, last = lax.axis_index("pipe") == 0, lax.axis_index("pipe") == 1
    me = find_place()

    weights = copies_of([(a.at[0], b) for a, b in zip(w_hbm, w)], w_sem)
    own_rows = copies_of(bucket_rows(n, content, query, inputs), in_sem)
    own_grads = copies_of(bucket_rows(n, content, query, dy), in_sem)

    @pl.when(first)
    def _():
        for cp in own_rows:
            cp.start()

    @pl.when(last)
    def _():
        for cp in own_grads:
            cp.start()

    greet_all(me)
    for cp in weights[:3]:
        cp.start()
    bias_and_mask(n, v, s.probs)
    for cp in weights[3:]:
        cp.start()
    hand_down = remote(dx, dy, pipe_send.at[n.micro], pipe_recv.at[n.micro], me.across)

    def hand_up(b):
        return remote(y.at[block_rows(n, b)], inputs.at[block_rows(n, b)], pipe_send.at[b], pipe_recv.at[b], me.across)


    def to_core(which, src, dst):
        return remote(src, dst, core_send.at[which], core_recv.at[which], me.sibling)

    def left_copy(which, at, size):
        return to_core(which, left.at[pl.ds(0, rows), pl.ds(at, size)], left.at[pl.ds(rows, rows), pl.ds(at, size)])

    def right_copy(which, at, size):
        return to_core(which, right.at[pl.ds(0, rows), pl.ds(at, size)], right.at[pl.ds(rows, rows), pl.ds(at, size)])

    share_left = left_copy(0, 0, 3 * width + n.hidden)
    share_attention = right_copy(1, 0, 3 * width)
    share_da = right_copy(2, 3 * width, width)
    share_df = right_copy(3, (4 + groups) * width, width)

    def share_dz(group):
        return right_copy(4 + group, pl.multiple_of((4 + group) * width, width), width)

    @pl.loop(0, n.micro)
    def _(b):
        @pl.when(first & (b == 0))
        def _():
            for cp in own_rows:
                cp.wait()

        @pl.when(last)
        def _():
            hand_up(b).wait_recv()

        def at_first(i):
            pl.when(b == 0)(weights[i].wait)

        project(n, b, at_first, w, v, s)
        attend(n, b, s)
        at_first(3)
        attend_out(n, b, w, v, s, resid)
        attend_norm(n, b, v, s, resid, y)
        at_first(4)
        go_up(n, b, w, v, s, y)
        at_first(5)
        go_down(n, b, w, v, s, resid)
        ffn_norm(n, b, v, s, resid, y)

        pl.when(b == 0)(lambda: all_here(me))

        @pl.when(first)
        def _():
            hand_up(b).start()

    share_left.start()
    results = copies_of([(b, a) for a, b in bucket_rows(n, content_out, query_out, y)], out_sem)
    results_back = copies_of([(b, a) for a, b in bucket_rows(n, content_out, query_out, dx)], out_sem)

    @pl.when(last)
    def _():
        for cp in results:
            cp.start()
        for cp in own_grads:
            cp.wait()

    @pl.when(first)
    def _():
        for b in range(n.micro):
            hand_up(b).wait_send()
        hand_down.wait_recv()

    borrowed = n.hidden // (4 * CHUNK)
    slot, slots, lend, finish = sums(me, first, last, borrowed, packed, out, land, arrive, sum_send, lent_sem)
    (ffn, ffn_count), (attention, attention_count) = tiles_of(n, me.core)
    ffn_norm_back(n, v, s, dy, mine_right, smalls, resid, dx)
    share_df.start()
    down_back(n, w, s, mine_right, smalls, dx, lambda group: share_dz(group).start())

    ffn_steps, attention_steps = (count // math.gcd(ffn_count // 2, UNROLL) for count in (ffn_count, attention_count))
    at_attend = ffn_steps * BESIDE
    at_attention = at_attend + jnp.where(first, n.micro * EARLY, 0)
    start = at_attention + attention_steps * BESIDE

    def some_slots(at, count):
        @pl.loop(0, count)
        def _(i):
            slot(at + i)

    def after_ffn(outside):
        some_slots(outside * BESIDE, BESIDE)

    def after_attention(outside):
        some_slots(at_attention + outside * BESIDE, BESIDE)

    def ffn_grads():
        share_left.wait_recv()
        share_df.wait_recv()
        half = ffn_count // 2
        weight_grads(n, ffn, half, 0, left, right, packed, after_ffn)
        for group in range(groups):
            share_dz(group).wait_recv()
        per = TILE // (4 * CHUNK)
        weight_grads(n, lambda i: ffn(half + i), half, half * per, left, right, packed, lambda i: after_ffn(ffn_steps // 2 + i))

    pl.when(first)(ffn_grads)
    up_back(n, w, dy, mine_right, resid)
    attend_norm_back(n, v, s, dy, mine_right, smalls, resid)
    share_da.start()
    out_back(n, w, dy, mine_right)
    def between(b):
        @pl.when(first)
        def _():
            some_slots(at_attend + b * EARLY, EARLY)

    attend_back(n, v, s, dy, mine_right, smalls, table_sum, chosen, between)
    share_attention.start()
    inputs_back(n, w, mine_right, resid, dx)

    @pl.when(last)
    def _():
        hand_down.start()

    small_step = small_sums(me, smalls, held, total, small_recv, small_send)

    @pl.when(first)
    def _():
        for cp in results_back:
            cp.start()

    pl.when(last)(ffn_grads)
    share_attention.wait_recv()
    share_da.wait_recv()
    weight_grads(n, attention, attention_count, borrowed + jnp.where(last, LENT, 0), left, right, packed, after_attention)
    pl.when(first)(lend)
    table_back(n, smalls, table_sum)
    small_step(-1)

    @pl.loop(0, slots - start)
    def _(i):
        slot(start + i)
        for j in range(4):
            pl.when(i == 3 * (j + 1))(functools.partial(small_step, j))

    finish()
    for which in [share_left, share_attention, share_da, share_df] + [share_dz(group) for group in range(groups)]:
        which.wait_send()
    for cp in results:
        cp.wait()

    @pl.when(last)
    def _():
        hand_down.wait_send()


def shaped(shape, dtype=BF16):
    return jax.ShapeDtypeStruct(shape, dtype)


def run_layers(n, content, query, w, v):
    rows, width = n.rows, n.width
    vmem, smem, anywhere = (pl.BlockSpec(memory_space=space) for space in (pltpu.VMEM, pltpu.SMEM, pl.ANY))
    dma = pltpu.SemaphoreType.DMA
    steps = (4 * width + 2 * n.hidden) // (2 * 4 * CHUNK)
    chunks = steps + LENT
    half = (chunks, 4, CHUNK, width)
    section, sections = pltpu.VMEM((chunks, CHUNK, width), BF16), pltpu.VMEM((chunks, 2, CHUNK, width), BF16)
    small_shape = (24, width)
    left, *others = state_shapes(n)
    scratch = [pltpu.VMEM(m.shape[1:], BF16) for m in w]
    scratch += [
        pltpu.VMEM((2 * rows, left[0][1]), BF16),
        pltpu.VMEM((2 * rows, 5 * width + n.hidden), BF16),
        pltpu.VMEM((rows, width), BF16),
        pltpu.VMEM((rows, width), BF16),
        pltpu.VMEM((rows, width), BF16),
        pltpu.VMEM((rows, width), F32),
        pltpu.VMEM((n.heads, n.seq, n.seq), F32),
        pltpu.VMEM((n.micro, n.seq, n.block), BF16),
        pltpu.VMEM(small_shape, F32),
        pltpu.VMEM((2, 4) + small_shape, F32),
        pltpu.VMEM(half, BF16),
    ]
    scratch += [pltpu.VMEM(shape, dtype) for shape, dtype in others]
    scratch += [section, sections, section, section, section, section]
    halved = (0, 3, 4, 5, 6, 7, 10, 13)
    scratch += [dma((RING // 2 if i in halved else RING,)) for i in range(14)]
    shares = 4 + n.hidden // width
    scratch += [dma((6,)), dma((2 * n.micro,)), dma((2 * n.micro,)), dma((2 * n.micro,)), dma((n.micro + 1,)), dma((n.micro + 1,)), dma((shares,)), dma((shares,)), dma((4,)), dma((4,)), dma((12,)), dma((2,))]
    return pl.pallas_call(
        functools.partial(whole_kernel, n),
        out_shape=[shaped(content.shape), shaped(query.shape), shaped((2,) + half), shaped(small_shape, F32)],
        in_specs=[anywhere] * 8 + [vmem] * 10 + [smem, vmem],
        out_specs=[anywhere] * 3 + [vmem],
        scratch_shapes=scratch,
        compiler_params=pltpu.CompilerParams(collective_id=1, has_side_effects=True, vmem_limit_bytes=VMEM_LIMIT),
    )(content, query, *w, *v)


def unpack_kernel(n, packed, smalls, content, query, *refs):
    (content_out, query_out), refs = refs[:2], refs[2:]
    grads, refs = Weights(*(ref.at[0] for ref in refs[:6])), refs[6:]
    vectors, table, (block, wide, in_sem, out_sem, row_sem, held_content, held_query) = refs[:9], refs[9], refs[10:]
    width = n.width
    groups = n.hidden // width
    places = []
    for core in range(2):
        places += [grads.down.at[pl.ds((core * groups // 2 + i) * width, width)] for i in range(groups // 2)]
        places += [grads.up.at[:, pl.ds((core * groups // 2 + i) * width, width)] for i in range(groups // 2)]
        places += [grads.value, grads.out] if core else [grads.query, grads.key]
    count, steps = block.shape[:2]
    loads = [pltpu.make_async_copy(packed.at[i // (count // 2), pl.ds(i % (count // 2) * steps, steps)], block.at[i], in_sem.at[i]) for i in range(count)]
    stores = [pltpu.make_async_copy(wide.at[i], place, out_sem.at[i]) for i, place in enumerate(places)]
    rows_in = copies_of([(content, held_content), (query, held_query)], row_sem)
    rows_back = copies_of([(held_content, content_out), (held_query, query_out)], row_sem)
    for cp in rows_in:
        cp.start()
    for cp in loads[:AHEAD]:
        cp.start()
    for i, vector in enumerate(vectors):
        for part in range(vector.shape[1] // width):
            at = part + (i if i <= 5 else i + 3)
            vector[:, part * width : (part + 1) * width] = smalls[at : at + 1, :]
    for h in range(n.heads):
        table[h] = smalls[12 + h : 13 + h, : n.buckets]
    rows = block.shape[2] * block.shape[3]
    for i in range(count):
        loads[i].wait()
        if i + AHEAD < count:
            loads[i + AHEAD].start()

        @pl.loop(0, steps)
        def _(step):
            wide[i, pl.ds(pl.multiple_of(step * rows, rows), rows), :] = block[i, step].astype(F32).reshape(rows, width)

        stores[i].start()
        if i == 0:
            for back, cp in zip(rows_back, rows_in):
                cp.wait()
                back.start()
    for cp in stores + rows_back:
        cp.wait()


def unpack(n, packed, smalls, content, query):
    width, hidden = n.width, n.hidden
    square, vector = (1, width, width), (1, width)
    matrices = [square] * 4 + [(1, width, hidden), (1, hidden, width)]
    vectors = [vector] * 5 + [(1, hidden)] + [vector] * 3
    vmem, anywhere = pl.BlockSpec(memory_space=pltpu.VMEM), pl.BlockSpec(memory_space=pl.ANY)
    count = 4 + 2 * hidden // width
    steps = 2 * (packed.shape[1] - LENT) // count
    content, query, *made, table = pl.pallas_call(
        functools.partial(unpack_kernel, n),
        out_shape=[shaped(content.shape), shaped(query.shape)] + [shaped(shape, F32) for shape in matrices + vectors + [(n.heads, 1, n.buckets)]],
        in_specs=[anywhere, vmem, anywhere, anywhere],
        out_specs=[anywhere] * 8 + [vmem] * 10,
        scratch_shapes=[
            pltpu.VMEM((count, steps) + packed.shape[2:], packed.dtype),
            pltpu.VMEM((count, width, width), F32),
            pltpu.SemaphoreType.DMA((count,)),
            pltpu.SemaphoreType.DMA((count,)),
            pltpu.SemaphoreType.DMA((2,)),
            pltpu.VMEM(content.shape, BF16),
            pltpu.VMEM(query.shape, BF16),
        ],
        compiler_params=pltpu.CompilerParams(vmem_limit_bytes=VMEM_LIMIT),
    )(packed, smalls, content, query)
    return content, query, made[:6], made[6:] + [jnp.transpose(table, (1, 2, 0))]


def across_blocks(packed, smalls):
    blocks = lax.axis_size("dp") // 16
    if blocks > 1:
        groups = [[block * 16 + i for block in range(blocks)] for i in range(16)]
        packed = lax.psum(packed.astype(F32), "dp", axis_index_groups=groups)
        smalls = lax.psum(smalls, "dp", axis_index_groups=groups)
    return packed, smalls


def on_device(content_ends, query_ends, w_query, b_query, w_key, w_value, b_value, w_out, b_out, gain_attn, shift_attn, w_up, b_up, w_down, b_down, gain_ffn, shift_ffn, rel_table, doc_lengths, position_order):
    micro, seq = position_order.shape
    n = Sizes(micro, seq, query_ends.shape[1] // micro, content_ends.shape[2], rel_table.shape[2], w_up.shape[2], rel_table.shape[1])
    w = Weights(w_query, w_key, w_value, w_out, w_up, w_down)
    v = Vectors(b_query, b_value, b_out, gain_attn, shift_attn, b_up, b_down, gain_ffn, shift_ffn, jnp.transpose(rel_table, (2, 0, 1)), doc_lengths, position_order)
    content_out, query_out, packed, smalls = run_layers(n, content_ends, query_ends, w, v)
    packed, smalls = across_blocks(packed, smalls)
    content_out, query_out, g, d = unpack(n, packed, smalls, content_out, query_out)
    return content_out, query_out, g[0], d[0], g[1], g[2], d[1], g[3], d[2], d[3], d[4], g[4], d[5], g[5], d[6], d[7], d[8], d[9]


def solution(mesh):
    rows, matrix, vector, buckets = P("pipe", "dp", None), P("pipe", None, None), P("pipe", None), P("dp", None)
    grads = (matrix, vector, matrix, matrix, vector, matrix, vector, vector, vector, matrix, vector, matrix, vector, vector, vector, matrix)
    return jax.shard_map(on_device, mesh=mesh, in_specs=(rows, rows, *grads, buckets, buckets), out_specs=(rows, rows, *grads), check_vma=False)
```
